128 devices in a mesh: row: 8 (over y, core), col: 16 (over x, z).
Axes of the slice: x: 4, y: 4, z: 4, core: 2. Of those that a mesh axis runs over, the one named last changes fastest.
Arguments:
- matrix: float32 [8, 2048, 4, 4096], P(None, 'row', None, 'col'), may hold values from -6 to 6
- diag_inverses: float32 [2, 256, 256], replicated, as said below
- band: int32 [64, 64], replicated, may hold values from 0 to 2, as said below
Outputs:
- trailing: float32 [8, 2048, 4, 4096], P(None, 'row', None, 'col')
- panel_second: float32 [8, 2048, 256], P(None, 'row')
The draws below stay inside these ranges and needn't reach their ends.
Inputs may be any that keep to these rules, and one draw needn't show every extreme that they name: band is 0 on the diagonal tiles. `diag_inverses`: each is lower triangular with a positive diagonal.
All inputs are finite; a program needn't handle non-finite values.
Results may differ from the reference program's by a relative error of at most 0.0003.
Values sent between devices are 32-bit elements; how exact they have to be, the bound alone decides.
No kernel may reach another device: no remote copies, remote signals or barrier semaphores. Data moves between devices by JAX's collectives and lax.ppermute only.
A program may use at most 128 MiB of HBM per device.

```python
import jax
import jax.numpy as jnp
from jax import lax

NB = 256
TC = 4
TR = 8
NT = 64
N_ROW = 8
N_COL = 16


def draw_matrix(key, part):
    key = jax.random.fold_in(key, 3)
    shape = (TR, N_ROW, NB, TC, N_COL, NB)
    values = jnp.clip(jax.random.normal(key, shape, jnp.float32), -6.0, 6.0)
    tile_rows = (jnp.arange(TR)[:, None] * N_ROW + jnp.arange(N_ROW)[None, :]).reshape(TR, N_ROW, 1, 1, 1, 1)
    tile_cols = (jnp.arange(TC)[:, None] * N_COL + jnp.arange(N_COL)[None, :]).reshape(1, 1, 1, TC, N_COL, 1)
    distance = jnp.abs(tile_rows - tile_cols).astype(jnp.float32)
    envelope = jnp.exp(distance * (-6.0 / NT))
    return (values * envelope).reshape(TR, N_ROW * NB, TC, N_COL * NB)


def draw_band(key, part):
    key = jax.random.fold_in(key, 5)
    index = jnp.arange(NT)
    distance = jnp.abs(index[:, None] - index[None, :])
    noise = jax.random.randint(key, (NT, NT), 0, 2)
    near = 16 * distance >= 7 * NT
    middle = 16 * distance >= 8 * NT
    beyond = 16 * distance >= 12 * NT
    classes = jnp.where(beyond, 2, jnp.where(middle, 1 + noise, jnp.where(near, noise, 0)))
    return classes.astype(jnp.int32)


def draw_diag_inverses(key, part):
    key = jax.random.fold_in(key, 11)
    first, second = jax.random.split(key)
    spread = 0.3 / NB ** 0.5
    below = jax.random.normal(first, (2, NB, NB), jnp.float32) * spread
    index = jnp.arange(NB)
    lower = (index[:, None] > index[None, :]).astype(jnp.float32)
    diagonal = jax.random.uniform(second, (2, NB), jnp.float32, 0.1, 0.3)
    ident = (index[:, None] == index[None, :]).astype(jnp.float32)
    return below * lower + diagonal[:, :, None] * ident


def setup_inputs(seed: int = 0) -> dict:
    splits = jax.random.split(jax.random.key(seed), 4)
    return {
        "matrix": draw_matrix(jax.random.fold_in(splits[3], 71), 0),
        "diag_inverses": draw_diag_inverses(jax.random.fold_in(splits[3], 71), 0),
        "band": draw_band(jax.random.fold_in(splits[3], 71), 0),
    }


def contribution(rows, panel, classes):
    full = jnp.dot(rows, panel.T, precision=lax.Precision.HIGHEST, preferred_element_type=jnp.float32)
    low = jnp.dot(rows.astype(jnp.bfloat16), panel.astype(jnp.bfloat16).T, preferred_element_type=jnp.float32)
    expanded = jnp.repeat(classes, NB)
    return jnp.where(expanded == 0, full, jnp.where(expanded == 1, low, jnp.zeros_like(full)))


def update(whole, panel, band):
    order = whole.shape[0]
    tiles = whole.reshape(NT, NB, order)
    pieces = panel.reshape(NT, NB, NB)

    def one_row(items):
        block, rows, classes = items
        return block - contribution(rows, panel, classes)

    return lax.map(one_row, (tiles, pieces, band)).reshape(order, order)


def reference(matrix, diag_inverses, band):
    order = NT * NB
    whole = matrix.reshape(order, order)
    panel_first = jnp.dot(whole[:, 0:NB], diag_inverses[0].T, precision=lax.Precision.HIGHEST, preferred_element_type=jnp.float32)
    whole = update(whole, panel_first, band)
    panel_second = jnp.dot(whole[:, NB:2 * NB], diag_inverses[1].T, precision=lax.Precision.HIGHEST, preferred_element_type=jnp.float32)
    whole = update(whole, panel_second, band)
    return whole.reshape(matrix.shape), panel_second.reshape(TR, N_ROW * NB, NB)
```

```python
import jax
import jax.numpy as jnp
from jax import lax
from jax.experimental import pallas as pl
from jax.experimental.pallas import tpu as pltpu
from jax.sharding import PartitionSpec as P

NB = 256
HALF = 128
TR = 8
TC = 4
N_ROW = 8
N_COL = 16
SIDE = 4
F32 = jnp.float32
BF16 = jnp.bfloat16


def split(value):
    high = value.astype(BF16)
    return high, (value - high.astype(F32)).astype(BF16)


def dot(a, b):
    return jnp.dot(a, b, preferred_element_type=F32)


def dot3(a, b_high, b_low):
    a_high, a_low = split(a)
    return dot(a_high, b_high) + (dot(a_high, b_low) + dot(a_low, b_high))


def shift_x(value, by):
    pairs = [(x * SIDE + z, (x + by) % SIDE * SIDE + z) for x in range(SIDE) for z in range(SIDE)]
    return lax.ppermute(value, "col", pairs)


def shift_z(value, by):
    pairs = [(x * SIDE + z, x * SIDE + (z + by) % SIDE) for x in range(SIDE) for z in range(SIDE)]
    return lax.ppermute(value, "col", pairs)


def shift_y(value, by):
    pairs = [(y * 2 + k, (y + by) % SIDE * 2 + k) for y in range(SIDE) for k in range(2)]
    return lax.ppermute(value, "row", pairs)


def swap_core(value):
    return lax.ppermute(value, "row", [(r, r ^ 1) for r in range(N_ROW)])


def to_columns(value, shift):
    pairs = []
    for r in range(N_ROW):
        for c in range(N_COL):
            k = (c - shift) % N_COL
            column = r + N_ROW * (k // 2 % 2)
            place = k // 4 * 2 + k % 2
            pairs.append((r * N_COL + c, place * N_COL + column))
    return lax.ppermute(value, ("row", "col"), pairs)


def gather_plane(own, first, second):
    got = {(0, 0): own}
    got[1, 0] = first(own, 1)
    got[3, 0] = first(own, -1)
    got[2, 0] = first(got[1, 0], 1)
    for a in (0, 1, 3, 2):
        got[a, 1] = second(got[a, 0], 1)
        got[a, 3] = second(got[a, 0], -1)
    for a in (0, 1, 3, 2):
        got[a, 2] = second(got[a, 1], 1) if a < 2 else second(got[a, 3], -1)
    return got


def gather_rows(own):
    got = {0: own}
    got[1] = shift_y(own, 1)
    got[3] = shift_y(own, -1)
    got[2] = shift_y(got[1], 1)
    return {(a, b): (swap_core(got[a]) if b else got[a]) for a in range(SIDE) for b in range(2)}


def pick_kernel(*refs):
    sources, first, second, sems = refs[:N_COL], refs[N_COL], refs[N_COL + 1], refs[N_COL + 2]
    me = lax.axis_index("col")
    for d in range(N_COL):

        @pl.when(me == d)
        def _():
            pltpu.make_async_copy(sources[d], first, sems.at[0]).start()

        @pl.when(lax.rem(me + N_COL - 1, N_COL) == d)
        def _():
            pltpu.make_async_copy(sources[d], second, sems.at[1]).start()

    pltpu.make_async_copy(sources[0], first, sems.at[0]).wait()
    pltpu.make_async_copy(sources[0], second, sems.at[1]).wait()


def pick(sources):
    shape = jax.ShapeDtypeStruct((HALF, NB), F32)
    return pl.pallas_call(
        pick_kernel,
        out_shape=(shape, shape),
        in_specs=[pl.BlockSpec(memory_space=pl.ANY)] * N_COL,
        out_specs=[pl.BlockSpec(memory_space=pl.ANY)] * 2,
        scratch_shapes=[pltpu.SemaphoreType.DMA((2,))],
        name="pick_pieces",
    )(*sources)


ROWS = TR * NB
COLS = TC * NB


def solve_kernel(*refs):
    n = SIDE * SIDE
    first, second, cols = refs[:n], refs[n : 2 * n], refs[2 * n : 2 * n + N_ROW]
    pivot, inv, row_class, col_class = refs[2 * n + N_ROW : 2 * n + N_ROW + 4]
    row_high, row_low, col_high, col_low, panel = refs[2 * n + N_ROW + 4 : 2 * n + N_ROW + 9]
    raw, = refs[2 * n + N_ROW + 9 :]
    r, c = lax.axis_index("row"), lax.axis_index("col")
    x, z = lax.div(c, SIDE), lax.rem(c, SIDE)
    y, core = lax.div(r, 2), lax.rem(r, 2)
    for a in range(SIDE):
        for b in range(SIDE):
            k = lax.rem(x + SIDE - b, SIDE) * SIDE + lax.rem(z + SIDE - a, SIDE)
            raw[0, pl.ds(pl.multiple_of(k * HALF, HALF), HALF), :] = first[a * SIDE + b][...]
            k = lax.rem(x + SIDE - a, SIDE) * SIDE + lax.rem(z + SIDE - b, SIDE)
            k = lax.rem(k + N_COL - 1, N_COL)
            raw[1, pl.ds(pl.multiple_of(k * HALF, HALF), HALF), :] = second[a * SIDE + b][...]
    for a in range(SIDE):
        for b in range(2):
            k = lax.rem(y + SIDE - a, SIDE) * 2 + lax.rem(core + b, 2)
            at = pl.ds(pl.multiple_of(ROWS + k * HALF, HALF), HALF)
            raw[0, at, :] = cols[a * 2 + b][0]
            raw[1, at, :] = cols[a * 2 + b][1]
    inv0 = split(inv[0].T)
    inv1 = split(inv[1].T)
    one_high, one_low = split(dot3(pivot[...], *inv0).T)

    def solve(at, code):
        p1 = dot3(raw[0, at, :], *inv0)
        high, low = split(p1)
        full = dot(high, one_high)
        rest = dot(high, one_low) + dot(low, one_high)
        used = jnp.where(code == 2, 0.0, full + jnp.where(code == 0, rest, 0.0))
        return high, low, dot3(raw[1, at, :] - used, *inv1)

    def rows(p, carry):
        at = pl.ds(pl.multiple_of(p * NB, NB), NB)
        high, low, p2 = solve(at, row_class[p, 0])
        panel[p] = p2
        row_high[p, :, :NB], row_low[p, :, :NB] = high, low
        row_high[p, :, NB:], row_low[p, :, NB:] = split(p2)
        return carry

    def columns(q, carry):
        at = pl.ds(pl.multiple_of(ROWS + q * NB, NB), NB)
        high, low, p2 = solve(at, col_class[q, 0])
        col_high[q, :NB, :] = high.astype(F32).T.astype(BF16)
        col_low[q, :NB, :] = low.astype(F32).T.astype(BF16)
        col_high[q, NB:, :], col_low[q, NB:, :] = split(p2.T)
        return carry

    lax.fori_loop(0, TC, columns, 0)
    lax.fori_loop(0, TR, rows, 0)


def solve_panels(first, second, cols, pivot, inv, row_class, col_class):
    vmem = pl.BlockSpec(memory_space=pltpu.VMEM)
    smem = pl.BlockSpec(memory_space=pltpu.SMEM)
    arrays = [*first, *second, *cols, pivot, inv]
    return pl.pallas_call(
        solve_kernel,
        out_shape=(
            jax.ShapeDtypeStruct((TR, NB, 2 * NB), BF16),
            jax.ShapeDtypeStruct((TR, NB, 2 * NB), BF16),
            jax.ShapeDtypeStruct((TC, 2 * NB, NB), BF16),
            jax.ShapeDtypeStruct((TC, 2 * NB, NB), BF16),
            jax.ShapeDtypeStruct((TR, NB, NB), F32),
        ),
        in_specs=[vmem] * len(arrays) + [smem] * 2,
        out_specs=[vmem] * 5,
        scratch_shapes=[pltpu.VMEM((2, ROWS + COLS, NB), F32)],
        compiler_params=pltpu.CompilerParams(vmem_limit_bytes=40 * 1024 * 1024),
        name="solve_panels",
    )(*arrays, row_class, col_class)


def update_kernel(classes, matrix, row_high, row_low, col_high, col_low, out):
    p = pl.program_id(0)
    for q in range(TC):
        code = classes[p, q]

        def write(acc):
            for b in range(2):
                at = pl.ds(b * TC + q, NB, stride=2 * TC)
                out[0, at, :] = matrix[0, at, :] - acc[:, b * HALF : (b + 1) * HALF]

        @pl.when(code == 0)
        def _():
            high = row_high[0]
            acc = dot(high, col_high[q]) + (dot(high, col_low[q]) + dot(row_low[0], col_high[q]))
            write(acc)

        @pl.when(code == 1)
        def _():
            write(dot(row_high[0], col_high[q]))

        @pl.when(code == 2)
        def _():
            for b in range(2):
                at = pl.ds(b * TC + q, NB, stride=2 * TC)
                out[0, at, :] = matrix[0, at, :]


def update(matrix, classes, row_high, row_low, col_high, col_low):
    lines = NB * TC * 2
    view = matrix.reshape(TR, NB, TC, 2, HALF).transpose(0, 1, 3, 2, 4).reshape(TR, lines, HALF)
    block = pl.BlockSpec((1, lines, HALF), lambda p: (p, 0, 0))
    rows = pl.BlockSpec((1, NB, 2 * NB), lambda p: (p, 0, 0))
    whole = pl.BlockSpec((TC, 2 * NB, NB), lambda p: (0, 0, 0))
    out = pl.pallas_call(
        update_kernel,
        grid=(TR,),
        out_shape=jax.ShapeDtypeStruct((TR, lines, HALF), F32),
        in_specs=[pl.BlockSpec(memory_space=pltpu.SMEM), block, rows, rows, whole, whole],
        out_specs=block,
        compiler_params=pltpu.CompilerParams(vmem_limit_bytes=40 * 1024 * 1024),
        name="update_tiles",
    )(classes, view, row_high, row_low, col_high, col_low)
    return out.reshape(TR, NB, 2, TC, HALF).transpose(0, 1, 3, 2, 4).reshape(TR, NB, TC, NB)


def body(matrix, diag_inverses, band):
    row, col = lax.axis_index("row"), lax.axis_index("col")
    grid = band.reshape(TR, N_ROW, TC, N_COL)
    classes = lax.dynamic_slice(grid, (0, row, 0, col), (TR, 1, TC, 1)).reshape(TR, TC)
    second_class = band[:, 1]
    row_class = lax.dynamic_slice(second_class.reshape(TR, N_ROW), (0, row), (TR, 1))
    col_class = lax.dynamic_slice(second_class.reshape(TC, N_COL), (0, col), (TC, 1))

    column = matrix[:, :, 0, :]
    pivot = lax.psum(jnp.where((row == 1) & (col == 0), column[0], 0.0), ("row", "col"))
    pieces = column.reshape(N_COL, HALF, NB)
    sent = [pieces[0]]
    for d in range(1, N_COL):
        sent.append(lax.ppermute(pieces[d], "col", [(0, d), (1, (d + 1) % N_COL)]))
    piece1, piece2 = pick(sent)
    own_cols = jnp.stack([to_columns(piece1, 0), to_columns(piece2, 1)])
    got1 = gather_plane(piece1, shift_z, shift_x)
    got2 = gather_plane(piece2, shift_x, shift_z)
    got_cols = gather_rows(own_cols)
    order = [(a, b) for a in range(SIDE) for b in range(SIDE)]
    first = [got1[k] for k in order]
    second = [got2[k] for k in order]
    cols = [got_cols[a, b] for a in range(SIDE) for b in range(2)]
    row_high, row_low, col_high, col_low, panel = solve_panels(
        first, second, cols, pivot, diag_inverses, row_class, col_class
    )
    return update(matrix, classes, row_high, row_low, col_high, col_low), panel


def solution(mesh):
    in_specs = (P(None, "row", None, "col"), P(), P())
    out_specs = (P(None, "row", None, "col"), P(None, "row", None))
    return jax.shard_map(body, mesh=mesh, in_specs=in_specs, out_specs=out_specs, check_vma=False)
```

```python
import jax
import jax.numpy as jnp
from jax import lax
from jax.experimental import pallas as pl
from jax.experimental.pallas import tpu as pltpu
from jax.sharding import PartitionSpec as P

NB = 256
HALF = 128
TR = 8
TC = 4
N_ROW = 8
N_COL = 16
SIDE = 4
F32 = jnp.float32
BF16 = jnp.bfloat16


def split(value):
    high = value.astype(BF16)
    return high, (value - high.astype(F32)).astype(BF16)


def dot(a, b):
    return jnp.dot(a, b, preferred_element_type=F32)


def dot3(a, weights):
    high, low = split(a)
    return dot(jnp.concatenate([high, high, low], axis=1), weights)


def deep(value):
    high, low = split(value)
    return jnp.concatenate([high, low, high], axis=0)


def shift_x(value, by):
    pairs = [(x * SIDE + z, (x + by) % SIDE * SIDE + z) for x in range(SIDE) for z in range(SIDE)]
    return lax.ppermute(value, "col", pairs)


def shift_z(value, by):
    pairs = [(x * SIDE + z, x * SIDE + (z + by) % SIDE) for x in range(SIDE) for z in range(SIDE)]
    return lax.ppermute(value, "col", pairs)


def shift_y(value, by):
    pairs = [(y * 2 + k, (y + by) % SIDE * 2 + k) for y in range(SIDE) for k in range(2)]
    return lax.ppermute(value, "row", pairs)


def swap_core(value):
    return lax.ppermute(value, "row", [(r, r ^ 1) for r in range(N_ROW)])


def to_columns(value):
    pairs = []
    for r in range(N_ROW):
        for c in range(N_COL):
            column = r + N_ROW * (c // 2 % 2)
            place = c // 4 * 2 + c % 2
            pairs.append((r * N_COL + c, place * N_COL + column))
    return lax.ppermute(value, ("row", "col"), pairs)


def spread_pivot(tile, row):
    def along_y(by):
        return {1: (1 + 2 * by) % N_ROW}

    up = lax.ppermute(tile, "row", complete(along_y(1), N_ROW))
    down = lax.ppermute(tile, "row", complete(along_y(-1), N_ROW))
    far = lax.ppermute(tile, "row", complete(along_y(2), N_ROW))
    odd = jnp.where(row == 3, up, jnp.where(row == 7, down, jnp.where(row == 5, far, tile)))
    return jnp.where(row % 2 == 1, odd, swap_core(odd))


def complete(moves, size):
    pairs = dict(moves)
    for device in range(size):
        if device not in pairs and device not in pairs.values():
            pairs[device] = device
    free = [device for device in range(size) if device not in pairs.values()]
    for device in range(size):
        if device not in pairs:
            pairs[device] = free.pop(0)
    return sorted(pairs.items())


ORDER = (4, 12, 1, 8, 3, 5, 13, 9, 2, 7, 15, 11, 6, 14, 10)


def scatter_pieces(column, col):
    pieces = column.reshape(SIDE, SIDE, HALF, NB)
    turned = jnp.concatenate([pieces[:, 1:], pieces[:, :1]], axis=1)
    pieces = jnp.where(col == 1, turned, pieces).reshape(N_COL, HALF, NB)
    piece1 = piece2 = pieces[0]
    got = {}
    for d in ORDER:
        other = d // SIDE * SIDE + (d + 1) % SIDE
        got[d] = lax.ppermute(pieces[d], "col", complete({0: d, 1: other}, N_COL))
    for d in ORDER:
        other = d // SIDE * SIDE + (d + 1) % SIDE
        piece1 = jnp.where(col == d, got[d], piece1)
        piece2 = jnp.where(col == other, got[d], piece2)
    return piece1, piece2


RELAY = (0, 1, 3, 2)


def gather_all(piece1, piece2):
    barrier = lax.optimization_barrier
    z_near, z_back, x_near, x_back, own = barrier((
        shift_z(piece1, 1),
        shift_z(piece1, -1),
        shift_x(piece2, 1),
        shift_x(piece2, -1),
        to_columns(jnp.concatenate([piece1, piece2], axis=0)),
    ))
    z_far, x_far, y_near, y_back = barrier((
        shift_z(z_near, 1),
        shift_x(x_near, 1),
        shift_y(own, 1),
        shift_y(own, -1),
    ))
    line1 = jnp.stack([piece1, z_near, z_back, z_far])
    line2 = jnp.stack([piece2, x_near, x_back, x_far])
    near1, back1, near2, back2, y_far = barrier((
        shift_x(line1, 1),
        shift_x(line1, -1),
        shift_z(line2, 1),
        shift_z(line2, -1),
        shift_y(y_near, 1),
    ))
    cols = jnp.stack([own, y_near, y_back, y_far])
    far1, far2, other1, other2, other_cols = barrier((
        shift_x(near1[:2], 1),
        shift_x(back1[2:], -1),
        shift_z(near2[:2], 1),
        shift_z(back2[2:], -1),
        swap_core(cols),
    ))
    pieces1 = [line1, near1, back1, far1, far2]
    pieces2 = [line2, near2, back2, other1, other2]
    return pieces1, pieces2, [cols, other_cols]


def find_piece(pieces, x, z):
    line, near, back, far_near, far_back = pieces
    far = jnp.concatenate([far_near, far_back], axis=0)
    block = jnp.where(x == 0, line, jnp.where(x == 1, near, jnp.where(x == 3, back, far)))
    place = jnp.where(z < 2, z, 5 - z)
    return lax.dynamic_index_in_dim(block, place, 0, keepdims=False)


VMEM = pl.BlockSpec(memory_space=pltpu.VMEM)
SMEM = pl.BlockSpec(memory_space=pltpu.SMEM)
ANY = pl.BlockSpec(memory_space=pl.ANY)
LIMIT = pltpu.CompilerParams(vmem_limit_bytes=40 * 1024 * 1024)
ROWS = TR * NB
COLS = TC * NB


def rows_at(index, size):
    return pl.ds(pl.multiple_of(index * size, size), size)


def plane_copies(pieces, raw, sems, swapped):
    c = lax.axis_index("col")
    x, z = lax.div(c, SIDE), lax.rem(c, SIDE)
    line, near, back, far_near, far_back = pieces
    sources = [(line.at[i], RELAY[i], 0) for i in range(4)]
    sources += [(near.at[i], RELAY[i], 1) for i in range(4)]
    sources += [(back.at[i], RELAY[i], 3) for i in range(4)]
    sources += [(far_near.at[i], RELAY[i], 2) for i in range(2)]
    sources += [(far_back.at[i], RELAY[i + 2], 2) for i in range(2)]
    copies = []
    for n, (ref, first, second) in enumerate(sources):
        dx, dz = (first, second) if swapped else (second, first)
        k = lax.rem(x + SIDE - dx, SIDE) * SIDE + lax.rem(z + SIDE - dz, SIDE)
        copies.append(pltpu.make_async_copy(ref, raw.at[rows_at(k, HALF), :], sems.at[n]))
    return copies


def column_copies(pieces, raw, sems, at, size):
    r = lax.axis_index("row")
    y, core = lax.div(r, 2), lax.rem(r, 2)
    copies = []
    for b in range(2):
        for i in range(SIDE):
            k = lax.rem(y + SIDE - RELAY[i], SIDE) * 2 + lax.rem(core + b, 2)
            ref = pieces[b].at[i, pl.ds(at, size), :]
            copies.append(pltpu.make_async_copy(ref, raw.at[rows_at(k, size), :], sems.at[b * SIDE + i]))
    return copies


def first_kernel(*refs):
    pieces, cols, inv = refs[:5], refs[5:7], refs[7]
    row_high, row_low, col_high, col_low, turned_high, turned_low = refs[8:14]
    raw, raw_cols, sems, col_sems = refs[14:]
    copies = plane_copies(pieces, raw, sems, False)
    col_copies = column_copies(cols, raw_cols, col_sems, 0, HALF)
    for copy in col_copies + copies:
        copy.start()
    weights = deep(inv[0].T)
    for copy in col_copies:
        copy.wait()

    def column(q, carry):
        solved = dot3(raw_cols[rows_at(q, NB), :], weights)
        col_high[q], col_low[q] = split(solved)
        turned_high[q], turned_low[q] = split(solved.T)
        return carry

    def row(p, carry):
        solved = dot3(raw[rows_at(p, 2 * NB), :], weights).reshape(2, NB, NB)
        high, low = split(solved)
        row_high[pl.ds(2 * p, 2)] = high
        row_low[pl.ds(2 * p, 2)] = low
        return carry

    lax.fori_loop(0, TC, column, 0, unroll=2)
    for copy in copies:
        copy.wait()
    lax.fori_loop(0, TR // 2, row, 0)


def solve_first(pieces, cols, inv):
    shapes = [jax.ShapeDtypeStruct((n, NB, NB), BF16) for n in (TR, TR, TC, TC, TC, TC)]
    return pl.pallas_call(
        first_kernel,
        out_shape=shapes,
        in_specs=[ANY] * 7 + [VMEM],
        out_specs=[VMEM] * 6,
        scratch_shapes=[
            pltpu.VMEM((ROWS, NB), F32),
            pltpu.VMEM((COLS, NB), F32),
            pltpu.SemaphoreType.DMA((N_COL,)),
            pltpu.SemaphoreType.DMA((N_ROW,)),
        ],
        compiler_params=LIMIT,
        cost_estimate=pl.CostEstimate(flops=12 * 3 * 2 * NB**3, bytes_accessed=6 * 2**20, transcendentals=0),
        name="solve_first",
    )(*pieces, *cols, inv)


def second_kernel(*refs):
    pieces, cols, inv, pivot, row_class, col_class = refs[:5], refs[5:7], *refs[7:11]
    row_high1, row_low1, col_high1, col_low1 = refs[11:15]
    panel, row_high, row_low, turned_high, turned_low = refs[15:20]
    raw, raw_cols, sems, col_sems = refs[20:]
    copies = plane_copies(pieces, raw, sems, True)
    col_copies = column_copies(cols, raw_cols, col_sems, HALF, HALF)
    for copy in col_copies + copies:
        copy.start()
    weights0 = deep(inv[0].T)
    weights1 = deep(inv[1].T)
    one = dot3(pivot[...], weights0).T
    one_high, one_low = split(one)
    rest_weights = jnp.concatenate([one_low, one_high], axis=0)

    def used(high, low, code):
        full = dot(high, one_high)
        rest = dot(jnp.concatenate([high, low], axis=1), rest_weights)
        return jnp.where(code == 2, 0.0, full + jnp.where(code == 0, rest, 0.0))

    for copy in col_copies:
        copy.wait()

    def column(q, carry):
        tile = raw_cols[rows_at(q, NB), :] - used(col_high1[q], col_low1[q], col_class[q, 0])
        solved = dot3(tile, weights1)
        turned_high[q], turned_low[q] = split(solved.T)
        return carry

    def row(p, carry):
        tile = raw[rows_at(p, NB), :] - used(row_high1[p], row_low1[p], row_class[p, 0])
        solved = dot3(tile, weights1)
        panel[p] = solved
        row_high[p], row_low[p] = split(solved)
        return carry

    lax.fori_loop(0, TC, column, 0, unroll=2)
    for copy in copies:
        copy.wait()
    lax.fori_loop(0, TR, row, 0, unroll=2)


def solve_second(pieces, cols, inv, pivot, row_class, col_class, first):
    shapes = [jax.ShapeDtypeStruct((TR, NB, NB), F32)]
    shapes += [jax.ShapeDtypeStruct((n, NB, NB), BF16) for n in (TR, TR, TC, TC)]
    return pl.pallas_call(
        second_kernel,
        out_shape=shapes,
        in_specs=[ANY] * 7 + [VMEM] * 2 + [SMEM] * 2 + [VMEM] * 4,
        out_specs=[VMEM] * 5,
        scratch_shapes=[
            pltpu.VMEM((ROWS, NB), F32),
            pltpu.VMEM((COLS, NB), F32),
            pltpu.SemaphoreType.DMA((N_COL,)),
            pltpu.SemaphoreType.DMA((N_ROW,)),
        ],
        compiler_params=LIMIT,
        cost_estimate=pl.CostEstimate(flops=24 * 3 * 2 * NB**3, bytes_accessed=12 * 2**20, transcendentals=0),
        name="solve_second",
    )(*pieces, *cols, inv, pivot, row_class, col_class, *first)


STEP = 2


def update_kernel(classes, matrix, high1, low1, high2, low2, chigh1, clow1, chigh2, clow2, out, product):
    step = pl.program_id(0)
    size = STEP * NB
    high = jnp.concatenate([high1[...].reshape(size, NB), high2[...].reshape(size, NB)], axis=1)
    low = jnp.concatenate([low1[...].reshape(size, NB), low2[...].reshape(size, NB)], axis=1)
    both = jnp.concatenate([high, low], axis=1)
    for q in range(TC):
        col_high = jnp.concatenate([chigh1[q], chigh2[q]], axis=0)
        col_low = jnp.concatenate([clow1[q], clow2[q]], axis=0)
        full = dot(high, col_high)
        rest = dot(both, jnp.concatenate([col_low, col_high], axis=0))
        for p in range(STEP):
            code = classes[step * STEP + p, q]
            at = slice(p * NB, (p + 1) * NB)
            total = jnp.where(code == 2, 0.0, full[at] + jnp.where(code == 0, rest[at], 0.0))
            for b in range(2):
                product[b * TC + q, at, :] = total[:, b * HALF : (b + 1) * HALF]
    lines = 2 * TC
    part = 32
    for p in range(STEP):
        for a in range(0, NB, part):
            turned = product[:, p * NB + a : p * NB + a + part, :].transpose(1, 0, 2).reshape(part * lines, HALF)
            at = pl.ds(a * lines, part * lines)
            out[p, at, :] = matrix[p, at, :] - turned


def update(matrix, classes, rows, cols):
    lines = NB * TC * 2
    view = matrix.reshape(TR, NB, TC, 2, HALF).transpose(0, 1, 3, 2, 4).reshape(TR, lines, HALF)
    block = pl.BlockSpec((STEP, lines, HALF), lambda p: (p, 0, 0))
    row = pl.BlockSpec((STEP, NB, NB), lambda p: (p, 0, 0))
    whole = pl.BlockSpec((TC, NB, NB), lambda p: (0, 0, 0))
    out = pl.pallas_call(
        update_kernel,
        grid=(TR // STEP,),
        out_shape=jax.ShapeDtypeStruct((TR, lines, HALF), F32),
        in_specs=[SMEM, block] + [row] * 4 + [whole] * 4,
        out_specs=block,
        scratch_shapes=[pltpu.VMEM((2 * TC, STEP * NB, HALF), F32)],
        compiler_params=LIMIT,
        name="update_tiles",
    )(classes, view, *rows, *cols)
    return out.reshape(TR, NB, 2, TC, HALF).transpose(0, 1, 3, 2, 4).reshape(TR, NB, TC, NB)


def body(matrix, diag_inverses, band):
    row, col = lax.axis_index("row"), lax.axis_index("col")
    grid = band.reshape(TR, N_ROW, TC, N_COL)
    classes = lax.dynamic_slice(grid, (0, row, 0, col), (TR, 1, TC, 1)).reshape(TR, TC)
    second_class = band[:, 1]
    row_class = lax.dynamic_slice(second_class.reshape(TR, N_ROW), (0, row), (TR, 1))
    col_class = lax.dynamic_slice(second_class.reshape(TC, N_COL), (0, col), (TC, 1))

    piece1, piece2 = scatter_pieces(matrix[:, :, 0, :], col)
    pieces1, pieces2, cols = gather_all(piece1, piece2)
    x, z = col // SIDE, col % SIDE
    first_half = find_piece(pieces1, x, z)
    second_half = find_piece(pieces1, x, (z + SIDE - 1) % SIDE)
    pivot = spread_pivot(jnp.concatenate([first_half, second_half], axis=0), row)
    row_high1, row_low1, col_high1, col_low1, turned_high1, turned_low1 = solve_first(pieces1, cols, diag_inverses)
    first = (row_high1, row_low1, col_high1, col_low1)
    panel, row_high2, row_low2, turned_high2, turned_low2 = solve_second(
        pieces2, cols, diag_inverses, pivot, row_class, col_class, first
    )
    rows = (row_high1, row_low1, row_high2, row_low2)
    turned = (turned_high1, turned_low1, turned_high2, turned_low2)
    return update(matrix, classes, rows, turned), panel


def solution(mesh):
    in_specs = (P(None, "row", None, "col"), P(), P())
    out_specs = (P(None, "row", None, "col"), P(None, "row", None))
    return jax.shard_map(body, mesh=mesh, in_specs=in_specs, out_specs=out_specs, check_vma=False)
```

```python
import functools

import jax
import jax.numpy as jnp
from jax import lax
from jax.experimental import pallas as pl
from jax.experimental.pallas import tpu as pltpu
from jax.sharding import PartitionSpec as P

NB = 256
HALF = 128
TR = 8
TC = 4
N_ROW = 8
N_COL = 16
SIDE = 4
F32 = jnp.float32
BF16 = jnp.bfloat16


def split(value):
    high = value.astype(BF16)
    return high, (value - high.astype(F32)).astype(BF16)


def dot(a, b):
    return jnp.dot(a, b, preferred_element_type=F32)


def dot3(a, weights):
    high, low = split(a)
    return dot(jnp.concatenate([high, high, low], axis=1), weights)


def deep(value):
    high, low = split(value)
    return jnp.concatenate([high, low, high], axis=0)


def shift_x(value, by):
    pairs = [(x * SIDE + z, (x + by) % SIDE * SIDE + z) for x in range(SIDE) for z in range(SIDE)]
    return lax.ppermute(value, "col", pairs)


def shift_z(value, by):
    pairs = [(x * SIDE + z, x * SIDE + (z + by) % SIDE) for x in range(SIDE) for z in range(SIDE)]
    return lax.ppermute(value, "col", pairs)


def shift_y(value, by):
    pairs = [(y * 2 + k, (y + by) % SIDE * 2 + k) for y in range(SIDE) for k in range(2)]
    return lax.ppermute(value, "row", pairs)


def swap_core(value):
    return lax.ppermute(value, "row", [(r, r ^ 1) for r in range(N_ROW)])


def to_columns(along_x, along_z, x, z):
    first, second = [], []
    for r in range(N_ROW):
        for a in range(SIDE):
            for b in range(SIDE):
                source = r * N_COL + a * SIDE + b
                first.append((source, (a // 2 * SIDE + b) * N_COL + r + N_ROW * (a % 2)))
                tile = b if a < 2 else (b + SIDE - 1) % SIDE
                second.append((source, (tile // 2 * SIDE + a) * N_COL + r + N_ROW * (tile % 2)))
    one = lax.dynamic_slice(along_x, (z * HALF, 0), (HALF, NB))
    two = lax.dynamic_slice(along_z, (x * HALF, 0), (HALF, NB))
    return lax.ppermute(one, ("row", "col"), first), lax.ppermute(two, ("row", "col"), second)


def choose(place, own, near, far, back):
    return jnp.where(place == 0, own, jnp.where(place == 1, near, jnp.where(place == 2, far, back)))


def join(one, two):
    return jnp.concatenate([one, two], axis=0)


def gather_all(raw, row, col):
    barrier = lax.optimization_barrier
    x, z = col // SIDE, col % SIDE
    after_z = (z + SIDE - 1) % SIDE

    xn, xb, zn, zb = barrier((
        shift_x(raw[NB : 2 * NB + HALF], 1),
        shift_x(raw[2 * NB + HALF : 4 * NB], -1),
        shift_z(raw[5 * NB : 6 * NB + HALF], 1),
        shift_z(raw[6 * NB + HALF :], -1),
    ))
    xc, xd, zc, zd = barrier((
        shift_x(xn[NB:], 1),
        shift_x(xb[:HALF], -1),
        shift_z(zn[NB:], 1),
        shift_z(zb[:HALF], -1),
    ))
    tile_a = choose(x, raw[:NB], xn[:NB], join(xc, xd), xb[HALF:])
    line_b = raw[4 * NB : 5 * NB], zn[:NB], join(zc, zd), zb[HALF:]
    tile_b = join(choose(z, *line_b), choose(after_z, *line_b))

    bn, bb, an, ab = barrier((
        shift_x(tile_b, 1),
        shift_x(tile_b, -1),
        shift_z(tile_a, 1),
        shift_z(tile_a, -1),
    ))
    bc, bd, ac, ad = barrier((
        shift_x(bn[:NB], 1),
        shift_x(bb[NB:], -1),
        shift_z(an[:HALF], 1),
        shift_z(ab[HALF:], -1),
    ))
    line_a = tile_a, an, join(ac, ad), ab
    along_x = join(choose(z, *line_a), choose(after_z, *line_a))
    along_z = choose(x, tile_b, bn, join(bc, bd), bb)

    corner = [(N_COL + z, N_COL + 2 * SIDE + z) for z in range(SIDE)]
    xn, xb, zn, zb, (part_a, part_b), pivot = barrier((
        shift_x(along_x, 1),
        shift_x(along_x, -1),
        shift_z(along_z, 1),
        shift_z(along_z, -1),
        to_columns(along_x, along_z, x, z),
        lax.ppermute(along_x[:NB], ("row", "col"), corner),
    ))
    own = join(part_a, part_b)
    pivot = choose(x, along_x[:NB], xn[:NB], pivot, xb[:NB])
    xc, xd, zc, zd, yn, yb, pivot_up, pivot_down = barrier((
        shift_x(xn[:NB], 1),
        shift_x(xb[NB:], -1),
        shift_z(zn[:NB], 1),
        shift_z(zb[NB:], -1),
        shift_y(own, 1),
        shift_y(own, -1),
        lax.ppermute(pivot, "row", [(1, 3)]),
        lax.ppermute(pivot, "row", [(1, 7)]),
    ))
    panel1 = [(along_x, 0), (xn, 0), (xc, 0), (xb, 0), (along_z, 0), (zn, 0), (zc, 0), (zb, 0)]
    panel2 = [(along_x, NB), (xn, NB), (xd, 0), (xb, NB), (along_z, NB), (zn, NB), (zd, 0), (zb, NB)]
    yc, yd, pivot_far = barrier((
        shift_y(yn[:HALF], 1),
        shift_y(yb[HALF:], -1),
        lax.ppermute(pivot_up, "row", [(3, 5)]),
    ))
    odd = jnp.where(row == 1, pivot, pivot_up + pivot_down + pivot_far)
    here = jnp.stack([own, yn, join(yc, yd), yb])
    there = swap_core(here)
    pivot = jnp.where(row % 2 == 1, odd, swap_core(odd))
    return panel1, panel2, [here, there], pivot


VMEM = pl.BlockSpec(memory_space=pltpu.VMEM)
SMEM = pl.BlockSpec(memory_space=pltpu.SMEM)
ANY = pl.BlockSpec(memory_space=pl.ANY)
LIMIT = pltpu.CompilerParams(vmem_limit_bytes=40 * 1024 * 1024)
ROWS = TR * NB
COLS = TC * NB


def rows_at(index, size):
    return pl.ds(pl.multiple_of(index * size, size), size)


def plane_copies(refs, starts, raw, sems, root):
    c = lax.axis_index("col")
    x, z = lax.div(c, SIDE), lax.rem(c, SIDE)
    copies = []
    for n in range(TR):
        line = x if n < SIDE else z + SIDE - root
        place = lax.rem(line + SIDE - n % SIDE, SIDE) + n // SIDE * SIDE
        source = refs[n].at[pl.ds(starts[n], NB), :]
        copies.append(pltpu.make_async_copy(source, raw.at[rows_at(place, NB), :], sems.at[n]))
    return copies


def column_copies(pieces, raw, sems):
    r = lax.axis_index("row")
    y, core = lax.div(r, 2), lax.rem(r, 2)
    copies = []
    for b in range(2):
        for i in range(SIDE):
            k = lax.rem(y + SIDE - i, SIDE) * 2 + lax.rem(core + b, 2)
            panel = lax.div(lax.rem(k, SIDE), 2)
            at = lax.div(k, SIDE) * 2 + lax.rem(k, 2)
            for part in range(2):
                source = pieces[b].at[i, pl.ds(part * HALF, HALF), :]
                target = raw.at[panel, rows_at(at + part * SIDE, HALF), :]
                copies.append(pltpu.make_async_copy(source, target, sems.at[(b * SIDE + i) * 2 + part]))
    return copies


def first_kernel(starts, *refs):
    pieces, inv, row_high, row_low, raw, sems = refs[:TR], *refs[TR:]
    copies = plane_copies(pieces, starts, raw, sems, 0)
    for copy in copies:
        copy.start()
    weights = deep(inv[0].T)
    for copy in copies:
        copy.wait()

    def row(p, carry):
        solved = dot3(raw[rows_at(p, 2 * NB), :], weights).reshape(2, NB, NB)
        high, low = split(solved)
        row_high[pl.ds(2 * p, 2)] = high
        row_low[pl.ds(2 * p, 2)] = low
        return carry

    lax.fori_loop(0, TR // 2, row, 0)


def solve_first(pieces, inv):
    return pl.pallas_call(
        functools.partial(first_kernel, tuple(start for _, start in pieces)),
        out_shape=[jax.ShapeDtypeStruct((TR, NB, NB), BF16)] * 2,
        in_specs=[ANY] * TR + [VMEM],
        out_specs=[VMEM] * 2,
        scratch_shapes=[pltpu.VMEM((ROWS, NB), F32), pltpu.SemaphoreType.DMA((TR,))],
        compiler_params=LIMIT,
        cost_estimate=pl.CostEstimate(flops=8 * 3 * 2 * NB**3, bytes_accessed=4 * 2**20, transcendentals=0),
        name="solve_first",
    )(*[array for array, _ in pieces], inv)


def second_kernel(starts, *refs):
    pieces, cols = refs[:TR], refs[TR : TR + 2]
    inv, pivot, row_class, col_class, row_high1, row_low1 = refs[TR + 2 : TR + 8]
    panel, row_high, row_low, high1, low1, high2, low2 = refs[TR + 8 : TR + 15]
    raw, raw_cols, sems, col_sems = refs[TR + 15 :]
    copies = plane_copies(pieces, starts, raw, sems, 1)
    col_copies = column_copies(cols, raw_cols, col_sems)
    for copy in copies + col_copies:
        copy.start()
    weights0 = deep(inv[0].T)
    weights1 = deep(inv[1].T)
    one_high, one_low = split(dot3(pivot[...], weights0).T)
    rest_weights = join(one_low, one_high)

    def used(high, low, code):
        full = dot(high, one_high)
        rest = dot(jnp.concatenate([high, low], axis=1), rest_weights)
        return jnp.where(code == 2, 0.0, full + jnp.where(code == 0, rest, 0.0))

    def row(p, carry):
        tile = raw[rows_at(p, NB), :] - used(row_high1[p], row_low1[p], row_class[p, 0])
        solved = dot3(tile, weights1)
        panel[p] = solved
        row_high[p], row_low[p] = split(solved)
        return carry

    def column(q, carry):
        first = dot3(raw_cols[0, rows_at(q, NB), :], weights0)
        high1[q], low1[q] = split(first.T)
        high, low = split(first)
        tile = raw_cols[1, rows_at(q, NB), :] - used(high, low, col_class[q, 0])
        high2[q], low2[q] = split(dot3(tile, weights1).T)
        return carry

    for copy in copies:
        copy.wait()
    lax.fori_loop(0, TR, row, 0, unroll=2)
    for copy in col_copies:
        copy.wait()
    lax.fori_loop(0, TC, column, 0, unroll=2)


def solve_second(pieces, cols, inv, pivot, row_class, col_class, first):
    shapes = [jax.ShapeDtypeStruct((TR, NB, NB), F32)]
    shapes += [jax.ShapeDtypeStruct((n, NB, NB), BF16) for n in (TR, TR, TC, TC, TC, TC)]
    return pl.pallas_call(
        functools.partial(second_kernel, tuple(start for _, start in pieces)),
        out_shape=shapes,
        in_specs=[ANY] * (TR + 2) + [VMEM] * 2 + [SMEM] * 2 + [VMEM] * 2,
        out_specs=[VMEM] * 7,
        scratch_shapes=[
            pltpu.VMEM((ROWS, NB), F32),
            pltpu.VMEM((2, COLS, NB), F32),
            pltpu.SemaphoreType.DMA((TR,)),
            pltpu.SemaphoreType.DMA((N_COL,)),
        ],
        compiler_params=LIMIT,
        cost_estimate=pl.CostEstimate(flops=28 * 3 * 2 * NB**3, bytes_accessed=12 * 2**20, transcendentals=0),
        name="solve_second",
    )(*[array for array, _ in pieces], *cols, inv, pivot, row_class, col_class, *first)


STEP = 2


def update_kernel(classes, matrix, high1, low1, high2, low2, chigh1, clow1, chigh2, clow2, out, product):
    step = pl.program_id(0)
    size = STEP * NB
    high = jnp.concatenate([high1[...].reshape(size, NB), high2[...].reshape(size, NB)], axis=1)
    low = jnp.concatenate([low1[...].reshape(size, NB), low2[...].reshape(size, NB)], axis=1)
    both = jnp.concatenate([high, low], axis=1)
    for q in range(TC):
        col_high = jnp.concatenate([chigh1[q], chigh2[q]], axis=0)
        col_low = jnp.concatenate([clow1[q], clow2[q]], axis=0)
        full = dot(high, col_high)
        rest = dot(both, jnp.concatenate([col_low, col_high], axis=0))
        for p in range(STEP):
            code = classes[step * STEP + p, q]
            at = slice(p * NB, (p + 1) * NB)
            total = jnp.where(code == 2, 0.0, full[at] + jnp.where(code == 0, rest[at], 0.0))
            for b in range(2):
                product[b * TC + q, at, :] = total[:, b * HALF : (b + 1) * HALF]
    lines = 2 * TC
    part = 32
    for p in range(STEP):
        for a in range(0, NB, part):
            turned = product[:, p * NB + a : p * NB + a + part, :].transpose(1, 0, 2).reshape(part * lines, HALF)
            at = pl.ds(a * lines, part * lines)
            out[p, at, :] = matrix[p, at, :] - turned


def update(matrix, classes, rows, cols):
    lines = NB * TC * 2
    view = matrix.reshape(TR, NB, TC, 2, HALF).transpose(0, 1, 3, 2, 4).reshape(TR, lines, HALF)
    block = pl.BlockSpec((STEP, lines, HALF), lambda p: (p, 0, 0))
    row = pl.BlockSpec((STEP, NB, NB), lambda p: (p, 0, 0))
    whole = pl.BlockSpec((TC, NB, NB), lambda p: (0, 0, 0))
    out = pl.pallas_call(
        update_kernel,
        grid=(TR // STEP,),
        out_shape=jax.ShapeDtypeStruct((TR, lines, HALF), F32),
        in_specs=[SMEM, block] + [row] * 4 + [whole] * 4,
        out_specs=block,
        scratch_shapes=[pltpu.VMEM((2 * TC, STEP * NB, HALF), F32)],
        compiler_params=LIMIT,
        name="update_tiles",
    )(classes, view, *rows, *cols)
    return out.reshape(TR, NB, 2, TC, HALF).transpose(0, 1, 3, 2, 4).reshape(TR, NB, TC, NB)


def body(matrix, diag_inverses, band):
    row, col = lax.axis_index("row"), lax.axis_index("col")
    grid = band.reshape(TR, N_ROW, TC, N_COL)
    classes = lax.dynamic_slice(grid, (0, row, 0, col), (TR, 1, TC, 1)).reshape(TR, TC)
    second_class = band[:, 1]
    row_class = lax.dynamic_slice(second_class.reshape(TR, N_ROW), (0, row), (TR, 1))
    col_class = lax.dynamic_slice(second_class.reshape(TC, N_COL), (0, col), (TC, 1))

    raw = matrix[:, :, 0, :].reshape(ROWS, NB)
    panel1, panel2, cols, pivot = gather_all(raw, row, col)
    first = solve_first(panel1, diag_inverses)
    panel, row_high2, row_low2, high1, low1, high2, low2 = solve_second(
        panel2, cols, diag_inverses, pivot, row_class, col_class, first
    )
    rows = (*first, row_high2, row_low2)
    return update(matrix, classes, rows, (high1, low1, high2, low2)), panel


def solution(mesh):
    in_specs = (P(None, "row", None, "col"), P(), P())
    out_specs = (P(None, "row", None, "col"), P(None, "row", None))
    return jax.shard_map(body, mesh=mesh, in_specs=in_specs, out_specs=out_specs, check_vma=False)
```

```python
import functools

import jax
import jax.numpy as jnp
from jax import lax
from jax.experimental import pallas as pl
from jax.experimental.pallas import tpu as pltpu
from jax.sharding import PartitionSpec as P

NB = 256
HALF = 128
TR = 8
TC = 4
N_ROW = 8
N_COL = 16
SIDE = 4
F32 = jnp.float32
BF16 = jnp.bfloat16


def split(value):
    high = value.astype(BF16)
    return high, (value - high.astype(F32)).astype(BF16)


def dot(a, b):
    return jnp.dot(a, b, preferred_element_type=F32)


def dot3(a, weights):
    high, low = split(a)
    return dot(jnp.concatenate([high, high, low], axis=1), weights)


def deep(value):
    high, low = split(value)
    return jnp.concatenate([high, low, high], axis=0)


def shift_plane(value, by, swapped):
    pairs = []
    for r in range(N_ROW):
        for x in range(SIDE):
            for z in range(SIDE):
                along_z = (r % 2 == 1) != swapped
                to = (x, (z + by) % SIDE) if along_z else ((x + by) % SIDE, z)
                pairs.append((r * N_COL + x * SIDE + z, r * N_COL + to[0] * SIDE + to[1]))
    return lax.ppermute(value, ("row", "col"), pairs)


def shift_line(value, by):
    return shift_plane(value, by, False)


def shift_cross(value, by):
    return shift_plane(value, by, True)


def send_far(value):
    pairs = []
    for r in range(N_ROW):
        for root in range(2):
            to = root + 2 if r % 2 else 2 * SIDE + root
            pairs.append((r * N_COL + root, r * N_COL + to))
    return lax.ppermute(value, ("row", "col"), pairs)


def shift_y(value, by):
    pairs = [(y * 2 + k, (y + by) % SIDE * 2 + k) for y in range(SIDE) for k in range(2)]
    return lax.ppermute(value, "row", pairs)


def swap_core(value):
    return lax.ppermute(value, "row", [(r, r ^ 1) for r in range(N_ROW)])


def to_columns(value):
    pairs = []
    for r in range(N_ROW):
        for x in range(SIDE):
            for z in range(SIDE):
                line, cross = (z, x) if r % 2 else (x, z)
                panel, odd = cross // 2, cross % 2
                quarter = (line - panel * (r % 2)) % SIDE
                target = (quarter * 2 + panel) * N_COL + r + N_ROW * odd
                pairs.append((r * N_COL + x * SIDE + z, target))
    return lax.ppermute(value, ("row", "col"), pairs)


def relay_y(near, back, core):
    pairs = [(r, (r + (2 if r % 2 == 0 else -2)) % N_ROW) for r in range(N_ROW)]
    return lax.ppermute(jnp.where(core == 0, near, back), "row", pairs)


def choose(place, own, near, far, back):
    return jnp.where(place == 0, own, jnp.where(place == 1, near, jnp.where(place == 2, far, back)))


def join(one, two):
    return jnp.concatenate([one, two], axis=0)


PAIR = 2 * NB


def gather_all(raw, row, col):
    barrier = lax.optimization_barrier
    x, z, core = col // SIDE, col % SIDE, row % 2
    line, cross = jnp.where(core == 0, x, z), jnp.where(core == 0, z, x)

    near, back, far = barrier((
        shift_line(raw[PAIR : 2 * PAIR], 1),
        shift_line(raw[3 * PAIR :], -1),
        send_far(raw[2 * PAIR : 3 * PAIR]),
    ))
    places = raw[:PAIR], near, far, back
    own1 = choose(line, *places)
    own2 = choose((line + SIDE - 1) % SIDE, *places)

    both = join(own1, own2)
    near, back = barrier((shift_cross(both, 1), shift_cross(both, -1)))
    far1, far2 = barrier((shift_cross(near[:PAIR], 1), shift_cross(back[PAIR:], -1)))
    block1 = choose(cross, own1, near[:PAIR], far1, back[:PAIR])
    after = (cross + SIDE - 1) % SIDE
    block2 = jnp.where(
        core == 0,
        choose(after, own1, near[:PAIR], far1, back[:PAIR]),
        choose(cross, own2, near[PAIR:], far2, back[PAIR:]),
    )
    block = join(block1, block2)
    tile = lax.dynamic_slice(block, (cross * NB, 0), (NB, NB))
    block, tile, pivot = barrier((block, tile, block1[:NB]))

    corner = [(N_COL + SIDE * a, N_COL + SIDE * a + 2) for a in range(SIDE)]
    near, back, own, pivot_far = barrier((
        shift_line(block, 1),
        shift_line(block, -1),
        to_columns(tile),
        lax.ppermute(pivot, ("row", "col"), corner),
    ))
    pivot = choose(z, pivot, near[:NB], pivot_far, back[:NB])
    far1, far2, up, down, own_other, pivot_up, pivot_down = barrier((
        shift_line(near[:PAIR], 1),
        shift_line(back[PAIR:], -1),
        shift_y(own, 1),
        shift_y(own, -1),
        swap_core(own),
        lax.ppermute(pivot, "row", [(1, 3)]),
        lax.ppermute(pivot, "row", [(1, 7)]),
    ))
    panel1 = [(block, 0), (near, 0), (far1, 0), (back, 0)]
    panel2 = [(block, PAIR), (near, PAIR), (far2, 0), (back, PAIR)]
    last, up_other, down_other, pivot_far = barrier((
        relay_y(up, down, core),
        swap_core(up),
        swap_core(down),
        lax.ppermute(pivot_up, "row", [(3, 5)]),
    ))
    odd = jnp.where(row == 1, pivot, pivot_up + pivot_down + pivot_far)
    cols = [own, up, last, down, own_other, up_other, swap_core(last), down_other]
    pivot = jnp.where(core == 1, odd, swap_core(odd))
    return panel1, panel2, cols, pivot


VMEM = pl.BlockSpec(memory_space=pltpu.VMEM)
SMEM = pl.BlockSpec(memory_space=pltpu.SMEM)
ANY = pl.BlockSpec(memory_space=pl.ANY)
LIMIT = pltpu.CompilerParams(vmem_limit_bytes=24 * 1024 * 1024)
ROWS = TR * NB
COLS = TC * NB


def rows_at(index, size):
    return pl.ds(pl.multiple_of(index * size, size), size)


def plane_copies(refs, starts, raw, sems, panel):
    c, core = lax.axis_index("col"), lax.rem(lax.axis_index("row"), 2)
    x, z = lax.div(c, SIDE), lax.rem(c, SIDE)
    line = jnp.where(core == 0, x, z + SIDE - panel)
    copies = []
    for n in range(SIDE):
        place = lax.rem(line + SIDE - n, SIDE)
        source = refs[n].at[pl.ds(starts[n], PAIR), :]
        copies.append(pltpu.make_async_copy(source, raw.at[rows_at(place, PAIR), :], sems.at[n]))
    return copies


def column_copies(tiles, raw, sems):
    r = lax.axis_index("row")
    y, core = lax.div(r, 2), lax.rem(r, 2)
    copies = []
    for n in range(N_ROW):
        k = lax.rem(y + SIDE - n % SIDE, SIDE) * 2 + lax.rem(core + n // SIDE, 2)
        target = raw.at[lax.rem(k, 2), rows_at(lax.div(k, 2), NB), :]
        copies.append(pltpu.make_async_copy(tiles[n], target, sems.at[n]))
    return copies


def first_kernel(starts, *refs):
    pieces, inv, row_high, row_low, raw, sems = refs[:SIDE], *refs[SIDE:]
    copies = plane_copies(pieces, starts, raw, sems, 0)
    for copy in copies:
        copy.start()
    weights = deep(inv[0].T)
    for copy in copies:
        copy.wait()

    def row(p, carry):
        solved = dot3(raw[rows_at(p, 2 * NB), :], weights).reshape(2, NB, NB)
        high, low = split(solved)
        row_high[pl.ds(2 * p, 2)] = high
        row_low[pl.ds(2 * p, 2)] = low
        return carry

    lax.fori_loop(0, TR // 2, row, 0)


def solve_first(pieces, inv):
    return pl.pallas_call(
        functools.partial(first_kernel, tuple(start for _, start in pieces)),
        out_shape=[jax.ShapeDtypeStruct((TR, NB, NB), BF16)] * 2,
        in_specs=[ANY] * SIDE + [VMEM],
        out_specs=[VMEM] * 2,
        scratch_shapes=[pltpu.VMEM((ROWS, NB), F32), pltpu.SemaphoreType.DMA((SIDE,))],
        compiler_params=LIMIT,
        cost_estimate=pl.CostEstimate(flops=8 * 3 * 2 * NB**3, bytes_accessed=4 * 2**20, transcendentals=0),
        name="solve_first",
    )(*[array for array, _ in pieces], inv)


def second_kernel(starts, *refs):
    pieces, cols = refs[:SIDE], refs[SIDE : SIDE + N_ROW]
    inv, pivot, band, row_high1, row_low1, *refs = refs[SIDE + N_ROW :]
    panel, row_high, row_low, high1, low1, high2, low2, raw, raw_cols, sems, col_sems = refs
    r, c = lax.axis_index("row"), lax.axis_index("col")
    copies = plane_copies(pieces, starts, raw, sems, 1)
    col_copies = column_copies(cols, raw_cols, col_sems)
    for copy in copies + col_copies:
        copy.start()
    weights0 = deep(inv[0].T)
    weights1 = deep(inv[1].T)
    one_high, one_low = split(dot3(pivot[...], weights0).T)
    rest_weights = join(one_low, one_high)

    def used(high, low, code):
        full = dot(high, one_high)
        rest = dot(jnp.concatenate([high, low], axis=1), rest_weights)
        return jnp.where(code == 2, 0.0, full + jnp.where(code == 0, rest, 0.0))

    def row(p, carry):
        tile = raw[rows_at(p, NB), :] - used(row_high1[p], row_low1[p], band[p * N_ROW + r, 1])
        solved = dot3(tile, weights1)
        panel[p] = solved
        row_high[p], row_low[p] = split(solved)
        return carry

    def column(q, carry):
        first = dot3(raw_cols[0, rows_at(q, NB), :], weights0)
        high1[q], low1[q] = split(first.T)
        high, low = split(first)
        tile = raw_cols[1, rows_at(q, NB), :] - used(high, low, band[q * N_COL + c, 1])
        high2[q], low2[q] = split(dot3(tile, weights1).T)
        return carry

    for copy in copies:
        copy.wait()
    lax.fori_loop(0, TR, row, 0, unroll=2)
    for copy in col_copies:
        copy.wait()
    lax.fori_loop(0, TC, column, 0, unroll=2)


def solve_second(pieces, cols, inv, pivot, band, first):
    shapes = [jax.ShapeDtypeStruct((TR, NB, NB), F32)]
    shapes += [jax.ShapeDtypeStruct((n, NB, NB), BF16) for n in (TR, TR, TC, TC, TC, TC)]
    return pl.pallas_call(
        functools.partial(second_kernel, tuple(start for _, start in pieces)),
        out_shape=shapes,
        in_specs=[ANY] * (SIDE + N_ROW) + [VMEM] * 2 + [SMEM] + [VMEM] * 2,
        out_specs=[VMEM] * 7,
        scratch_shapes=[
            pltpu.VMEM((ROWS, NB), F32),
            pltpu.VMEM((2, COLS, NB), F32),
            pltpu.SemaphoreType.DMA((SIDE,)),
            pltpu.SemaphoreType.DMA((N_ROW,)),
        ],
        compiler_params=LIMIT,
        cost_estimate=pl.CostEstimate(flops=28 * 3 * 2 * NB**3, bytes_accessed=12 * 2**20, transcendentals=0),
        name="solve_second",
    )(*[array for array, _ in pieces], *cols, inv, pivot, band, *first)


STEP = 2


def update_kernel(band, matrix, high1, low1, high2, low2, chigh1, clow1, chigh2, clow2, out, product):
    step = pl.program_id(0)
    r, c = lax.axis_index("row"), lax.axis_index("col")
    size = STEP * NB
    high = jnp.concatenate([high1[...].reshape(size, NB), high2[...].reshape(size, NB)], axis=1)
    low = jnp.concatenate([low1[...].reshape(size, NB), low2[...].reshape(size, NB)], axis=1)
    both = jnp.concatenate([high, low], axis=1)
    for q in range(TC):
        col_high = jnp.concatenate([chigh1[q], chigh2[q]], axis=0)
        col_low = jnp.concatenate([clow1[q], clow2[q]], axis=0)
        full = dot(high, col_high)
        rest = dot(both, jnp.concatenate([col_low, col_high], axis=0))
        for p in range(STEP):
            code = band[(step * STEP + p) * N_ROW + r, q * N_COL + c]
            at = slice(p * NB, (p + 1) * NB)
            total = jnp.where(code == 2, 0.0, full[at] + jnp.where(code == 0, rest[at], 0.0))
            for b in range(2):
                product[b * TC + q, at, :] = total[:, b * HALF : (b + 1) * HALF]
    lines = 2 * TC
    part = 32
    for p in range(STEP):
        for a in range(0, NB, part):
            turned = product[:, p * NB + a : p * NB + a + part, :].transpose(1, 0, 2).reshape(part * lines, HALF)
            at = pl.ds(a * lines, part * lines)
            out[p, at, :] = matrix[p, at, :] - turned


def update(matrix, band, rows, cols):
    lines = NB * TC * 2
    view = matrix.reshape(TR, NB, TC, 2, HALF).transpose(0, 1, 3, 2, 4).reshape(TR, lines, HALF)
    block = pl.BlockSpec((STEP, lines, HALF), lambda p: (p, 0, 0))
    row = pl.BlockSpec((STEP, NB, NB), lambda p: (p, 0, 0))
    whole = pl.BlockSpec((TC, NB, NB), lambda p: (0, 0, 0))
    out = pl.pallas_call(
        update_kernel,
        grid=(TR // STEP,),
        out_shape=jax.ShapeDtypeStruct((TR, lines, HALF), F32),
        in_specs=[SMEM, block] + [row] * 4 + [whole] * 4,
        out_specs=block,
        scratch_shapes=[pltpu.VMEM((2 * TC, STEP * NB, HALF), F32)],
        compiler_params=LIMIT,
        name="update_tiles",
    )(band, view, *rows, *cols)
    return out.reshape(TR, NB, 2, TC, HALF).transpose(0, 1, 3, 2, 4).reshape(TR, NB, TC, NB)


def body(matrix, diag_inverses, band):
    raw = matrix[:, :, 0, :].reshape(ROWS, NB)
    panel1, panel2, cols, pivot = gather_all(raw, lax.axis_index("row"), lax.axis_index("col"))
    first = solve_first(panel1, diag_inverses)
    panel, row_high2, row_low2, high1, low1, high2, low2 = solve_second(
        panel2, cols, diag_inverses, pivot, band, first
    )
    rows = (*first, row_high2, row_low2)
    return update(matrix, band, rows, (high1, low1, high2, low2)), panel


def solution(mesh):
    in_specs = (P(None, "row", None, "col"), P(), P())
    out_specs = (P(None, "row", None, "col"), P(None, "row", None))
    return jax.shard_map(body, mesh=mesh, in_specs=in_specs, out_specs=out_specs, check_vma=False)
```

```python
import functools

import jax
import jax.numpy as jnp
from jax import lax
from jax.experimental import pallas as pl
from jax.experimental.pallas import tpu as pltpu
from jax.sharding import PartitionSpec as P

NB = 256
HALF = 128
TR = 8
TC = 4
N_ROW = 8
N_COL = 16
SIDE = 4
F32 = jnp.float32
BF16 = jnp.bfloat16


def split(value):
    high = value.astype(BF16)
    return high, (value - high.astype(F32)).astype(BF16)


def dot(a, b):
    return jnp.dot(a, b, preferred_element_type=F32)


def dot3(a, weights):
    high, low = split(a)
    return dot(jnp.concatenate([high, high, low], axis=1), weights)


def deep(value):
    high, low = split(value)
    return jnp.concatenate([high, low, high], axis=0)


def shift_plane(value, by, swapped):
    pairs = []
    for r in range(N_ROW):
        for x in range(SIDE):
            for z in range(SIDE):
                along_z = (r % 2 == 1) != swapped
                to = (x, (z + by) % SIDE) if along_z else ((x + by) % SIDE, z)
                pairs.append((r * N_COL + x * SIDE + z, r * N_COL + to[0] * SIDE + to[1]))
    return lax.ppermute(value, ("row", "col"), pairs)


def shift_line(value, by):
    return shift_plane(value, by, False)


def shift_cross(value, by):
    return shift_plane(value, by, True)


def send_far(value):
    pairs = []
    for r in range(N_ROW):
        for root in range(2):
            to = root + 2 if r % 2 else 2 * SIDE + root
            pairs.append((r * N_COL + root, r * N_COL + to))
    return lax.ppermute(value, ("row", "col"), pairs)


def shift_y(value, by):
    pairs = [(y * 2 + k, (y + by) % SIDE * 2 + k) for y in range(SIDE) for k in range(2)]
    return lax.ppermute(value, "row", pairs)


def swap_core(value):
    return lax.ppermute(value, "row", [(r, r ^ 1) for r in range(N_ROW)])


def to_columns(value):
    pairs = []
    for r in range(N_ROW):
        for x in range(SIDE):
            for z in range(SIDE):
                line, cross = (z, x) if r % 2 else (x, z)
                panel, odd = cross // 2, cross % 2
                quarter = (line - panel * (r % 2)) % SIDE
                target = (quarter * 2 + panel) * N_COL + r + N_ROW * odd
                pairs.append((r * N_COL + x * SIDE + z, target))
    return lax.ppermute(value, ("row", "col"), pairs)


def relay_y(near, back, core):
    pairs = [(r, (r + (2 if r % 2 == 0 else -2)) % N_ROW) for r in range(N_ROW)]
    return lax.ppermute(jnp.where(core == 0, near, back), "row", pairs)


def choose(place, own, near, far, back):
    return jnp.where(place == 0, own, jnp.where(place == 1, near, jnp.where(place == 2, far, back)))


def join(one, two):
    return jnp.concatenate([one, two], axis=0)


PAIR = 2 * NB


def gather_all(raw, row, col):
    barrier = lax.optimization_barrier
    x, z, core = col // SIDE, col % SIDE, row % 2
    line, cross = jnp.where(core == 0, x, z), jnp.where(core == 0, z, x)

    near, back, far = barrier((
        shift_line(raw[PAIR : 2 * PAIR], 1),
        shift_line(raw[3 * PAIR :], -1),
        send_far(raw[2 * PAIR : 3 * PAIR]),
    ))
    places = raw[:PAIR], near, far, back
    own1 = choose(line, *places)
    own2 = choose((line + SIDE - 1) % SIDE, *places)

    near1, back2 = shift_cross(own1, 1), shift_cross(own2, -1)
    back1, near2 = shift_cross(own1, -1), shift_cross(own2, 1)
    far1, far2 = shift_cross(near1, 1), shift_cross(back2, -1)
    near1, far1, back1, near2, far2, back2 = barrier((near1, far1, back1, near2, far2, back2))
    after = (cross + SIDE - 1) % SIDE
    block1 = choose(cross, own1, near1, far1, back1)
    block2 = jnp.where(
        core == 0,
        choose(after, own1, near1, far1, back1),
        choose(cross, own2, near2, far2, back2),
    )
    half = jnp.where(cross < 2, block1, block2)
    tile = lax.dynamic_slice(half, (cross % 2 * NB, 0), (NB, NB))
    block1, block2, tile, pivot = barrier((block1, block2, tile, block1[:NB]))

    corner = [(N_COL + SIDE * a, N_COL + SIDE * a + 2) for a in range(SIDE)]
    near1, back2 = shift_line(block1, 1), shift_line(block2, -1)
    back1, near2 = shift_line(block1, -1), shift_line(block2, 1)
    own, pivot_far = to_columns(tile), lax.ppermute(pivot, ("row", "col"), corner)
    pivot = choose(z, pivot, near1[:NB], pivot_far, back1[:NB])
    far1, far2, up, down, own_other, pivot_up, pivot_down, pivot_swap = barrier((
        shift_line(near1, 1),
        shift_line(back2, -1),
        shift_y(own, 1),
        shift_y(own, -1),
        swap_core(own),
        lax.ppermute(pivot, "row", [(1, 3)]),
        lax.ppermute(pivot, "row", [(1, 7)]),
        lax.ppermute(pivot, "row", [(1, 0)]),
    ))
    panel1 = [block1, near1, far1, back1]
    panel2 = [block2, near2, far2, back2]
    ends = pivot_up + pivot_down
    last, up_other, down_other, pivot_far, ends_swap = barrier((
        relay_y(up, down, core),
        swap_core(up),
        swap_core(down),
        lax.ppermute(ends, "row", [(3, 5)]),
        lax.ppermute(ends, "row", [(3, 2), (7, 6)]),
    ))
    cols = [own, up, last, down, own_other, up_other, swap_core(last), down_other]
    far_swap = lax.ppermute(pivot_far, "row", [(5, 4)])
    pivots = [pivot_swap, pivot, ends_swap, ends, far_swap, pivot_far]
    return panel1, panel2, cols, pivots


VMEM = pl.BlockSpec(memory_space=pltpu.VMEM)
SMEM = pl.BlockSpec(memory_space=pltpu.SMEM)
ANY = pl.BlockSpec(memory_space=pl.ANY)
ROWS = TR * NB
COLS = TC * NB


def rows_at(index, size):
    return pl.ds(pl.multiple_of(index * size, size), size)


def plane_copies(refs, raw, sems, panel):
    c, core = lax.axis_index("col"), lax.rem(lax.axis_index("row"), 2)
    x, z = lax.div(c, SIDE), lax.rem(c, SIDE)
    line = jnp.where(core == 0, x, z + SIDE - panel)
    copies = []
    for n in range(SIDE):
        place = lax.rem(line + SIDE - n, SIDE)
        copies.append(pltpu.make_async_copy(refs[n], raw.at[rows_at(place, PAIR), :], sems.at[n]))
    return copies


def column_copies(tiles, raw, sems):
    r = lax.axis_index("row")
    y, core = lax.div(r, 2), lax.rem(r, 2)
    copies = []
    for n in range(N_ROW):
        k = lax.rem(y + SIDE - n % SIDE, SIDE) * 2 + lax.rem(core + n // SIDE, 2)
        target = raw.at[lax.rem(k, 2), rows_at(lax.div(k, 2), NB), :]
        copies.append(pltpu.make_async_copy(tiles[n], target, sems.at[n]))
    return copies


def first_kernel(*refs):
    pieces, inv_in, row_high, row_low, raw, inv, sems = refs[:SIDE], *refs[SIDE:]
    copies = plane_copies(pieces, raw, sems, 0)
    weights_copy = pltpu.make_async_copy(inv_in.at[0], inv, sems.at[SIDE])
    for copy in [weights_copy, *copies]:
        copy.start()
    weights_copy.wait()
    weights = deep(inv[...].T)
    for copy in copies:
        copy.wait()

    def row(p, carry):
        solved = dot3(raw[rows_at(p, PAIR), :], weights).reshape(2, NB, NB)
        high, low = split(solved)
        row_high[pl.ds(2 * p, 2)] = high
        row_low[pl.ds(2 * p, 2)] = low
        return carry

    lax.fori_loop(0, TR // 2, row, 0)


def solve_first(pieces, inv):
    return pl.pallas_call(
        first_kernel,
        out_shape=[jax.ShapeDtypeStruct((TR, NB, NB), BF16)] * 2,
        in_specs=[ANY] * (SIDE + 1),
        out_specs=[VMEM] * 2,
        scratch_shapes=[
            pltpu.VMEM((ROWS, NB), F32),
            pltpu.VMEM((NB, NB), F32),
            pltpu.SemaphoreType.DMA((SIDE + 1,)),
        ],
        compiler_params=pltpu.CompilerParams(vmem_limit_bytes=16 * 1024 * 1024),
        cost_estimate=pl.CostEstimate(flops=8 * 3 * 2 * NB**3, bytes_accessed=4 * 2**20, transcendentals=0),
        name="solve_first",
    )(*pieces, inv)


STEP = 2
LINES = NB * TC * 2
PART = 32


def last_kernel(*refs):
    pieces, cols = refs[:SIDE], refs[SIDE : SIDE + N_ROW]
    pivots, refs = refs[SIDE + N_ROW : SIDE + N_ROW + 6], refs[SIDE + N_ROW + 6 :]
    matrix, inv_in, high_in, low_in, band, out, panel, *refs = refs
    tiles, raw, raw_cols, row_high1, row_low1, row_high2, row_low2, col_high, col_low, even, odd, *refs = refs
    inv, pivot, sems, col_sems, in_sems, out_sems, panel_sems, small_sems = refs
    r, c = lax.axis_index("row"), lax.axis_index("col")
    copies = plane_copies(pieces, raw, sems, 1)
    col_copies = column_copies(cols, raw_cols, col_sems)
    loads = [pltpu.make_async_copy(matrix.at[p], tiles.at[p], in_sems.at[p]) for p in range(TR)]
    small = [(inv_in, inv), (pivots[0], pivot), (high_in, row_high1), (low_in, row_low1)]
    small = [pltpu.make_async_copy(a, b, small_sems.at[n]) for n, (a, b) in enumerate(small)]
    small[0].start()
    for n, rows in enumerate(((0,), (1,), (2, 6), (3, 7), (4,), (5,))):

        @pl.when(functools.reduce(jnp.logical_or, [r == row for row in rows]))
        def _():
            pltpu.make_async_copy(pivots[n], pivot, small_sems.at[1]).start()

    for copy in small[2:] + copies + col_copies + loads:
        copy.start()
    small[0].wait()
    weights0 = deep(inv[0].T)
    weights1 = deep(inv[1].T)
    small[1].wait()
    one_high, one_low = split(dot3(pivot[...], weights0).T)
    rest_weights = join(one_low, one_high)

    def used(high, low, code):
        full = dot(high, one_high)
        rest = dot(jnp.concatenate([high, low], axis=1), rest_weights)
        return jnp.where(code == 2, 0.0, full + jnp.where(code == 0, rest, 0.0))

    def row(p, carry):
        tile = raw[rows_at(p, NB), :] - used(row_high1[p], row_low1[p], band[p * N_ROW + r, 1])
        solved = dot3(tile, weights1)
        raw[rows_at(p, NB), :] = solved
        row_high2[p], row_low2[p] = split(solved)
        return carry

    def column(q, carry):
        first = dot3(raw_cols[0, rows_at(q, NB), :], weights0)
        col_high[q, :NB, :], col_low[q, :NB, :] = split(first.T)
        high, low = split(first)
        tile = raw_cols[1, rows_at(q, NB), :] - used(high, low, band[q * N_COL + c, 1])
        col_high[q, NB:, :], col_low[q, NB:, :] = split(dot3(tile, weights1).T)
        return carry

    for copy in small[2:] + copies:
        copy.wait()
    lax.fori_loop(0, TR, row, 0, unroll=4)
    panels = [pltpu.make_async_copy(raw.at[pl.ds(p * NB, NB), :], panel.at[p], panel_sems.at[p]) for p in range(TR)]
    for copy in panels:
        copy.start()
    for copy in col_copies:
        copy.wait()
    lax.fori_loop(0, TC, column, 0, unroll=4)

    size = STEP * NB

    def multiply(step, q, product):
        at = pl.ds(step * STEP, STEP)
        high = jnp.concatenate([row_high1[at].reshape(size, NB), row_high2[at].reshape(size, NB)], axis=1)
        low = jnp.concatenate([row_low1[at].reshape(size, NB), row_low2[at].reshape(size, NB)], axis=1)
        full = dot(high, col_high[q])
        rest = dot(jnp.concatenate([high, low], axis=1), join(col_low[q], col_high[q]))
        for p in range(STEP):
            code = band[(step * STEP + p) * N_ROW + r, q * N_COL + c]
            at = slice(p * NB, (p + 1) * NB)
            total = jnp.where(code == 2, 0.0, full[at] + jnp.where(code == 0, rest[at], 0.0))
            for b in range(2):
                product[b * TC + q, at, :] = total[:, b * HALF : (b + 1) * HALF]

    def subtract(step, share, product):
        for a in range(share * size // TC, (share + 1) * size // TC, PART):
            turned = product[:, a : a + PART, :].transpose(1, 0, 2).reshape(PART * 2 * TC, HALF)
            at = pl.ds(a % NB * 2 * TC, PART * 2 * TC)
            tiles[step * STEP + a // NB, at, :] -= turned

    steps = TR // STEP
    stores = [pltpu.make_async_copy(tiles.at[p], out.at[p], out_sems.at[p]) for p in range(TR)]
    for step in range(steps + 1):
        product, before = (even, odd) if step % 2 == 0 else (odd, even)
        if step:
            for p in range(STEP):
                loads[(step - 1) * STEP + p].wait()
        for q in range(TC):
            if step < steps:
                multiply(step, q, product)
            if step:
                subtract(step - 1, q, before)
        if step:
            for p in range(STEP):
                stores[(step - 1) * STEP + p].start()
    for copy in stores + panels:
        copy.wait()


def finish(pieces, cols, pivots, matrix, inv, first, band):
    view = matrix.reshape(TR, NB, TC, 2, HALF).transpose(0, 1, 3, 2, 4).reshape(TR, LINES, HALF)
    out, panel = pl.pallas_call(
        last_kernel,
        out_shape=(
            jax.ShapeDtypeStruct((TR, LINES, HALF), F32),
            jax.ShapeDtypeStruct((TR, NB, NB), F32),
        ),
        in_specs=[ANY] * (SIDE + N_ROW + 6 + 4) + [SMEM],
        out_specs=[ANY] * 2,
        scratch_shapes=[
            pltpu.VMEM((TR, LINES, HALF), F32),
            pltpu.VMEM((ROWS, NB), F32),
            pltpu.VMEM((2, COLS, NB), F32),
            pltpu.VMEM((TR, NB, NB), BF16),
            pltpu.VMEM((TR, NB, NB), BF16),
            pltpu.VMEM((TR, NB, NB), BF16),
            pltpu.VMEM((TR, NB, NB), BF16),
            pltpu.VMEM((TC, PAIR, NB), BF16),
            pltpu.VMEM((TC, PAIR, NB), BF16),
            pltpu.VMEM((2 * TC, STEP * NB, HALF), F32),
            pltpu.VMEM((2 * TC, STEP * NB, HALF), F32),
            pltpu.VMEM((2, NB, NB), F32),
            pltpu.VMEM((NB, NB), F32),
            pltpu.SemaphoreType.DMA((SIDE,)),
            pltpu.SemaphoreType.DMA((N_ROW,)),
            pltpu.SemaphoreType.DMA((TR,)),
            pltpu.SemaphoreType.DMA((TR,)),
            pltpu.SemaphoreType.DMA((TR,)),
            pltpu.SemaphoreType.DMA((4,)),
        ],
        compiler_params=pltpu.CompilerParams(vmem_limit_bytes=40 * 1024 * 1024),
        cost_estimate=pl.CostEstimate(flops=200 * 2 * NB**3, bytes_accessed=20 * 2**20, transcendentals=0),
        name="solve_and_update",
    )(*pieces, *cols, *pivots, view, inv, *first, band)
    return out.reshape(TR, NB, 2, TC, HALF).transpose(0, 1, 3, 2, 4).reshape(TR, NB, TC, NB), panel


def body(matrix, diag_inverses, band):
    raw = lax.optimization_barrier(matrix[:, :, 0, :].reshape(ROWS, NB))
    panel1, panel2, cols, pivots = gather_all(raw, lax.axis_index("row"), lax.axis_index("col"))
    first = solve_first(panel1, diag_inverses)
    return finish(panel2, cols, pivots, matrix, diag_inverses, first, band)


def solution(mesh):
    in_specs = (P(None, "row", None, "col"), P(), P())
    out_specs = (P(None, "row", None, "col"), P(None, "row", None))
    return jax.shard_map(body, mesh=mesh, in_specs=in_specs, out_specs=out_specs, check_vma=False)
```

```python
import functools

import jax
import jax.numpy as jnp
from jax import lax
from jax.experimental import pallas as pl
from jax.experimental.pallas import tpu as pltpu
from jax.sharding import PartitionSpec as P

NB = 256
HALF = 128
TR = 8
TC = 4
N_ROW = 8
N_COL = 16
SIDE = 4
F32 = jnp.float32
BF16 = jnp.bfloat16


def split(value):
    high = value.astype(BF16)
    return high, (value - high.astype(F32)).astype(BF16)


def dot(a, b):
    return jnp.dot(a, b, preferred_element_type=F32)


def dot3(a, weights):
    high, low = split(a)
    return dot(jnp.concatenate([high, high, low], axis=1), weights)


def deep(value):
    high, low = split(value)
    return jnp.concatenate([high, low, high], axis=0)


def shift_plane(value, by, swapped):
    pairs = []
    for r in range(N_ROW):
        for x in range(SIDE):
            for z in range(SIDE):
                along_z = (r % 2 == 1) != swapped
                to = (x, (z + by) % SIDE) if along_z else ((x + by) % SIDE, z)
                pairs.append((r * N_COL + x * SIDE + z, r * N_COL + to[0] * SIDE + to[1]))
    return lax.ppermute(value, ("row", "col"), pairs)


def shift_line(value, by):
    return shift_plane(value, by, False)


def shift_cross(value, by):
    return shift_plane(value, by, True)


def send_far(value):
    pairs = []
    for r in range(N_ROW):
        for root in range(2):
            to = root + 2 if r % 2 else 2 * SIDE + root
            pairs.append((r * N_COL + root, r * N_COL + to))
    return lax.ppermute(value, ("row", "col"), pairs)


def shift_y(value, by):
    pairs = [(y * 2 + k, (y + by) % SIDE * 2 + k) for y in range(SIDE) for k in range(2)]
    return lax.ppermute(value, "row", pairs)


def swap_core(value):
    return lax.ppermute(value, "row", [(r, r ^ 1) for r in range(N_ROW)])


def to_columns(value):
    pairs = []
    for r in range(N_ROW):
        for x in range(SIDE):
            for z in range(SIDE):
                line, cross = (z, x) if r % 2 else (x, z)
                panel, odd = cross // 2, cross % 2
                quarter = (line - panel * (r % 2)) % SIDE
                target = (quarter * 2 + panel) * N_COL + r + N_ROW * odd
                pairs.append((r * N_COL + x * SIDE + z, target))
    return lax.ppermute(value, ("row", "col"), pairs)


def relay_y(near, back, core):
    pairs = [(r, (r + (2 if r % 2 == 0 else -2)) % N_ROW) for r in range(N_ROW)]
    return lax.ppermute(jnp.where(core == 0, near, back), "row", pairs)


def choose(place, own, near, far, back):
    return jnp.where(place == 0, own, jnp.where(place == 1, near, jnp.where(place == 2, far, back)))


def join(one, two):
    return jnp.concatenate([one, two], axis=0)


PAIR = 2 * NB


def gather_all(raw, row, col):
    barrier = lax.optimization_barrier
    x, z, core = col // SIDE, col % SIDE, row % 2
    line, cross = jnp.where(core == 0, x, z), jnp.where(core == 0, z, x)

    near, back, far = barrier((
        shift_line(raw[PAIR : 2 * PAIR], 1),
        shift_line(raw[3 * PAIR :], -1),
        send_far(raw[2 * PAIR : 3 * PAIR]),
    ))
    places = raw[:PAIR], near, far, back
    own1 = choose(line, *places)
    own2 = choose((line + SIDE - 1) % SIDE, *places)

    near1, back2 = shift_cross(own1, 1), shift_cross(own2, -1)
    back1, near2 = shift_cross(own1, -1), shift_cross(own2, 1)
    far1, far2 = shift_cross(near1, 1), shift_cross(back2, -1)
    near1, far1, back1, near2, far2, back2 = barrier((near1, far1, back1, near2, far2, back2))
    after = (cross + SIDE - 1) % SIDE
    block1 = choose(cross, own1, near1, far1, back1)
    block2 = jnp.where(
        core == 0,
        choose(after, own1, near1, far1, back1),
        choose(cross, own2, near2, far2, back2),
    )
    half = jnp.where(cross < 2, block1, block2)
    tile = lax.dynamic_slice(half, (cross % 2 * NB, 0), (NB, NB))
    block1, block2, tile, pivot = barrier((block1, block2, tile, block1[:NB]))

    corner = [(N_COL + SIDE * a, N_COL + SIDE * a + 2) for a in range(SIDE)]
    own, pivot_near, pivot_back, pivot_far = barrier((
        to_columns(tile),
        shift_line(pivot, 1),
        shift_line(pivot, -1),
        lax.ppermute(pivot, ("row", "col"), corner),
    ))
    pivot = choose(z, pivot, pivot_near, pivot_far, pivot_back)
    block1, block2, own, pivot = barrier((block1, block2, own, pivot))

    near1, back2 = shift_line(block1, 1), shift_line(block2, -1)
    back1, near2 = shift_line(block1, -1), shift_line(block2, 1)
    own_other = swap_core(own)
    near1, back2, own, pivot = barrier((near1, back2, own, pivot))
    far1, far2, back1, near2, own_other, up, down, pivot_up, pivot_down, pivot_swap = barrier((
        shift_line(near1, 1),
        shift_line(back2, -1),
        back1,
        near2,
        own_other,
        shift_y(own, 1),
        shift_y(own, -1),
        lax.ppermute(pivot, "row", [(1, 3)]),
        lax.ppermute(pivot, "row", [(1, 7)]),
        lax.ppermute(pivot, "row", [(1, 0)]),
    ))
    panel1 = [block1, near1, far1, back1]
    panel2 = [block2, near2, far2, back2]
    ends = pivot_up + pivot_down
    last, up_other, down_other, pivot_far, ends_swap = barrier((
        relay_y(up, down, core),
        swap_core(up),
        swap_core(down),
        lax.ppermute(ends, "row", [(3, 5)]),
        lax.ppermute(ends, "row", [(3, 2), (7, 6)]),
    ))
    cols = [own, up, last, down, own_other, up_other, swap_core(last), down_other]
    far_swap = lax.ppermute(pivot_far, "row", [(5, 4)])
    pivots = [pivot_swap, pivot, ends_swap, ends, far_swap, pivot_far]
    return panel1, panel2, cols, pivots


VMEM = pl.BlockSpec(memory_space=pltpu.VMEM)
SMEM = pl.BlockSpec(memory_space=pltpu.SMEM)
ANY = pl.BlockSpec(memory_space=pl.ANY)
ROWS = TR * NB
COLS = TC * NB


def rows_at(index, size):
    return pl.ds(pl.multiple_of(index * size, size), size)


def plane_copies(refs, raw, sems, panel):
    c, core = lax.axis_index("col"), lax.rem(lax.axis_index("row"), 2)
    x, z = lax.div(c, SIDE), lax.rem(c, SIDE)
    line = jnp.where(core == 0, x, z + SIDE - panel)
    copies = []
    for n in range(SIDE):
        place = lax.rem(line + SIDE - n, SIDE)
        copies.append(pltpu.make_async_copy(refs[n], raw.at[rows_at(place, PAIR), :], sems.at[n]))
    return copies


def column_copies(tiles, raw, sems):
    r = lax.axis_index("row")
    y, core = lax.div(r, 2), lax.rem(r, 2)
    copies = []
    for n in range(N_ROW):
        k = lax.rem(y + SIDE - n % SIDE, SIDE) * 2 + lax.rem(core + n // SIDE, 2)
        target = raw.at[lax.rem(k, 2), rows_at(lax.div(k, 2), NB), :]
        copies.append(pltpu.make_async_copy(tiles[n], target, sems.at[n]))
    return copies


def first_kernel(*refs):
    pieces, inv_in, row_high, row_low, raw, inv, sems = refs[:SIDE], *refs[SIDE:]
    copies = plane_copies(pieces, raw, sems, 0)
    weights_copy = pltpu.make_async_copy(inv_in.at[0], inv, sems.at[SIDE])
    for copy in [weights_copy, *copies]:
        copy.start()
    weights_copy.wait()
    weights = deep(inv[...].T)
    for copy in copies:
        copy.wait()

    def row(p, carry):
        solved = dot3(raw[rows_at(p, PAIR), :], weights).reshape(2, NB, NB)
        high, low = split(solved)
        row_high[pl.ds(2 * p, 2)] = high
        row_low[pl.ds(2 * p, 2)] = low
        return carry

    lax.fori_loop(0, TR // 2, row, 0)


def solve_first(pieces, inv):
    return pl.pallas_call(
        first_kernel,
        out_shape=[jax.ShapeDtypeStruct((TR, NB, NB), BF16)] * 2,
        in_specs=[ANY] * (SIDE + 1),
        out_specs=[VMEM] * 2,
        scratch_shapes=[
            pltpu.VMEM((ROWS, NB), F32),
            pltpu.VMEM((NB, NB), F32),
            pltpu.SemaphoreType.DMA((SIDE + 1,)),
        ],
        compiler_params=pltpu.CompilerParams(vmem_limit_bytes=16 * 1024 * 1024),
        cost_estimate=pl.CostEstimate(flops=8 * 3 * 2 * NB**3, bytes_accessed=4 * 2**20, transcendentals=0),
        name="solve_first",
    )(*pieces, inv)


STEP = 2
LINES = NB * TC * 2
PART = 32


def last_kernel(*refs):
    pieces, cols = refs[:SIDE], refs[SIDE : SIDE + N_ROW]
    pivots, refs = refs[SIDE + N_ROW : SIDE + N_ROW + 6], refs[SIDE + N_ROW + 6 :]
    matrix, inv_in, high_in, low_in, band, out, panel, *refs = refs
    tiles, raw, raw_cols, row_high1, row_low1, row_high2, row_low2, col_high, col_low, even, odd, *refs = refs
    inv, pivot, sems, col_sems, in_sems, out_sems, panel_sems, small_sems = refs
    r, c = lax.axis_index("row"), lax.axis_index("col")
    copies = plane_copies(pieces, raw, sems, 1)
    col_copies = column_copies(cols, raw_cols, col_sems)
    loads = [pltpu.make_async_copy(matrix.at[p], tiles.at[p], in_sems.at[p]) for p in range(TR)]
    small = [(inv_in, inv), (pivots[0], pivot), (high_in, row_high1), (low_in, row_low1)]
    small = [pltpu.make_async_copy(a, b, small_sems.at[n]) for n, (a, b) in enumerate(small)]
    small[0].start()
    for n, rows in enumerate(((0,), (1,), (2, 6), (3, 7), (4,), (5,))):

        @pl.when(functools.reduce(jnp.logical_or, [r == row for row in rows]))
        def _():
            pltpu.make_async_copy(pivots[n], pivot, small_sems.at[1]).start()

    for copy in small[2:] + copies + col_copies + loads:
        copy.start()
    small[0].wait()
    weights0 = deep(inv[0].T)
    weights1 = deep(inv[1].T)
    small[1].wait()
    one_high, one_low = split(dot3(pivot[...], weights0).T)
    rest_weights = join(one_low, one_high)

    def used(high, low, code):
        full = dot(high, one_high)
        rest = dot(jnp.concatenate([high, low], axis=1), rest_weights)
        return jnp.where(code == 2, 0.0, full + jnp.where(code == 0, rest, 0.0))

    def column(q, carry):
        first = dot3(raw_cols[0, rows_at(q, NB), :], weights0)
        col_high[q, :NB, :], col_low[q, :NB, :] = split(first.T)
        high, low = split(first)
        tile = raw_cols[1, rows_at(q, NB), :] - used(high, low, band[q * N_COL + c, 1])
        col_high[q, NB:, :], col_low[q, NB:, :] = split(dot3(tile, weights1).T)
        return carry

    panels = [pltpu.make_async_copy(raw.at[pl.ds(p * NB, NB), :], panel.at[p], panel_sems.at[p]) for p in range(TR)]

    def solve(p):
        at = pl.ds(p * NB, NB)
        tile = raw[at, :] - used(row_high1[p], row_low1[p], band[p * N_ROW + r, 1])
        solved = dot3(tile, weights1)
        raw[at, :] = solved
        row_high2[p], row_low2[p] = split(solved)

    for copy in col_copies:
        copy.wait()
    lax.fori_loop(0, TC, column, 0, unroll=2)
    for copy in small[2:] + copies:
        copy.wait()

    size = STEP * NB

    def multiply(step, q, product):
        at = pl.ds(step * STEP, STEP)
        high = jnp.concatenate([row_high1[at].reshape(size, NB), row_high2[at].reshape(size, NB)], axis=1)
        low = jnp.concatenate([row_low1[at].reshape(size, NB), row_low2[at].reshape(size, NB)], axis=1)
        full = dot(high, col_high[q])
        rest = dot(jnp.concatenate([high, low], axis=1), join(col_low[q], col_high[q]))
        for p in range(STEP):
            code = band[(step * STEP + p) * N_ROW + r, q * N_COL + c]
            at = slice(p * NB, (p + 1) * NB)
            total = jnp.where(code == 2, 0.0, full[at] + jnp.where(code == 0, rest[at], 0.0))
            for b in range(2):
                product[b * TC + q, at, :] = total[:, b * HALF : (b + 1) * HALF]

    def subtract(step, share, product):
        for a in range(share * size // TC, (share + 1) * size // TC, PART):
            turned = product[:, a : a + PART, :].transpose(1, 0, 2).reshape(PART * 2 * TC, HALF)
            at = pl.ds(a % NB * 2 * TC, PART * 2 * TC)
            tiles[step * STEP + a // NB, at, :] -= turned

    steps = TR // STEP
    stores = [pltpu.make_async_copy(tiles.at[p], out.at[p], out_sems.at[p]) for p in range(TR)]
    for step in range(-1, steps + 1):
        product, before = (even, odd) if step % 2 == 0 else (odd, even)
        if step > 0:
            for p in range(STEP):
                loads[(step - 1) * STEP + p].wait()
        for q in range(TC):
            if step + 1 < steps and q < STEP:
                solve((step + 1) * STEP + q)
            if 0 <= step < steps:
                multiply(step, q, product)
            if step > 0:
                subtract(step - 1, q, before)
        if step + 1 < steps:
            for p in range(STEP):
                panels[(step + 1) * STEP + p].start()
        if step > 0:
            for p in range(STEP):
                stores[(step - 1) * STEP + p].start()
    for copy in stores + panels:
        copy.wait()


def finish(pieces, cols, pivots, matrix, inv, first, band):
    view = matrix.reshape(TR, NB, TC, 2, HALF).transpose(0, 1, 3, 2, 4).reshape(TR, LINES, HALF)
    out, panel = pl.pallas_call(
        last_kernel,
        out_shape=(
            jax.ShapeDtypeStruct((TR, LINES, HALF), F32),
            jax.ShapeDtypeStruct((TR, NB, NB), F32),
        ),
        in_specs=[ANY] * (SIDE + N_ROW + 6 + 4) + [SMEM],
        out_specs=[ANY] * 2,
        scratch_shapes=[
            pltpu.VMEM((TR, LINES, HALF), F32),
            pltpu.VMEM((ROWS, NB), F32),
            pltpu.VMEM((2, COLS, NB), F32),
            pltpu.VMEM((TR, NB, NB), BF16),
            pltpu.VMEM((TR, NB, NB), BF16),
            pltpu.VMEM((TR, NB, NB), BF16),
            pltpu.VMEM((TR, NB, NB), BF16),
            pltpu.VMEM((TC, PAIR, NB), BF16),
            pltpu.VMEM((TC, PAIR, NB), BF16),
            pltpu.VMEM((2 * TC, STEP * NB, HALF), F32),
            pltpu.VMEM((2 * TC, STEP * NB, HALF), F32),
            pltpu.VMEM((2, NB, NB), F32),
            pltpu.VMEM((NB, NB), F32),
            pltpu.SemaphoreType.DMA((SIDE,)),
            pltpu.SemaphoreType.DMA((N_ROW,)),
            pltpu.SemaphoreType.DMA((TR,)),
            pltpu.SemaphoreType.DMA((TR,)),
            pltpu.SemaphoreType.DMA((TR,)),
            pltpu.SemaphoreType.DMA((4,)),
        ],
        compiler_params=pltpu.CompilerParams(vmem_limit_bytes=40 * 1024 * 1024),
        cost_estimate=pl.CostEstimate(flops=200 * 2 * NB**3, bytes_accessed=20 * 2**20, transcendentals=0),
        name="solve_and_update",
    )(*pieces, *cols, *pivots, view, inv, *first, band)
    return out.reshape(TR, NB, 2, TC, HALF).transpose(0, 1, 3, 2, 4).reshape(TR, NB, TC, NB), panel


def body(matrix, diag_inverses, band):
    raw = lax.optimization_barrier(matrix[:, :, 0, :].reshape(ROWS, NB))
    panel1, panel2, cols, pivots = gather_all(raw, lax.axis_index("row"), lax.axis_index("col"))
    first = solve_first(panel1, diag_inverses)
    return finish(panel2, cols, pivots, matrix, diag_inverses, first, band)


def solution(mesh):
    in_specs = (P(None, "row", None, "col"), P(), P())
    out_specs = (P(None, "row", None, "col"), P(None, "row", None))
    return jax.shard_map(body, mesh=mesh, in_specs=in_specs, out_specs=out_specs, check_vma=False)
```

```python
import functools

import jax
import jax.numpy as jnp
from jax import lax
from jax.experimental import pallas as pl
from jax.experimental.pallas import tpu as pltpu
from jax.sharding import PartitionSpec as P

NB = 256
HALF = 128
TR = 8
TC = 4
N_ROW = 8
N_COL = 16
SIDE = 4
F32 = jnp.float32
BF16 = jnp.bfloat16


def split(value):
    high = value.astype(BF16)
    return high, (value - high.astype(F32)).astype(BF16)


def dot(a, b):
    return jnp.dot(a, b, preferred_element_type=F32)


def dot3(a, weights):
    high, low = split(a)
    return dot(jnp.concatenate([high, high, low], axis=1), weights)


def deep(value):
    high, low = split(value)
    return jnp.concatenate([high, low, high], axis=0)


def shift_plane(value, by, swapped):
    pairs = []
    for r in range(N_ROW):
        for x in range(SIDE):
            for z in range(SIDE):
                along_z = (r % 2 == 1) != swapped
                to = (x, (z + by) % SIDE) if along_z else ((x + by) % SIDE, z)
                pairs.append((r * N_COL + x * SIDE + z, r * N_COL + to[0] * SIDE + to[1]))
    return lax.ppermute(value, ("row", "col"), pairs)


def shift_line(value, by):
    return shift_plane(value, by, False)


def shift_cross(value, by):
    return shift_plane(value, by, True)


def send_far(value):
    pairs = []
    for r in range(N_ROW):
        for root in range(2):
            to = root + 2 if r % 2 else 2 * SIDE + root
            pairs.append((r * N_COL + root, r * N_COL + to))
    return lax.ppermute(value, ("row", "col"), pairs)


def shift_y(value, by):
    pairs = [(y * 2 + k, (y + by) % SIDE * 2 + k) for y in range(SIDE) for k in range(2)]
    return lax.ppermute(value, "row", pairs)


def swap_core(value):
    return lax.ppermute(value, "row", [(r, r ^ 1) for r in range(N_ROW)])


def to_columns(value):
    pairs = []
    for r in range(N_ROW):
        for x in range(SIDE):
            for z in range(SIDE):
                line, cross = (z, x) if r % 2 else (x, z)
                panel, odd = cross // 2, cross % 2
                quarter = (line - panel * (r % 2)) % SIDE
                target = (quarter * 2 + panel) * N_COL + r + N_ROW * odd
                pairs.append((r * N_COL + x * SIDE + z, target))
    return lax.ppermute(value, ("row", "col"), pairs)


def relay_y(near, back, core):
    pairs = [(r, (r + (2 if r % 2 == 0 else -2)) % N_ROW) for r in range(N_ROW)]
    return lax.ppermute(jnp.where(core == 0, near, back), "row", pairs)


def choose(place, own, near, far, back):
    return jnp.where(place == 0, own, jnp.where(place == 1, near, jnp.where(place == 2, far, back)))


def join(one, two):
    return jnp.concatenate([one, two], axis=0)


PAIR = 2 * NB


def gather_all(raw, row, col):
    barrier = lax.optimization_barrier
    x, z, core = col // SIDE, col % SIDE, row % 2
    line, cross = jnp.where(core == 0, x, z), jnp.where(core == 0, z, x)

    near, back, far = barrier((
        shift_line(raw[PAIR : 2 * PAIR], 1),
        shift_line(raw[3 * PAIR :], -1),
        send_far(raw[2 * PAIR : 3 * PAIR]),
    ))
    places = raw[:PAIR], near, far, back
    own1 = choose(line, *places)
    own2 = choose((line + SIDE - 1) % SIDE, *places)

    near1, back2 = shift_cross(own1, 1), shift_cross(own2, -1)
    back1, near2 = shift_cross(own1, -1), shift_cross(own2, 1)
    far1, far2 = shift_cross(near1, 1), shift_cross(back2, -1)
    near1, far1, back1, near2, far2, back2 = barrier((near1, far1, back1, near2, far2, back2))
    after = (cross + SIDE - 1) % SIDE
    block1 = choose(cross, own1, near1, far1, back1)
    block2 = jnp.where(
        core == 0,
        choose(after, own1, near1, far1, back1),
        choose(cross, own2, near2, far2, back2),
    )
    half = jnp.where(cross < 2, block1, block2)
    tile = lax.dynamic_slice(half, (cross % 2 * NB, 0), (NB, NB))
    block1, block2, tile, pivot = barrier((block1, block2, tile, block1[:NB]))

    corner = [(N_COL + SIDE * a, N_COL + SIDE * a + 2) for a in range(SIDE)]
    near1, back2, back1, near2, own, pivot_far = barrier((
        shift_line(block1, 1),
        shift_line(block2, -1),
        shift_line(block1, -1),
        shift_line(block2, 1),
        to_columns(tile),
        lax.ppermute(pivot, ("row", "col"), corner),
    ))
    pivot = choose(z, pivot, near1[:NB], pivot_far, back1[:NB])
    near1, back2, own, pivot = barrier((near1, back2, own, pivot))
    far1, far2, up, down, own_other, pivot_up, pivot_down, pivot_far, pivot_swap = barrier((
        shift_line(near1, 1),
        shift_line(back2, -1),
        shift_y(own, 1),
        shift_y(own, -1),
        swap_core(own),
        lax.ppermute(pivot, "row", [(1, 3)]),
        lax.ppermute(pivot, "row", [(1, 7)]),
        lax.ppermute(pivot, "row", [(1, 5)]),
        lax.ppermute(pivot, "row", [(1, 0)]),
    ))
    panel1 = [block1, near1, far1, back1]
    panel2 = [block2, near2, far2, back2]
    odd = pivot_up + pivot_down + pivot_far
    last, up_other, down_other, even = barrier((
        relay_y(up, down, core),
        swap_core(up),
        swap_core(down),
        lax.ppermute(odd, "row", [(3, 2), (5, 4), (7, 6)]),
    ))
    cols = [own, up, last, down, own_other, up_other, swap_core(last), down_other]
    pivots = [pivot_swap, pivot, even, odd]
    return panel1, panel2, cols, pivots


VMEM = pl.BlockSpec(memory_space=pltpu.VMEM)
SMEM = pl.BlockSpec(memory_space=pltpu.SMEM)
ANY = pl.BlockSpec(memory_space=pl.ANY)
ROWS = TR * NB
COLS = TC * NB


def rows_at(index, size):
    return pl.ds(pl.multiple_of(index * size, size), size)


def plane_copies(refs, raw, sems, panel):
    c, core = lax.axis_index("col"), lax.rem(lax.axis_index("row"), 2)
    x, z = lax.div(c, SIDE), lax.rem(c, SIDE)
    line = jnp.where(core == 0, x, z + SIDE - panel)
    copies = []
    for n in range(SIDE):
        place = lax.rem(line + SIDE - n, SIDE)
        copies.append(pltpu.make_async_copy(refs[n], raw.at[rows_at(place, PAIR), :], sems.at[n]))
    return copies


def column_copies(tiles, raw, sems):
    r = lax.axis_index("row")
    y, core = lax.div(r, 2), lax.rem(r, 2)
    copies = []
    for n in range(N_ROW):
        k = lax.rem(y + SIDE - n % SIDE, SIDE) * 2 + lax.rem(core + n // SIDE, 2)
        target = raw.at[lax.rem(k, 2), rows_at(lax.div(k, 2), NB), :]
        copies.append(pltpu.make_async_copy(tiles[n], target, sems.at[n]))
    return copies


def first_kernel(*refs):
    pieces, inv_in, row_high, row_low, raw, inv, sems = refs[:SIDE], *refs[SIDE:]
    copies = plane_copies(pieces, raw, sems, 0)
    weights_copy = pltpu.make_async_copy(inv_in.at[0], inv, sems.at[SIDE])
    for copy in [weights_copy, *copies]:
        copy.start()
    weights_copy.wait()
    weights = deep(inv[...].T)
    for copy in copies:
        copy.wait()

    def row(p, carry):
        solved = dot3(raw[rows_at(p, PAIR), :], weights).reshape(2, NB, NB)
        high, low = split(solved)
        row_high[pl.ds(2 * p, 2)] = high
        row_low[pl.ds(2 * p, 2)] = low
        return carry

    lax.fori_loop(0, TR // 2, row, 0)


def solve_first(pieces, inv):
    return pl.pallas_call(
        first_kernel,
        out_shape=[jax.ShapeDtypeStruct((TR, NB, NB), BF16)] * 2,
        in_specs=[ANY] * (SIDE + 1),
        out_specs=[VMEM] * 2,
        scratch_shapes=[
            pltpu.VMEM((ROWS, NB), F32),
            pltpu.VMEM((NB, NB), F32),
            pltpu.SemaphoreType.DMA((SIDE + 1,)),
        ],
        compiler_params=pltpu.CompilerParams(vmem_limit_bytes=16 * 1024 * 1024),
        cost_estimate=pl.CostEstimate(flops=8 * 3 * 2 * NB**3, bytes_accessed=4 * 2**20, transcendentals=0),
        name="solve_first",
    )(*pieces, inv)


STEP = 2
LINES = NB * TC * 2
PART = 32


def last_kernel(*refs):
    pieces, cols = refs[:SIDE], refs[SIDE : SIDE + N_ROW]
    pivots, refs = refs[SIDE + N_ROW : SIDE + N_ROW + 4], refs[SIDE + N_ROW + 4 :]
    matrix, inv_in, high_in, low_in, band, out, panel, *refs = refs
    tiles, raw, raw_cols, row_high1, row_low1, row_high2, row_low2, col_high, col_low, even, odd, *refs = refs
    inv, pivot, sems, col_sems, in_sems, out_sems, panel_sems, small_sems = refs
    r, c = lax.axis_index("row"), lax.axis_index("col")
    copies = plane_copies(pieces, raw, sems, 1)
    col_copies = column_copies(cols, raw_cols, col_sems)
    loads = [pltpu.make_async_copy(matrix.at[p], tiles.at[p], in_sems.at[p]) for p in range(TR)]
    small = [(inv_in, inv), (pivots[0], pivot), (high_in, row_high1), (low_in, row_low1)]
    small = [pltpu.make_async_copy(a, b, small_sems.at[n]) for n, (a, b) in enumerate(small)]
    small[0].start()
    for n, rows in enumerate(((0,), (1,), (2, 4, 6), (3, 5, 7))):

        @pl.when(functools.reduce(jnp.logical_or, [r == row for row in rows]))
        def _():
            pltpu.make_async_copy(pivots[n], pivot, small_sems.at[1]).start()

    for copy in small[2:] + copies + col_copies + loads:
        copy.start()
    small[0].wait()
    weights0 = deep(inv[0].T)
    weights1 = deep(inv[1].T)
    small[1].wait()
    one_high, one_low = split(dot3(pivot[...], weights0).T)
    rest_weights = join(one_low, one_high)

    def used(high, low, code):
        full = dot(high, one_high)
        rest = dot(jnp.concatenate([high, low], axis=1), rest_weights)
        return jnp.where(code == 2, 0.0, full + jnp.where(code == 0, rest, 0.0))

    def column(q, carry):
        first = dot3(raw_cols[0, rows_at(q, NB), :], weights0)
        col_high[q, :NB, :], col_low[q, :NB, :] = split(first.T)
        high, low = split(first)
        tile = raw_cols[1, rows_at(q, NB), :] - used(high, low, band[q * N_COL + c, 1])
        col_high[q, NB:, :], col_low[q, NB:, :] = split(dot3(tile, weights1).T)
        return carry

    panels = [pltpu.make_async_copy(raw.at[pl.ds(p * NB, NB), :], panel.at[p], panel_sems.at[p]) for p in range(TR)]

    def solve(p):
        at = pl.ds(p * NB, NB)
        tile = raw[at, :] - used(row_high1[p], row_low1[p], band[p * N_ROW + r, 1])
        solved = dot3(tile, weights1)
        raw[at, :] = solved
        row_high2[p], row_low2[p] = split(solved)

    for copy in col_copies:
        copy.wait()
    lax.fori_loop(0, TC, column, 0, unroll=2)
    for copy in small[2:] + copies:
        copy.wait()

    size = STEP * NB

    def multiply(step, q, product):
        at = pl.ds(step * STEP, STEP)
        high = jnp.concatenate([row_high1[at].reshape(size, NB), row_high2[at].reshape(size, NB)], axis=1)
        low = jnp.concatenate([row_low1[at].reshape(size, NB), row_low2[at].reshape(size, NB)], axis=1)
        full = dot(high, col_high[q])
        rest = dot(jnp.concatenate([high, low], axis=1), join(col_low[q], col_high[q]))
        for p in range(STEP):
            code = band[(step * STEP + p) * N_ROW + r, q * N_COL + c]
            at = slice(p * NB, (p + 1) * NB)
            total = jnp.where(code == 2, 0.0, full[at] + jnp.where(code == 0, rest[at], 0.0))
            for b in range(2):
                product[b * TC + q, at, :] = total[:, b * HALF : (b + 1) * HALF]

    def subtract(step, share, product):
        for a in range(share * size // TC, (share + 1) * size // TC, PART):
            turned = product[:, a : a + PART, :].transpose(1, 0, 2).reshape(PART * 2 * TC, HALF)
            at = pl.ds(a % NB * 2 * TC, PART * 2 * TC)
            tiles[step * STEP + a // NB, at, :] -= turned

    steps = TR // STEP
    stores = [pltpu.make_async_copy(tiles.at[p], out.at[p], out_sems.at[p]) for p in range(TR)]
    for step in range(-1, steps + 1):
        product, before = (even, odd) if step % 2 == 0 else (odd, even)
        if step > 0:
            for p in range(STEP):
                loads[(step - 1) * STEP + p].wait()
        for q in range(TC):
            if step + 1 < steps and q < STEP:
                solve((step + 1) * STEP + q)
            if 0 <= step < steps:
                multiply(step, q, product)
            if step > 0:
                subtract(step - 1, q, before)
        if step + 1 < steps:
            for p in range(STEP):
                panels[(step + 1) * STEP + p].start()
        if step > 0:
            for p in range(STEP):
                stores[(step - 1) * STEP + p].start()
    for copy in stores + panels:
        copy.wait()


def finish(pieces, cols, pivots, matrix, inv, first, band):
    view = matrix.reshape(TR, NB, TC, 2, HALF).transpose(0, 1, 3, 2, 4).reshape(TR, LINES, HALF)
    out, panel = pl.pallas_call(
        last_kernel,
        out_shape=(
            jax.ShapeDtypeStruct((TR, LINES, HALF), F32),
            jax.ShapeDtypeStruct((TR, NB, NB), F32),
        ),
        in_specs=[ANY] * (SIDE + N_ROW + 4 + 4) + [SMEM],
        out_specs=[ANY] * 2,
        scratch_shapes=[
            pltpu.VMEM((TR, LINES, HALF), F32),
            pltpu.VMEM((ROWS, NB), F32),
            pltpu.VMEM((2, COLS, NB), F32),
            pltpu.VMEM((TR, NB, NB), BF16),
            pltpu.VMEM((TR, NB, NB), BF16),
            pltpu.VMEM((TR, NB, NB), BF16),
            pltpu.VMEM((TR, NB, NB), BF16),
            pltpu.VMEM((TC, PAIR, NB), BF16),
            pltpu.VMEM((TC, PAIR, NB), BF16),
            pltpu.VMEM((2 * TC, STEP * NB, HALF), F32),
            pltpu.VMEM((2 * TC, STEP * NB, HALF), F32),
            pltpu.VMEM((2, NB, NB), F32),
            pltpu.VMEM((NB, NB), F32),
            pltpu.SemaphoreType.DMA((SIDE,)),
            pltpu.SemaphoreType.DMA((N_ROW,)),
            pltpu.SemaphoreType.DMA((TR,)),
            pltpu.SemaphoreType.DMA((TR,)),
            pltpu.SemaphoreType.DMA((TR,)),
            pltpu.SemaphoreType.DMA((4,)),
        ],
        compiler_params=pltpu.CompilerParams(vmem_limit_bytes=40 * 1024 * 1024),
        cost_estimate=pl.CostEstimate(flops=200 * 2 * NB**3, bytes_accessed=20 * 2**20, transcendentals=0),
        name="solve_and_update",
    )(*pieces, *cols, *pivots, view, inv, *first, band)
    return out.reshape(TR, NB, 2, TC, HALF).transpose(0, 1, 3, 2, 4).reshape(TR, NB, TC, NB), panel


def body(matrix, diag_inverses, band):
    raw = lax.optimization_barrier(matrix[:, :, 0, :].reshape(ROWS, NB))
    panel1, panel2, cols, pivots = gather_all(raw, lax.axis_index("row"), lax.axis_index("col"))
    first = solve_first(panel1, diag_inverses)
    return finish(panel2, cols, pivots, matrix, diag_inverses, first, band)


def solution(mesh):
    in_specs = (P(None, "row", None, "col"), P(), P())
    out_specs = (P(None, "row", None, "col"), P(None, "row", None))
    return jax.shard_map(body, mesh=mesh, in_specs=in_specs, out_specs=out_specs, check_vma=False)
```

```python
import functools

import jax
import jax.numpy as jnp
from jax import lax
from jax.experimental import pallas as pl
from jax.experimental.pallas import tpu as pltpu
from jax.sharding import PartitionSpec as P

NB = 256
HALF = 128
TR = 8
TC = 4
N_ROW = 8
N_COL = 16
SIDE = 4
F32 = jnp.float32
BF16 = jnp.bfloat16


def split(value):
    high = value.astype(BF16)
    return high, (value - high.astype(F32)).astype(BF16)


def dot(a, b):
    return jnp.dot(a, b, preferred_element_type=F32)


def dot3(a, weights):
    high, low = split(a)
    return dot(jnp.concatenate([high, high, low], axis=1), weights)


def deep(value):
    high, low = split(value)
    return jnp.concatenate([high, low, high], axis=0)


def shift_plane(value, by, swapped):
    pairs = []
    for r in range(N_ROW):
        for x in range(SIDE):
            for z in range(SIDE):
                along_z = (r % 2 == 1) != swapped
                to = (x, (z + by) % SIDE) if along_z else ((x + by) % SIDE, z)
                pairs.append((r * N_COL + x * SIDE + z, r * N_COL + to[0] * SIDE + to[1]))
    return lax.ppermute(value, ("row", "col"), pairs)


def shift_line(value, by):
    return shift_plane(value, by, False)


def shift_cross(value, by):
    return shift_plane(value, by, True)


def send_far(value):
    pairs = []
    for r in range(N_ROW):
        for root in range(2):
            to = root + 2 if r % 2 else 2 * SIDE + root
            pairs.append((r * N_COL + root, r * N_COL + to))
    return lax.ppermute(value, ("row", "col"), pairs)


def shift_y(value, by):
    pairs = [(y * 2 + k, (y + by) % SIDE * 2 + k) for y in range(SIDE) for k in range(2)]
    return lax.ppermute(value, "row", pairs)


def swap_core(value):
    return lax.ppermute(value, "row", [(r, r ^ 1) for r in range(N_ROW)])


def tile_choice(r, line, cross):
    turned = (cross - r // 4) % SIDE
    return (turned // 2, turned % 2) if r % 2 else (cross % 2, cross // 2)


def to_columns(value):
    pairs = []
    for r in range(N_ROW):
        for x in range(SIDE):
            for z in range(SIDE):
                line, cross = (z, x) if r % 2 else (x, z)
                odd, panel = tile_choice(r, line, cross)
                quarter = (line - panel * (r % 2)) % SIDE
                target = ((quarter + r // 2) % SIDE * 2 + panel) * N_COL + r + N_ROW * odd
                pairs.append((r * N_COL + x * SIDE + z, target))
    return lax.ppermute(value, ("row", "col"), pairs)


def send_corner(value, moves):
    return lax.ppermute(value, ("row", "col"), [(N_COL + a, N_COL + b) for a, b in moves])


def relay_y(near, back, core):
    pairs = [(r, (r + (2 if r % 2 == 0 else -2)) % N_ROW) for r in range(N_ROW)]
    return lax.ppermute(jnp.where(core == 0, near, back), "row", pairs)


def choose(place, own, near, far, back):
    return jnp.where(place == 0, own, jnp.where(place == 1, near, jnp.where(place == 2, far, back)))


def join(one, two):
    return jnp.concatenate([one, two], axis=0)


PAIR = 2 * NB


def gather_all(raw, row, col):
    barrier = lax.optimization_barrier
    x, z, core = col // SIDE, col % SIDE, row % 2
    line, cross = jnp.where(core == 0, x, z), jnp.where(core == 0, z, x)

    near, back, far, *spread = barrier((
        shift_line(raw[PAIR : 2 * PAIR], 1),
        shift_line(raw[3 * PAIR :], -1),
        send_far(raw[2 * PAIR : 3 * PAIR]),
        *[send_corner(raw[:NB], [(0, a)]) for a in range(1, SIDE)],
    ))
    pivot = jnp.where(z == 0, raw[:NB], sum(spread))
    places = raw[:PAIR], near, far, back
    own1 = choose(line, *places)
    own2 = choose((line + SIDE - 1) % SIDE, *places)

    near1, back2 = shift_cross(own1, 1), shift_cross(own2, -1)
    back1, near2 = shift_cross(own1, -1), shift_cross(own2, 1)
    far1, far2 = shift_cross(near1, 1), shift_cross(back2, -1)
    spread = [send_corner(pivot, [(a, b * SIDE + a) for a in range(SIDE)]) for b in range(1, SIDE)]
    near1, far1, back1, near2, far2, back2, *spread = barrier((near1, far1, back1, near2, far2, back2, *spread))
    pivot = jnp.where(x == 0, pivot, sum(spread))
    after = (cross + SIDE - 1) % SIDE
    block1 = choose(cross, own1, near1, far1, back1)
    block2 = jnp.where(
        core == 0,
        choose(after, own1, near1, far1, back1),
        choose(cross, own2, near2, far2, back2),
    )
    turned = (cross - row // 4) % SIDE
    odd = jnp.where(core == 0, cross % 2, turned // 2)
    panel = jnp.where(core == 0, cross // 2, turned % 2)
    tile = lax.dynamic_slice(jnp.where(panel == 0, block1, block2), (odd * NB, 0), (NB, NB))
    block1, block2, tile, pivot = barrier((block1, block2, tile, pivot))

    near1, back2, back1, near2, own, pivot_swap, *odd = barrier((
        shift_line(block1, 1),
        shift_line(block2, -1),
        shift_line(block1, -1),
        shift_line(block2, 1),
        to_columns(tile),
        lax.ppermute(pivot, "row", [(1, 0)]),
        *[lax.ppermute(pivot, "row", [(1, to)]) for to in (3, 5, 7)],
    ))
    near1, back2, own, odd = barrier((near1, back2, own, sum(odd)))
    far1, far2, up, down, own_other, even = barrier((
        shift_line(near1, 1),
        shift_line(back2, -1),
        shift_y(own, 1),
        shift_y(own, -1),
        swap_core(own),
        lax.ppermute(odd, "row", [(3, 2), (5, 4), (7, 6)]),
    ))
    panel1 = [block1, near1, far1, back1]
    panel2 = [block2, near2, far2, back2]
    pivots = [pivot_swap, pivot, even, odd]
    last, up_other, down_other = relay_y(up, down, core), swap_core(up), swap_core(down)
    return panel1, panel2, (own, up, last, down, own_other, up_other, down_other), pivots


VMEM = pl.BlockSpec(memory_space=pltpu.VMEM)
SMEM = pl.BlockSpec(memory_space=pltpu.SMEM)
ANY = pl.BlockSpec(memory_space=pl.ANY)
ROWS = TR * NB
COLS = TC * NB


def rows_at(index, size):
    return pl.ds(pl.multiple_of(index * size, size), size)


def plane_copies(refs, raw, sems, panel):
    c, core = lax.axis_index("col"), lax.rem(lax.axis_index("row"), 2)
    x, z = lax.div(c, SIDE), lax.rem(c, SIDE)
    line = jnp.where(core == 0, x, z + SIDE - panel)
    copies = []
    for n in range(SIDE):
        place = lax.rem(line + SIDE - n, SIDE)
        copies.append(pltpu.make_async_copy(refs[n], raw.at[rows_at(place, PAIR), :], sems.at[n]))
    return copies


def column_copies(tiles, raw, sems):
    r = lax.axis_index("row")
    y, core = lax.div(r, 2), lax.rem(r, 2)
    copies = []
    for n in range(N_ROW):
        k = lax.rem(y + SIDE - n % SIDE, SIDE) * 2 + lax.rem(core + n // SIDE, 2)
        source_y = lax.div(lax.rem(lax.axis_index("col"), N_ROW), 2)
        tile = lax.rem(lax.div(k, 2) + SIDE - source_y, SIDE)
        target = raw.at[lax.rem(k, 2), rows_at(tile, NB), :]
        copies.append(pltpu.make_async_copy(tiles[n], target, sems.at[n]))
    return copies


def rows_kernel(*refs):
    pieces1, pieces2, pivots = refs[:SIDE], refs[SIDE : 2 * SIDE], refs[2 * SIDE : 3 * SIDE]
    inv_in, band, high1, low1, high2, low2, one, panel, raw1, raw2, inv, pivot, *sems = refs[3 * SIDE :]
    sems1, sems2, small_sems, panel_sems = sems
    r = lax.axis_index("row")
    copies1 = plane_copies(pieces1, raw1, sems1, 0)
    copies2 = plane_copies(pieces2, raw2, sems2, 1)
    pltpu.make_async_copy(inv_in, inv, small_sems.at[0]).start()
    for n, rows in enumerate(((0,), (1,), (2, 4, 6), (3, 5, 7))):

        @pl.when(functools.reduce(jnp.logical_or, [r == row for row in rows]))
        def _():
            pltpu.make_async_copy(pivots[n], pivot, small_sems.at[1]).start()

    for copy in copies1 + copies2:
        copy.start()
    pltpu.make_async_copy(inv_in, inv, small_sems.at[0]).wait()
    weights0 = deep(inv[0].T)
    weights1 = deep(inv[1].T)
    pltpu.make_async_copy(pivots[0], pivot, small_sems.at[1]).wait()
    one_high, one_low = split(dot3(pivot[...], weights0).T)
    one[:NB], one[NB:] = one_high, one_low
    rest_weights = join(one_low, one_high)
    for copy in copies1 + copies2:
        copy.wait()

    def solve(i, carry):
        at, tiles = rows_at(i, PAIR), pl.ds(2 * i, 2)
        high, low = split(dot3(raw1[at, :], weights0))
        high1[tiles], low1[tiles] = high.reshape(2, NB, NB), low.reshape(2, NB, NB)
        full = dot(high, one_high)
        rest = dot(jnp.concatenate([high, low], axis=1), rest_weights)
        used = []
        for n in range(2):
            code, part = band[(2 * i + n) * N_ROW + r, 1], slice(n * NB, (n + 1) * NB)
            used.append(jnp.where(code == 2, 0.0, full[part] + jnp.where(code == 0, rest[part], 0.0)))
        solved = dot3(raw2[at, :] - join(*used), weights1)
        raw2[at, :] = solved
        high, low = split(solved)
        high2[tiles], low2[tiles] = high.reshape(2, NB, NB), low.reshape(2, NB, NB)
        return carry

    lax.fori_loop(0, TR // 2, solve, 0, unroll=2)
    panels = [pltpu.make_async_copy(raw2.at[pl.ds(p * NB, NB), :], panel.at[p], panel_sems.at[p]) for p in range(TR)]
    for copy in panels:
        copy.start()
    for copy in panels:
        copy.wait()


def solve_rows(pieces1, pieces2, pivots, inv, band):
    half = jax.ShapeDtypeStruct((TR, NB, NB), BF16)
    return pl.pallas_call(
        rows_kernel,
        out_shape=[half] * 4 + [jax.ShapeDtypeStruct((PAIR, NB), BF16), jax.ShapeDtypeStruct((TR, NB, NB), F32)],
        in_specs=[ANY] * (3 * SIDE + 1) + [SMEM],
        out_specs=[VMEM] * 5 + [ANY],
        scratch_shapes=[
            pltpu.VMEM((ROWS, NB), F32),
            pltpu.VMEM((ROWS, NB), F32),
            pltpu.VMEM((2, NB, NB), F32),
            pltpu.VMEM((NB, NB), F32),
            pltpu.SemaphoreType.DMA((SIDE,)),
            pltpu.SemaphoreType.DMA((SIDE,)),
            pltpu.SemaphoreType.DMA((2,)),
            pltpu.SemaphoreType.DMA((TR,)),
        ],
        compiler_params=pltpu.CompilerParams(vmem_limit_bytes=24 * 1024 * 1024),
        cost_estimate=pl.CostEstimate(flops=80 * 2 * NB**3, bytes_accessed=10 * 2**20, transcendentals=0),
        name="solve_rows",
    )(*pieces1, *pieces2, *pivots, inv, band)


STEP = 2
LINES = NB * TC * 2
PART = 32


def last_kernel(*refs):
    cols, refs = refs[:N_ROW], refs[N_ROW:]
    matrix, inv_in, *rows_in, one_in, band, out, tiles, raw_cols = refs[:11]
    row_high1, row_low1, row_high2, row_low2, one, col_high, col_low, even, odd, inv, *sems = refs[11:]
    col_sems, in_sems, out_sems, small_sems = sems
    r, c = lax.axis_index("row"), lax.axis_index("col")
    col_copies = column_copies(cols, raw_cols, col_sems)
    loads = [pltpu.make_async_copy(matrix.at[p], tiles.at[p], in_sems.at[p]) for p in range(TR)]
    small = [(inv_in, inv), (one_in, one), *zip(rows_in, (row_high1, row_low1, row_high2, row_low2))]
    small = [pltpu.make_async_copy(a, b, small_sems.at[n]) for n, (a, b) in enumerate(small)]
    for copy in small[:2] + col_copies + small[2:] + loads:
        copy.start()
    small[0].wait()
    weights0 = deep(inv[0].T)
    weights1 = deep(inv[1].T)
    small[1].wait()
    one_high = one[:NB]
    rest_weights = join(one[NB:], one_high)
    for copy in col_copies:
        copy.wait()

    def column(q, carry):
        first = dot3(raw_cols[0, rows_at(q, NB), :], weights0)
        col_high[q, :NB, :], col_low[q, :NB, :] = split(first.T)
        high, low = split(first)
        code = band[q * N_COL + c, 1]
        rest = dot(jnp.concatenate([high, low], axis=1), rest_weights)
        used = jnp.where(code == 2, 0.0, dot(high, one_high) + jnp.where(code == 0, rest, 0.0))
        solved = dot3(raw_cols[1, rows_at(q, NB), :] - used, weights1)
        col_high[q, NB:, :], col_low[q, NB:, :] = split(solved.T)
        return carry

    lax.fori_loop(0, TC, column, 0, unroll=2)
    for copy in small[2:]:
        copy.wait()
    size = STEP * NB

    def multiply(step, q, product):
        at = pl.ds(step * STEP, STEP)
        high = jnp.concatenate([row_high1[at].reshape(size, NB), row_high2[at].reshape(size, NB)], axis=1)
        low = jnp.concatenate([row_low1[at].reshape(size, NB), row_low2[at].reshape(size, NB)], axis=1)
        full = dot(high, col_high[q])
        rest = dot(jnp.concatenate([high, low], axis=1), join(col_low[q], col_high[q]))
        for p in range(STEP):
            code = band[(step * STEP + p) * N_ROW + r, q * N_COL + c]
            at = slice(p * NB, (p + 1) * NB)
            total = jnp.where(code == 2, 0.0, full[at] + jnp.where(code == 0, rest[at], 0.0))
            for b in range(2):
                product[b * TC + q, at, :] = total[:, b * HALF : (b + 1) * HALF]

    def subtract(step, share, product):
        for a in range(share * size // TC, (share + 1) * size // TC, PART):
            turned = product[:, a : a + PART, :].transpose(1, 0, 2).reshape(PART * 2 * TC, HALF)
            at = pl.ds(a % NB * 2 * TC, PART * 2 * TC)
            tiles[step * STEP + a // NB, at, :] -= turned

    steps = TR // STEP
    stores = [pltpu.make_async_copy(tiles.at[p], out.at[p], out_sems.at[p]) for p in range(TR)]
    for step in range(steps + 1):
        product, before = (even, odd) if step % 2 == 0 else (odd, even)
        if step > 0:
            for p in range(STEP):
                loads[(step - 1) * STEP + p].wait()
        for q in range(TC):
            if step < steps:
                multiply(step, q, product)
            if step > 0:
                subtract(step - 1, q, before)
        if step > 0:
            for p in range(STEP):
                stores[(step - 1) * STEP + p].start()
    for copy in stores:
        copy.wait()


def finish(cols, matrix, inv, rows, one, band):
    view = matrix.reshape(TR, NB, TC, 2, HALF).transpose(0, 1, 3, 2, 4).reshape(TR, LINES, HALF)
    half = pltpu.VMEM((TR, NB, NB), BF16)
    out = pl.pallas_call(
        last_kernel,
        out_shape=jax.ShapeDtypeStruct((TR, LINES, HALF), F32),
        in_specs=[ANY] * (N_ROW + 7) + [SMEM],
        out_specs=ANY,
        scratch_shapes=[
            pltpu.VMEM((TR, LINES, HALF), F32),
            pltpu.VMEM((2, COLS, NB), F32),
            half,
            half,
            half,
            half,
            pltpu.VMEM((PAIR, NB), BF16),
            pltpu.VMEM((TC, PAIR, NB), BF16),
            pltpu.VMEM((TC, PAIR, NB), BF16),
            pltpu.VMEM((2 * TC, STEP * NB, HALF), F32),
            pltpu.VMEM((2 * TC, STEP * NB, HALF), F32),
            pltpu.VMEM((2, NB, NB), F32),
            pltpu.SemaphoreType.DMA((N_ROW,)),
            pltpu.SemaphoreType.DMA((TR,)),
            pltpu.SemaphoreType.DMA((TR,)),
            pltpu.SemaphoreType.DMA((6,)),
        ],
        compiler_params=pltpu.CompilerParams(vmem_limit_bytes=42 * 1024 * 1024),
        cost_estimate=pl.CostEstimate(flops=220 * 2 * NB**3, bytes_accessed=20 * 2**20, transcendentals=0),
        name="update_tiles",
    )(*cols, view, inv, *rows, one, band)
    return out.reshape(TR, NB, 2, TC, HALF).transpose(0, 1, 3, 2, 4).reshape(TR, NB, TC, NB)


def body(matrix, diag_inverses, band):
    raw = lax.optimization_barrier(matrix[:, :, 0, :].reshape(ROWS, NB))
    panel1, panel2, cols, pivots = gather_all(raw, lax.axis_index("row"), lax.axis_index("col"))
    *rows, one, panel = solve_rows(panel1, panel2, pivots, diag_inverses, band)
    cols, rows = lax.optimization_barrier((cols, rows))
    own, up, last, down, own_other, up_other, down_other = cols
    cols = [own, up, last, down, own_other, up_other, swap_core(last), down_other]
    return finish(cols, matrix, diag_inverses, rows, one, band), panel


def solution(mesh):
    in_specs = (P(None, "row", None, "col"), P(), P())
    out_specs = (P(None, "row", None, "col"), P(None, "row", None))
    return jax.shard_map(body, mesh=mesh, in_specs=in_specs, out_specs=out_specs, check_vma=False)
```

```python
import functools

import jax
import jax.numpy as jnp
from jax import lax
from jax.experimental import pallas as pl
from jax.experimental.pallas import tpu as pltpu
from jax.sharding import PartitionSpec as P

NB = 256
HALF = 128
TR = 8
TC = 4
N_ROW = 8
N_COL = 16
SIDE = 4
F32 = jnp.float32
BF16 = jnp.bfloat16


def split(value):
    high = value.astype(BF16)
    return high, (value - high.astype(F32)).astype(BF16)


def dot(a, b):
    return jnp.dot(a, b, preferred_element_type=F32)


def dot3(a, weights):
    high, low = split(a)
    return dot(jnp.concatenate([high, high, low], axis=1), weights)


def deep(value):
    high, low = split(value)
    return jnp.concatenate([high, low, high], axis=0)


def shift_plane(value, by, swapped):
    pairs = []
    for r in range(N_ROW):
        for x in range(SIDE):
            for z in range(SIDE):
                along_z = (r % 2 == 1) != swapped
                to = (x, (z + by) % SIDE) if along_z else ((x + by) % SIDE, z)
                pairs.append((r * N_COL + x * SIDE + z, r * N_COL + to[0] * SIDE + to[1]))
    return lax.ppermute(value, ("row", "col"), pairs)


def shift_line(value, by):
    return shift_plane(value, by, False)


def shift_cross(value, by):
    return shift_plane(value, by, True)


def send_far(value):
    pairs = []
    for r in range(N_ROW):
        for root in range(2):
            to = root + 2 if r % 2 else 2 * SIDE + root
            pairs.append((r * N_COL + root, r * N_COL + to))
    return lax.ppermute(value, ("row", "col"), pairs)


def shift_y(value, by):
    pairs = [(y * 2 + k, (y + by) % SIDE * 2 + k) for y in range(SIDE) for k in range(2)]
    return lax.ppermute(value, "row", pairs)


def swap_core(value):
    return lax.ppermute(value, "row", [(r, r ^ 1) for r in range(N_ROW)])


def tile_choice(r, line, cross):
    turned = (cross - r // 4) % SIDE
    return (turned // 2, turned % 2) if r % 2 else (cross % 2, cross // 2)


def to_columns(value):
    pairs = []
    for r in range(N_ROW):
        for x in range(SIDE):
            for z in range(SIDE):
                line, cross = (z, x) if r % 2 else (x, z)
                odd, panel = tile_choice(r, line, cross)
                quarter = (line - panel * (r % 2)) % SIDE
                target = ((quarter + r // 2) % SIDE * 2 + panel) * N_COL + r + N_ROW * odd
                pairs.append((r * N_COL + x * SIDE + z, target))
    return lax.ppermute(value, ("row", "col"), pairs)


def relay_y(near, back, core):
    pairs = [(r, (r + (2 if r % 2 == 0 else -2)) % N_ROW) for r in range(N_ROW)]
    return lax.ppermute(jnp.where(core == 0, near, back), "row", pairs)


def choose(place, own, near, far, back):
    return jnp.where(place == 0, own, jnp.where(place == 1, near, jnp.where(place == 2, far, back)))


def join(one, two):
    return jnp.concatenate([one, two], axis=0)


PAIR = 2 * NB


def gather_all(raw, row, col):
    barrier = lax.optimization_barrier
    x, z, core = col // SIDE, col % SIDE, row % 2
    line, cross = jnp.where(core == 0, x, z), jnp.where(core == 0, z, x)

    near, back, far = barrier((
        shift_line(raw[PAIR : 2 * PAIR], 1),
        shift_line(raw[3 * PAIR :], -1),
        send_far(raw[2 * PAIR : 3 * PAIR]),
    ))
    places = raw[:PAIR], near, far, back
    own1 = choose(line, *places)
    own2 = choose((line + SIDE - 1) % SIDE, *places)

    near1, back2 = shift_cross(own1, 1), shift_cross(own2, -1)
    back1, near2 = shift_cross(own1, -1), shift_cross(own2, 1)
    far1, far2 = shift_cross(near1, 1), shift_cross(back2, -1)
    near1, far1, back1, near2, far2, back2 = barrier((near1, far1, back1, near2, far2, back2))
    after = (cross + SIDE - 1) % SIDE
    block1 = choose(cross, own1, near1, far1, back1)
    block2 = jnp.where(
        core == 0,
        choose(after, own1, near1, far1, back1),
        choose(cross, own2, near2, far2, back2),
    )
    turned = (cross - row // 4) % SIDE
    odd = jnp.where(core == 0, cross % 2, turned // 2)
    panel = jnp.where(core == 0, cross // 2, turned % 2)
    tile = lax.dynamic_slice(jnp.where(panel == 0, block1, block2), (odd * NB, 0), (NB, NB))
    block1, block2, tile = barrier((block1, block2, tile))

    near1, back2 = shift_line(block1, 1), shift_line(block2, -1)
    back1, near2 = shift_line(block1, -1), shift_line(block2, 1)
    far1, far2 = shift_line(near1, 1), shift_line(back2, -1)
    near1, far1, back1, near2, far2, back2, own = barrier((near1, far1, back1, near2, far2, back2, to_columns(tile)))
    pivot = choose(z, block1[:NB], near1[:NB], far1[:NB], back1[:NB])
    up, down, own_other, pivot_up, pivot_down, pivot_far, pivot_swap = barrier((
        shift_y(own, 1),
        shift_y(own, -1),
        swap_core(own),
        lax.ppermute(pivot, "row", [(1, 3)]),
        lax.ppermute(pivot, "row", [(1, 7)]),
        lax.ppermute(pivot, "row", [(1, 5)]),
        lax.ppermute(pivot, "row", [(1, 0)]),
    ))
    panel1 = [block1, near1, far1, back1]
    panel2 = [block2, near2, far2, back2]
    odd = pivot_up + pivot_down + pivot_far
    last, up_other, down_other, even = barrier((
        relay_y(up, down, core),
        swap_core(up),
        swap_core(down),
        lax.ppermute(odd, "row", [(3, 2), (5, 4), (7, 6)]),
    ))
    cols = [own, up, last, down, own_other, up_other, swap_core(last), down_other]
    pivots = [pivot_swap, pivot, even, odd]
    return panel1, panel2, cols, pivots


VMEM = pl.BlockSpec(memory_space=pltpu.VMEM)
SMEM = pl.BlockSpec(memory_space=pltpu.SMEM)
ANY = pl.BlockSpec(memory_space=pl.ANY)
ROWS = TR * NB
COLS = TC * NB


def rows_at(index, size):
    return pl.ds(pl.multiple_of(index * size, size), size)


def plane_copies(refs, raw, sems, panel):
    c, core = lax.axis_index("col"), lax.rem(lax.axis_index("row"), 2)
    x, z = lax.div(c, SIDE), lax.rem(c, SIDE)
    line = jnp.where(core == 0, x, z + SIDE - panel)
    copies = []
    for n in range(SIDE):
        place = lax.rem(line + SIDE - n, SIDE)
        copies.append(pltpu.make_async_copy(refs[n], raw.at[rows_at(place, PAIR), :], sems.at[n]))
    return copies


def column_copies(tiles, raw, sems):
    r = lax.axis_index("row")
    y, core = lax.div(r, 2), lax.rem(r, 2)
    copies = []
    for n in range(N_ROW):
        k = lax.rem(y + SIDE - n % SIDE, SIDE) * 2 + lax.rem(core + n // SIDE, 2)
        source_y = lax.div(lax.rem(lax.axis_index("col"), N_ROW), 2)
        tile = lax.rem(lax.div(k, 2) + SIDE - source_y, SIDE)
        target = raw.at[lax.rem(k, 2), rows_at(tile, NB), :]
        copies.append(pltpu.make_async_copy(tiles[n], target, sems.at[n]))
    return copies


def first_kernel(*refs):
    pieces, inv_in, row_high, row_low, raw, inv, sems = refs[:SIDE], *refs[SIDE:]
    copies = plane_copies(pieces, raw, sems, 0)
    weights_copy = pltpu.make_async_copy(inv_in.at[0], inv, sems.at[SIDE])
    for copy in [weights_copy, *copies]:
        copy.start()
    weights_copy.wait()
    weights = deep(inv[...].T)
    for copy in copies:
        copy.wait()

    def row(p, carry):
        solved = dot3(raw[rows_at(p, PAIR), :], weights).reshape(2, NB, NB)
        high, low = split(solved)
        row_high[pl.ds(2 * p, 2)] = high
        row_low[pl.ds(2 * p, 2)] = low
        return carry

    lax.fori_loop(0, TR // 2, row, 0)


def solve_first(pieces, inv):
    return pl.pallas_call(
        first_kernel,
        out_shape=[jax.ShapeDtypeStruct((TR, NB, NB), BF16)] * 2,
        in_specs=[ANY] * (SIDE + 1),
        out_specs=[VMEM] * 2,
        scratch_shapes=[
            pltpu.VMEM((ROWS, NB), F32),
            pltpu.VMEM((NB, NB), F32),
            pltpu.SemaphoreType.DMA((SIDE + 1,)),
        ],
        compiler_params=pltpu.CompilerParams(vmem_limit_bytes=16 * 1024 * 1024),
        cost_estimate=pl.CostEstimate(flops=8 * 3 * 2 * NB**3, bytes_accessed=4 * 2**20, transcendentals=0),
        name="solve_first",
    )(*pieces, inv)


STEP = 2
LINES = NB * TC * 2
PART = 32


def last_kernel(*refs):
    pieces, cols = refs[:SIDE], refs[SIDE : SIDE + N_ROW]
    pivots, refs = refs[SIDE + N_ROW : SIDE + N_ROW + 4], refs[SIDE + N_ROW + 4 :]
    matrix, inv_in, high_in, low_in, band, out, panel, *refs = refs
    tiles, raw, raw_cols, row_high1, row_low1, row_high2, row_low2, col_high, col_low, even, odd, *refs = refs
    inv, pivot, sems, col_sems, in_sems, out_sems, panel_sems, small_sems = refs
    r, c = lax.axis_index("row"), lax.axis_index("col")
    copies = plane_copies(pieces, raw, sems, 1)
    col_copies = column_copies(cols, raw_cols, col_sems)
    loads = [pltpu.make_async_copy(matrix.at[p], tiles.at[p], in_sems.at[p]) for p in range(TR)]
    small = [(inv_in, inv), (pivots[0], pivot), (high_in, row_high1), (low_in, row_low1)]
    small = [pltpu.make_async_copy(a, b, small_sems.at[n]) for n, (a, b) in enumerate(small)]
    small[0].start()
    for n, rows in enumerate(((0,), (1,), (2, 4, 6), (3, 5, 7))):

        @pl.when(functools.reduce(jnp.logical_or, [r == row for row in rows]))
        def _():
            pltpu.make_async_copy(pivots[n], pivot, small_sems.at[1]).start()

    for copy in small[2:] + copies + col_copies + loads:
        copy.start()
    small[0].wait()
    weights0 = deep(inv[0].T)
    weights1 = deep(inv[1].T)
    small[1].wait()
    one_high, one_low = split(dot3(pivot[...], weights0).T)
    rest_weights = join(one_low, one_high)

    def used(high, low, code):
        full = dot(high, one_high)
        rest = dot(jnp.concatenate([high, low], axis=1), rest_weights)
        return jnp.where(code == 2, 0.0, full + jnp.where(code == 0, rest, 0.0))

    def column(q, carry):
        first = dot3(raw_cols[0, rows_at(q, NB), :], weights0)
        col_high[q, :NB, :], col_low[q, :NB, :] = split(first.T)
        high, low = split(first)
        tile = raw_cols[1, rows_at(q, NB), :] - used(high, low, band[q * N_COL + c, 1])
        col_high[q, NB:, :], col_low[q, NB:, :] = split(dot3(tile, weights1).T)
        return carry

    panels = [pltpu.make_async_copy(raw.at[pl.ds(p * NB, NB), :], panel.at[p], panel_sems.at[p]) for p in range(TR)]

    def solve(p):
        at = pl.ds(p * NB, NB)
        tile = raw[at, :] - used(row_high1[p], row_low1[p], band[p * N_ROW + r, 1])
        solved = dot3(tile, weights1)
        raw[at, :] = solved
        row_high2[p], row_low2[p] = split(solved)

    for copy in col_copies:
        copy.wait()
    lax.fori_loop(0, TC, column, 0, unroll=2)
    for copy in small[2:] + copies:
        copy.wait()

    size = STEP * NB

    def multiply(step, q, product):
        at = pl.ds(step * STEP, STEP)
        high = jnp.concatenate([row_high1[at].reshape(size, NB), row_high2[at].reshape(size, NB)], axis=1)
        low = jnp.concatenate([row_low1[at].reshape(size, NB), row_low2[at].reshape(size, NB)], axis=1)
        full = dot(high, col_high[q])
        rest = dot(jnp.concatenate([high, low], axis=1), join(col_low[q], col_high[q]))
        for p in range(STEP):
            code = band[(step * STEP + p) * N_ROW + r, q * N_COL + c]
            at = slice(p * NB, (p + 1) * NB)
            total = jnp.where(code == 2, 0.0, full[at] + jnp.where(code == 0, rest[at], 0.0))
            for b in range(2):
                product[b * TC + q, at, :] = total[:, b * HALF : (b + 1) * HALF]

    def subtract(step, share, product):
        for a in range(share * size // TC, (share + 1) * size // TC, PART):
            turned = product[:, a : a + PART, :].transpose(1, 0, 2).reshape(PART * 2 * TC, HALF)
            at = pl.ds(a % NB * 2 * TC, PART * 2 * TC)
            tiles[step * STEP + a // NB, at, :] -= turned

    steps = TR // STEP
    stores = [pltpu.make_async_copy(tiles.at[p], out.at[p], out_sems.at[p]) for p in range(TR)]
    for step in range(-1, steps + 1):
        product, before = (even, odd) if step % 2 == 0 else (odd, even)
        if step > 0:
            for p in range(STEP):
                loads[(step - 1) * STEP + p].wait()
        for q in range(TC):
            if step + 1 < steps and q < STEP:
                solve((step + 1) * STEP + q)
            if 0 <= step < steps:
                multiply(step, q, product)
            if step > 0:
                subtract(step - 1, q, before)
        if step + 1 < steps:
            for p in range(STEP):
                panels[(step + 1) * STEP + p].start()
        if step > 0:
            for p in range(STEP):
                stores[(step - 1) * STEP + p].start()
    for copy in stores + panels:
        copy.wait()


def finish(pieces, cols, pivots, matrix, inv, first, band):
    view = matrix.reshape(TR, NB, TC, 2, HALF).transpose(0, 1, 3, 2, 4).reshape(TR, LINES, HALF)
    out, panel = pl.pallas_call(
        last_kernel,
        out_shape=(
            jax.ShapeDtypeStruct((TR, LINES, HALF), F32),
            jax.ShapeDtypeStruct((TR, NB, NB), F32),
        ),
        in_specs=[ANY] * (SIDE + N_ROW + 4 + 4) + [SMEM],
        out_specs=[ANY] * 2,
        scratch_shapes=[
            pltpu.VMEM((TR, LINES, HALF), F32),
            pltpu.VMEM((ROWS, NB), F32),
            pltpu.VMEM((2, COLS, NB), F32),
            pltpu.VMEM((TR, NB, NB), BF16),
            pltpu.VMEM((TR, NB, NB), BF16),
            pltpu.VMEM((TR, NB, NB), BF16),
            pltpu.VMEM((TR, NB, NB), BF16),
            pltpu.VMEM((TC, PAIR, NB), BF16),
            pltpu.VMEM((TC, PAIR, NB), BF16),
            pltpu.VMEM((2 * TC, STEP * NB, HALF), F32),
            pltpu.VMEM((2 * TC, STEP * NB, HALF), F32),
            pltpu.VMEM((2, NB, NB), F32),
            pltpu.VMEM((NB, NB), F32),
            pltpu.SemaphoreType.DMA((SIDE,)),
            pltpu.SemaphoreType.DMA((N_ROW,)),
            pltpu.SemaphoreType.DMA((TR,)),
            pltpu.SemaphoreType.DMA((TR,)),
            pltpu.SemaphoreType.DMA((TR,)),
            pltpu.SemaphoreType.DMA((4,)),
        ],
        compiler_params=pltpu.CompilerParams(vmem_limit_bytes=40 * 1024 * 1024),
        cost_estimate=pl.CostEstimate(flops=200 * 2 * NB**3, bytes_accessed=20 * 2**20, transcendentals=0),
        name="solve_and_update",
    )(*pieces, *cols, *pivots, view, inv, *first, band)
    return out.reshape(TR, NB, 2, TC, HALF).transpose(0, 1, 3, 2, 4).reshape(TR, NB, TC, NB), panel


def body(matrix, diag_inverses, band):
    raw = lax.optimization_barrier(matrix[:, :, 0, :].reshape(ROWS, NB))
    panel1, panel2, cols, pivots = gather_all(raw, lax.axis_index("row"), lax.axis_index("col"))
    first = solve_first(panel1, diag_inverses)
    return finish(panel2, cols, pivots, matrix, diag_inverses, first, band)


def solution(mesh):
    in_specs = (P(None, "row", None, "col"), P(), P())
    out_specs = (P(None, "row", None, "col"), P(None, "row", None))
    return jax.shard_map(body, mesh=mesh, in_specs=in_specs, out_specs=out_specs, check_vma=False)
```

```python
import jax
import jax.numpy as jnp
from jax import lax
from jax.experimental import pallas as pl
from jax.experimental.pallas import tpu as pltpu
from jax.sharding import PartitionSpec as P

NB = 256
HALF = 128
TR = 8
TC = 4
N_ROW = 8
N_COL = 16
SIDE = 4
F32 = jnp.float32
BF16 = jnp.bfloat16


def split(value):
    high = value.astype(BF16)
    return high, (value - high.astype(F32)).astype(BF16)


def dot(a, b):
    return jnp.dot(a, b, preferred_element_type=F32)


def dot3(a, weights):
    high, low = split(a)
    return dot(jnp.concatenate([high, high, low], axis=1), weights)


def deep(value):
    high, low = split(value)
    return jnp.concatenate([high, low, high], axis=0)


def shift_plane(value, by, swapped):
    pairs = []
    for r in range(N_ROW):
        for x in range(SIDE):
            for z in range(SIDE):
                along_z = (r % 2 == 1) != swapped
                to = (x, (z + by) % SIDE) if along_z else ((x + by) % SIDE, z)
                pairs.append((r * N_COL + x * SIDE + z, r * N_COL + to[0] * SIDE + to[1]))
    return lax.ppermute(value, ("row", "col"), pairs)


def shift_line(value, by):
    return shift_plane(value, by, False)


def shift_cross(value, by):
    return shift_plane(value, by, True)


def send_far(value):
    pairs = []
    for r in range(N_ROW):
        for root in range(2):
            to = root + 2 if r % 2 else 2 * SIDE + root
            pairs.append((r * N_COL + root, r * N_COL + to))
    return lax.ppermute(value, ("row", "col"), pairs)


def shift_y(value, by):
    pairs = [(y * 2 + k, (y + by) % SIDE * 2 + k) for y in range(SIDE) for k in range(2)]
    return lax.ppermute(value, "row", pairs)


def swap_core(value):
    return lax.ppermute(value, "row", [(r, r ^ 1) for r in range(N_ROW)])


def tile_choice(r, line, cross):
    turned = (cross - r // 4) % SIDE
    return (turned // 2, turned % 2) if r % 2 else (cross % 2, cross // 2)


def to_columns(value):
    pairs = []
    for r in range(N_ROW):
        for x in range(SIDE):
            for z in range(SIDE):
                line, cross = (z, x) if r % 2 else (x, z)
                odd, panel = tile_choice(r, line, cross)
                quarter = (line - panel * (r % 2)) % SIDE
                target = ((quarter + r // 2) % SIDE * 2 + panel) * N_COL + r + N_ROW * odd
                pairs.append((r * N_COL + x * SIDE + z, target))
    return lax.ppermute(value, ("row", "col"), pairs)


def relay_y(near, back, core):
    pairs = [(r, (r + (2 if r % 2 == 0 else -2)) % N_ROW) for r in range(N_ROW)]
    return lax.ppermute(jnp.where(core == 0, near, back), "row", pairs)


def choose(place, own, near, far, back):
    return jnp.where(place == 0, own, jnp.where(place == 1, near, jnp.where(place == 2, far, back)))


def join(one, two):
    return jnp.concatenate([one, two], axis=0)


PAIR = 2 * NB


def gather_all(raw, row, col):
    barrier = lax.optimization_barrier
    x, z, core = col // SIDE, col % SIDE, row % 2
    line, cross = jnp.where(core == 0, x, z), jnp.where(core == 0, z, x)

    near, back, far = barrier((
        shift_line(raw[PAIR : 2 * PAIR], 1),
        shift_line(raw[3 * PAIR :], -1),
        send_far(raw[2 * PAIR : 3 * PAIR]),
    ))
    places = raw[:PAIR], near, far, back
    own1 = choose(line, *places)
    own2 = choose((line + SIDE - 1) % SIDE, *places)

    near1, back2 = shift_cross(own1, 1), shift_cross(own2, -1)
    back1, near2 = shift_cross(own1, -1), shift_cross(own2, 1)
    far1, far2 = shift_cross(near1, 1), shift_cross(back2, -1)
    near1, far1, back1, near2, far2, back2 = barrier((near1, far1, back1, near2, far2, back2))
    after = (cross + SIDE - 1) % SIDE
    block1 = choose(cross, own1, near1, far1, back1)
    block2 = jnp.where(
        core == 0,
        choose(after, own1, near1, far1, back1),
        choose(cross, own2, near2, far2, back2),
    )
    turned = (cross - row // 4) % SIDE
    odd = jnp.where(core == 0, cross % 2, turned // 2)
    panel = jnp.where(core == 0, cross // 2, turned % 2)
    tile = lax.dynamic_slice(jnp.where(panel == 0, block1, block2), (odd * NB, 0), (NB, NB))
    block1, block2, tile = barrier((block1, block2, tile))

    near1, back2 = shift_line(block1, 1), shift_line(block2, -1)
    back1, near2 = shift_line(block1, -1), shift_line(block2, 1)
    far1, far2 = shift_line(near1, 1), shift_line(back2, -1)
    near1, far1, back1, near2, far2, back2, own = barrier((near1, far1, back1, near2, far2, back2, to_columns(tile)))
    pivot = choose(z, block1[:NB], near1[:NB], far1[:NB], back1[:NB])
    up, down, own_other, *odd = barrier((
        shift_y(own, 1),
        shift_y(own, -1),
        swap_core(own),
        *[lax.ppermute(pivot, "row", [(1, to)]) for to in (3, 5, 7)],
    ))
    panel1 = [block1, near1, far1, back1]
    panel2 = [block2, near2, far2, back2]
    odd = jnp.where(row == 1, pivot, sum(odd))
    last, up_other, down_other, even = barrier((
        relay_y(up, down, core),
        swap_core(up),
        swap_core(down),
        lax.ppermute(odd, "row", [(1, 0), (3, 2), (5, 4), (7, 6)]),
    ))
    cols = [own, up, last, down, own_other, up_other, swap_core(last), down_other]
    pivots = [even, odd]
    return panel1, panel2, cols, pivots


VMEM = pl.BlockSpec(memory_space=pltpu.VMEM)
SMEM = pl.BlockSpec(memory_space=pltpu.SMEM)
ANY = pl.BlockSpec(memory_space=pl.ANY)
ROWS = TR * NB
COLS = TC * NB


def rows_at(index, size):
    return pl.ds(pl.multiple_of(index * size, size), size)


def plane_copies(refs, raw, sems, panel):
    c, core = lax.axis_index("col"), lax.rem(lax.axis_index("row"), 2)
    x, z = lax.div(c, SIDE), lax.rem(c, SIDE)
    line = jnp.where(core == 0, x, z + SIDE - panel)
    copies = []
    for n in range(SIDE):
        place = lax.rem(line + SIDE - n, SIDE)
        copies.append(pltpu.make_async_copy(refs[n], raw.at[rows_at(place, PAIR), :], sems.at[n]))
    return copies


def column_copies(tiles, raw, sems):
    r = lax.axis_index("row")
    y, core = lax.div(r, 2), lax.rem(r, 2)
    copies = []
    for n in range(N_ROW):
        k = lax.rem(y + SIDE - n % SIDE, SIDE) * 2 + lax.rem(core + n // SIDE, 2)
        source_y = lax.div(lax.rem(lax.axis_index("col"), N_ROW), 2)
        tile = lax.rem(lax.div(k, 2) + SIDE - source_y, SIDE)
        target = raw.at[lax.rem(k, 2), rows_at(tile, NB), :]
        copies.append(pltpu.make_async_copy(tiles[n], target, sems.at[n]))
    return copies


def first_kernel(*refs):
    pieces, inv_in, row_high, row_low, raw, inv, sems = refs[:SIDE], *refs[SIDE:]
    copies = plane_copies(pieces, raw, sems, 0)
    weights_copy = pltpu.make_async_copy(inv_in.at[0], inv, sems.at[SIDE])
    for copy in [weights_copy, *copies]:
        copy.start()
    weights_copy.wait()
    weights = deep(inv[...].T)
    for copy in copies:
        copy.wait()

    def row(p, carry):
        solved = dot3(raw[rows_at(p, PAIR), :], weights).reshape(2, NB, NB)
        high, low = split(solved)
        row_high[pl.ds(2 * p, 2)] = high
        row_low[pl.ds(2 * p, 2)] = low
        return carry

    lax.fori_loop(0, TR // 2, row, 0)


def solve_first(pieces, inv):
    return pl.pallas_call(
        first_kernel,
        out_shape=[jax.ShapeDtypeStruct((TR, NB, NB), BF16)] * 2,
        in_specs=[ANY] * (SIDE + 1),
        out_specs=[VMEM] * 2,
        scratch_shapes=[
            pltpu.VMEM((ROWS, NB), F32),
            pltpu.VMEM((NB, NB), F32),
            pltpu.SemaphoreType.DMA((SIDE + 1,)),
        ],
        compiler_params=pltpu.CompilerParams(vmem_limit_bytes=16 * 1024 * 1024),
        cost_estimate=pl.CostEstimate(flops=8 * 3 * 2 * NB**3, bytes_accessed=4 * 2**20, transcendentals=0),
        name="solve_first",
    )(*pieces, inv)


STEP = 2
LINES = NB * TC * 2
PART = 32


def last_kernel(*refs):
    pieces, cols = refs[:SIDE], refs[SIDE : SIDE + N_ROW]
    pivots, refs = refs[SIDE + N_ROW : SIDE + N_ROW + 2], refs[SIDE + N_ROW + 2 :]
    matrix, inv_in, high_in, low_in, band, out, panel, *refs = refs
    tiles, raw, raw_cols, row_high1, row_low1, row_high2, row_low2, col_high, col_low, even, odd, *refs = refs
    inv, pivot, sems, col_sems, in_sems, out_sems, panel_sems, small_sems = refs
    r, c = lax.axis_index("row"), lax.axis_index("col")
    copies = plane_copies(pieces, raw, sems, 1)
    col_copies = column_copies(cols, raw_cols, col_sems)
    loads = [pltpu.make_async_copy(matrix.at[p], tiles.at[p], in_sems.at[p]) for p in range(TR)]
    small = [(inv_in, inv), (pivots[0], pivot), (high_in, row_high1), (low_in, row_low1)]
    small = [pltpu.make_async_copy(a, b, small_sems.at[n]) for n, (a, b) in enumerate(small)]
    small[0].start()
    for n in range(2):

        @pl.when(lax.rem(r, 2) == n)
        def _():
            pltpu.make_async_copy(pivots[n], pivot, small_sems.at[1]).start()

    for copy in col_copies + small[2:] + copies + loads:
        copy.start()
    small[0].wait()
    weights0 = deep(inv[0].T)
    weights1 = deep(inv[1].T)
    small[1].wait()
    one_high, one_low = split(dot3(pivot[...], weights0).T)
    rest_weights = join(one_low, one_high)

    def subtracted(raw_part, high, low, codes):
        full = dot(high, one_high)
        rest = dot(jnp.concatenate([high, low], axis=1), rest_weights)
        parts = []
        for n, code in enumerate(codes):
            at = slice(n * NB, (n + 1) * NB)
            taken = jnp.where(code == 2, 0.0, full[at] + jnp.where(code == 0, rest[at], 0.0))
            parts.append(raw_part[at] - taken)
        return jnp.concatenate(parts, axis=0)

    panels = [pltpu.make_async_copy(raw.at[pl.ds(p * NB, NB), :], panel.at[p], panel_sems.at[p]) for p in range(TR)]

    def solve(step):
        at, tiles_at = pl.ds(step * PAIR, PAIR), pl.ds(step * STEP, STEP)
        high, low = row_high1[tiles_at].reshape(PAIR, NB), row_low1[tiles_at].reshape(PAIR, NB)
        codes = [band[(step * STEP + p) * N_ROW + r, 1] for p in range(STEP)]
        solved = dot3(subtracted(raw[at, :], high, low, codes), weights1)
        raw[at, :] = solved
        high, low = split(solved)
        row_high2[tiles_at], row_low2[tiles_at] = high.reshape(STEP, NB, NB), low.reshape(STEP, NB, NB)

    for copy in col_copies:
        copy.wait()
    first = dot3(raw_cols[0], weights0)
    high, low = split(first)
    codes = [band[q * N_COL + c, 1] for q in range(TC)]
    second = dot3(subtracted(raw_cols[1], high, low, codes), weights1)
    for q in range(TC):
        at = slice(q * NB, (q + 1) * NB)
        col_high[q, :NB, :], col_low[q, :NB, :] = split(first[at].T)
        col_high[q, NB:, :], col_low[q, NB:, :] = split(second[at].T)
    for copy in small[2:] + copies:
        copy.wait()

    size = STEP * NB

    def multiply(step, q, product):
        at = pl.ds(step * STEP, STEP)
        high = jnp.concatenate([row_high1[at].reshape(size, NB), row_high2[at].reshape(size, NB)], axis=1)
        low = jnp.concatenate([row_low1[at].reshape(size, NB), row_low2[at].reshape(size, NB)], axis=1)
        full = dot(high, col_high[q])
        rest = dot(jnp.concatenate([high, low], axis=1), join(col_low[q], col_high[q]))
        for p in range(STEP):
            code = band[(step * STEP + p) * N_ROW + r, q * N_COL + c]
            at = slice(p * NB, (p + 1) * NB)
            total = jnp.where(code == 2, 0.0, full[at] + jnp.where(code == 0, rest[at], 0.0))
            for b in range(2):
                product[b * TC + q, at, :] = total[:, b * HALF : (b + 1) * HALF]

    def subtract(step, share, product):
        for a in range(share * size // TC, (share + 1) * size // TC, PART):
            turned = product[:, a : a + PART, :].transpose(1, 0, 2).reshape(PART * 2 * TC, HALF)
            at = pl.ds(a % NB * 2 * TC, PART * 2 * TC)
            tiles[step * STEP + a // NB, at, :] -= turned

    steps = TR // STEP
    stores = [pltpu.make_async_copy(tiles.at[p], out.at[p], out_sems.at[p]) for p in range(TR)]
    for step in range(-1, steps + 1):
        product, before = (even, odd) if step % 2 == 0 else (odd, even)
        if step > 0:
            for p in range(STEP):
                loads[(step - 1) * STEP + p].wait()
        for q in range(TC):
            if step + 1 < steps and q == 0:
                solve(step + 1)
            if 0 <= step < steps:
                multiply(step, q, product)
            if step > 0:
                subtract(step - 1, q, before)
        if step + 1 < steps:
            for p in range(STEP):
                panels[(step + 1) * STEP + p].start()
        if step > 0:
            for p in range(STEP):
                stores[(step - 1) * STEP + p].start()
    for copy in stores + panels:
        copy.wait()


def finish(pieces, cols, pivots, matrix, inv, first, band):
    view = matrix.reshape(TR, NB, TC, 2, HALF).transpose(0, 1, 3, 2, 4).reshape(TR, LINES, HALF)
    out, panel = pl.pallas_call(
        last_kernel,
        out_shape=(
            jax.ShapeDtypeStruct((TR, LINES, HALF), F32),
            jax.ShapeDtypeStruct((TR, NB, NB), F32),
        ),
        in_specs=[ANY] * (SIDE + N_ROW + 2 + 4) + [SMEM],
        out_specs=[ANY] * 2,
        scratch_shapes=[
            pltpu.VMEM((TR, LINES, HALF), F32),
            pltpu.VMEM((ROWS, NB), F32),
            pltpu.VMEM((2, COLS, NB), F32),
            pltpu.VMEM((TR, NB, NB), BF16),
            pltpu.VMEM((TR, NB, NB), BF16),
            pltpu.VMEM((TR, NB, NB), BF16),
            pltpu.VMEM((TR, NB, NB), BF16),
            pltpu.VMEM((TC, PAIR, NB), BF16),
            pltpu.VMEM((TC, PAIR, NB), BF16),
            pltpu.VMEM((2 * TC, STEP * NB, HALF), F32),
            pltpu.VMEM((2 * TC, STEP * NB, HALF), F32),
            pltpu.VMEM((2, NB, NB), F32),
            pltpu.VMEM((NB, NB), F32),
            pltpu.SemaphoreType.DMA((SIDE,)),
            pltpu.SemaphoreType.DMA((N_ROW,)),
            pltpu.SemaphoreType.DMA((TR,)),
            pltpu.SemaphoreType.DMA((TR,)),
            pltpu.SemaphoreType.DMA((TR,)),
            pltpu.SemaphoreType.DMA((4,)),
        ],
        compiler_params=pltpu.CompilerParams(vmem_limit_bytes=40 * 1024 * 1024),
        cost_estimate=pl.CostEstimate(flops=200 * 2 * NB**3, bytes_accessed=20 * 2**20, transcendentals=0),
        name="solve_and_update",
    )(*pieces, *cols, *pivots, view, inv, *first, band)
    return out.reshape(TR, NB, 2, TC, HALF).transpose(0, 1, 3, 2, 4).reshape(TR, NB, TC, NB), panel


def body(matrix, diag_inverses, band):
    raw = lax.optimization_barrier(matrix[:, :, 0, :].reshape(ROWS, NB))
    panel1, panel2, cols, pivots = gather_all(raw, lax.axis_index("row"), lax.axis_index("col"))
    first = solve_first(panel1, diag_inverses)
    return finish(panel2, cols, pivots, matrix, diag_inverses, first, band)


def solution(mesh):
    in_specs = (P(None, "row", None, "col"), P(), P())
    out_specs = (P(None, "row", None, "col"), P(None, "row", None))
    return jax.shard_map(body, mesh=mesh, in_specs=in_specs, out_specs=out_specs, check_vma=False)
```

```python
import functools

import jax
import jax.numpy as jnp
from jax import lax
from jax.experimental import pallas as pl
from jax.experimental.pallas import tpu as pltpu
from jax.sharding import PartitionSpec as P

NB = 256
HALF = 128
TR = 8
TC = 4
N_ROW = 8
N_COL = 16
SIDE = 4
F32 = jnp.float32
BF16 = jnp.bfloat16


def split(value):
    high = value.astype(BF16)
    return high, (value - high.astype(F32)).astype(BF16)


def dot(a, b):
    return jnp.dot(a, b, preferred_element_type=F32)


def dot3(a, weights):
    high, low = split(a)
    return dot(jnp.concatenate([high, high, low], axis=1), weights)


def deep(value):
    high, low = split(value)
    return jnp.concatenate([high, low, high], axis=0)


def shift_plane(value, by, swapped):
    pairs = []
    for r in range(N_ROW):
        for x in range(SIDE):
            for z in range(SIDE):
                along_z = (r % 2 == 1) != swapped
                to = (x, (z + by) % SIDE) if along_z else ((x + by) % SIDE, z)
                pairs.append((r * N_COL + x * SIDE + z, r * N_COL + to[0] * SIDE + to[1]))
    return lax.ppermute(value, ("row", "col"), pairs)


def shift_line(value, by):
    return shift_plane(value, by, False)


def shift_cross(value, by):
    return shift_plane(value, by, True)


def send_far(value):
    pairs = []
    for r in range(N_ROW):
        for root in range(2):
            to = root + 2 if r % 2 else 2 * SIDE + root
            pairs.append((r * N_COL + root, r * N_COL + to))
    return lax.ppermute(value, ("row", "col"), pairs)


def shift_y(value, by):
    pairs = [(y * 2 + k, (y + by) % SIDE * 2 + k) for y in range(SIDE) for k in range(2)]
    return lax.ppermute(value, "row", pairs)


def swap_core(value):
    return lax.ppermute(value, "row", [(r, r ^ 1) for r in range(N_ROW)])


def to_columns(value):
    pairs = []
    for r in range(N_ROW):
        for x in range(SIDE):
            for z in range(SIDE):
                line, cross = (z, x) if r % 2 else (x, z)
                panel, odd = cross // 2, cross % 2
                quarter = (line - panel * (r % 2)) % SIDE
                target = (quarter * 2 + panel) * N_COL + r + N_ROW * odd
                pairs.append((r * N_COL + x * SIDE + z, target))
    return lax.ppermute(value, ("row", "col"), pairs)


def relay_y(near, back, core):
    pairs = [(r, (r + (2 if r % 2 == 0 else -2)) % N_ROW) for r in range(N_ROW)]
    return lax.ppermute(jnp.where(core == 0, near, back), "row", pairs)


def choose(place, own, near, far, back):
    return jnp.where(place == 0, own, jnp.where(place == 1, near, jnp.where(place == 2, far, back)))


def join(one, two):
    return jnp.concatenate([one, two], axis=0)


PAIR = 2 * NB


def gather_all(raw, row, col):
    barrier = lax.optimization_barrier
    x, z, core = col // SIDE, col % SIDE, row % 2
    line, cross = jnp.where(core == 0, x, z), jnp.where(core == 0, z, x)

    near, back, far = barrier((
        shift_line(raw[PAIR : 2 * PAIR], 1),
        shift_line(raw[3 * PAIR :], -1),
        send_far(raw[2 * PAIR : 3 * PAIR]),
    ))
    places = raw[:PAIR], near, far, back
    own1 = choose(line, *places)
    own2 = choose((line + SIDE - 1) % SIDE, *places)

    near1, back2 = shift_cross(own1, 1), shift_cross(own2, -1)
    back1, near2 = shift_cross(own1, -1), shift_cross(own2, 1)
    far1, far2 = shift_cross(near1, 1), shift_cross(back2, -1)
    near1, far1, back1, near2, far2, back2 = barrier((near1, far1, back1, near2, far2, back2))
    after = (cross + SIDE - 1) % SIDE
    block1 = choose(cross, own1, near1, far1, back1)
    block2 = jnp.where(
        core == 0,
        choose(after, own1, near1, far1, back1),
        choose(cross, own2, near2, far2, back2),
    )
    half = jnp.where(cross < 2, block1, block2)
    tile = lax.dynamic_slice(half, (cross % 2 * NB, 0), (NB, NB))
    block1, block2, tile, pivot = barrier((block1, block2, tile, block1[:NB]))

    corner = [(N_COL + SIDE * a, N_COL + SIDE * a + 2) for a in range(SIDE)]
    near1, back2, back1, near2, own, pivot_far = barrier((
        shift_line(block1, 1),
        shift_line(block2, -1),
        shift_line(block1, -1),
        shift_line(block2, 1),
        to_columns(tile),
        lax.ppermute(pivot, ("row", "col"), corner),
    ))
    pivot = choose(z, pivot, near1[:NB], pivot_far, back1[:NB])
    near1, back2, own, pivot = barrier((near1, back2, own, pivot))
    far1, far2, up, down, own_other, pivot_up, pivot_down, pivot_far, pivot_swap = barrier((
        shift_line(near1, 1),
        shift_line(back2, -1),
        shift_y(own, 1),
        shift_y(own, -1),
        swap_core(own),
        lax.ppermute(pivot, "row", [(1, 3)]),
        lax.ppermute(pivot, "row", [(1, 7)]),
        lax.ppermute(pivot, "row", [(1, 5)]),
        lax.ppermute(pivot, "row", [(1, 0)]),
    ))
    panel1 = [block1, near1, far1, back1]
    panel2 = [block2, near2, far2, back2]
    odd = pivot_up + pivot_down + pivot_far
    last, up_other, down_other, even = barrier((
        relay_y(up, down, core),
        swap_core(up),
        swap_core(down),
        lax.ppermute(odd, "row", [(3, 2), (5, 4), (7, 6)]),
    ))
    cols = [own, up, last, down, own_other, up_other, swap_core(last), down_other]
    pivots = [pivot_swap, pivot, even, odd]
    return panel1, panel2, cols, pivots


VMEM = pl.BlockSpec(memory_space=pltpu.VMEM)
SMEM = pl.BlockSpec(memory_space=pltpu.SMEM)
ANY = pl.BlockSpec(memory_space=pl.ANY)
ROWS = TR * NB
COLS = TC * NB


def rows_at(index, size):
    return pl.ds(pl.multiple_of(index * size, size), size)


def plane_copies(refs, raw, sems, panel):
    c, core = lax.axis_index("col"), lax.rem(lax.axis_index("row"), 2)
    x, z = lax.div(c, SIDE), lax.rem(c, SIDE)
    line = jnp.where(core == 0, x, z + SIDE - panel)
    copies = []
    for n in range(SIDE):
        place = lax.rem(line + SIDE - n, SIDE)
        copies.append(pltpu.make_async_copy(refs[n], raw.at[rows_at(place, PAIR), :], sems.at[n]))
    return copies


def column_copies(tiles, raw, sems):
    r = lax.axis_index("row")
    y, core = lax.div(r, 2), lax.rem(r, 2)
    copies = []
    for n in range(N_ROW):
        k = lax.rem(y + SIDE - n % SIDE, SIDE) * 2 + lax.rem(core + n // SIDE, 2)
        target = raw.at[lax.rem(k, 2), rows_at(lax.div(k, 2), NB), :]
        copies.append(pltpu.make_async_copy(tiles[n], target, sems.at[n]))
    return copies


def first_kernel(*refs):
    pieces, inv_in, row_high, row_low, raw, inv, sems = refs[:SIDE], *refs[SIDE:]
    copies = plane_copies(pieces, raw, sems, 0)
    weights_copy = pltpu.make_async_copy(inv_in.at[0], inv, sems.at[SIDE])
    for copy in [weights_copy, *copies]:
        copy.start()
    weights_copy.wait()
    weights = deep(inv[...].T)
    for copy in copies:
        copy.wait()

    def row(p, carry):
        solved = dot3(raw[rows_at(p, PAIR), :], weights).reshape(2, NB, NB)
        high, low = split(solved)
        row_high[pl.ds(2 * p, 2)] = high
        row_low[pl.ds(2 * p, 2)] = low
        return carry

    lax.fori_loop(0, TR // 2, row, 0)


def solve_first(pieces, inv):
    return pl.pallas_call(
        first_kernel,
        out_shape=[jax.ShapeDtypeStruct((TR, NB, NB), BF16)] * 2,
        in_specs=[ANY] * (SIDE + 1),
        out_specs=[VMEM] * 2,
        scratch_shapes=[
            pltpu.VMEM((ROWS, NB), F32),
            pltpu.VMEM((NB, NB), F32),
            pltpu.SemaphoreType.DMA((SIDE + 1,)),
        ],
        compiler_params=pltpu.CompilerParams(vmem_limit_bytes=16 * 1024 * 1024),
        cost_estimate=pl.CostEstimate(flops=8 * 3 * 2 * NB**3, bytes_accessed=4 * 2**20, transcendentals=0),
        name="solve_first",
    )(*pieces, inv)


STEP = 2
LINES = NB * TC * 2


def last_kernel(*refs):
    pieces, cols = refs[:SIDE], refs[SIDE : SIDE + N_ROW]
    pivots, refs = refs[SIDE + N_ROW : SIDE + N_ROW + 4], refs[SIDE + N_ROW + 4 :]
    matrix, inv_in, high_in, low_in, band, out, panel, *refs = refs
    tiles, raw, raw_cols, row_high1, row_low1, row_high2, row_low2, col_high, col_low, *refs = refs
    inv, pivot, sems, col_sems, in_sems, out_sems, panel_sems, small_sems = refs
    r, c = lax.axis_index("row"), lax.axis_index("col")
    copies = plane_copies(pieces, raw, sems, 1)
    col_copies = column_copies(cols, raw_cols, col_sems)
    loads = [pltpu.make_async_copy(matrix.at[p], tiles.at[p], in_sems.at[p]) for p in range(TR)]
    small = [(inv_in, inv), (pivots[0], pivot), (high_in, row_high1), (low_in, row_low1)]
    small = [pltpu.make_async_copy(a, b, small_sems.at[n]) for n, (a, b) in enumerate(small)]
    small[0].start()
    for n, rows in enumerate(((0,), (1,), (2, 4, 6), (3, 5, 7))):

        @pl.when(functools.reduce(jnp.logical_or, [r == row for row in rows]))
        def _():
            pltpu.make_async_copy(pivots[n], pivot, small_sems.at[1]).start()

    for copy in col_copies + small[2:] + copies + loads:
        copy.start()
    small[0].wait()
    weights0 = deep(inv[0].T)
    weights1 = deep(inv[1].T)
    small[1].wait()
    one_high, one_low = split(dot3(pivot[...], weights0).T)
    rest_weights = join(one_low, one_high)

    def used(high, low, code):
        full = dot(high, one_high)
        rest = dot(jnp.concatenate([high, low], axis=1), rest_weights)
        return jnp.where(code == 2, 0.0, full + jnp.where(code == 0, rest, 0.0))

    def column(q, carry):
        first = dot3(raw_cols[0, rows_at(q, NB), :], weights0)
        col_high[q, :NB, :], col_low[q, :NB, :] = split(first.T)
        high, low = split(first)
        tile = raw_cols[1, rows_at(q, NB), :] - used(high, low, band[q * N_COL + c, 1])
        col_high[q, NB:, :], col_low[q, NB:, :] = split(dot3(tile, weights1).T)
        return carry

    panels = [pltpu.make_async_copy(raw.at[pl.ds(p * NB, NB), :], panel.at[p], panel_sems.at[p]) for p in range(TR)]

    def solve(p):
        at = pl.ds(p * NB, NB)
        tile = raw[at, :] - used(row_high1[p], row_low1[p], band[p * N_ROW + r, 1])
        solved = dot3(tile, weights1)
        raw[at, :] = solved
        row_high2[p], row_low2[p] = split(solved)

    for copy in col_copies:
        copy.wait()
    lax.fori_loop(0, TC, column, 0, unroll=2)
    for copy in small[2:] + copies:
        copy.wait()

    size = STEP * NB

    def multiply(step, q):
        at = pl.ds(step * STEP, STEP)
        high = jnp.concatenate([row_high1[at].reshape(size, NB), row_high2[at].reshape(size, NB)], axis=1)
        low = jnp.concatenate([row_low1[at].reshape(size, NB), row_low2[at].reshape(size, NB)], axis=1)
        full = dot(high, col_high[q])
        rest = dot(jnp.concatenate([high, low], axis=1), join(col_low[q], col_high[q]))
        for p in range(STEP):
            code = band[(step * STEP + p) * N_ROW + r, q * N_COL + c]
            at = slice(p * NB, (p + 1) * NB)
            total = jnp.where(code == 2, 0.0, full[at] + jnp.where(code == 0, rest[at], 0.0))
            for b in range(2):
                lines = pl.ds(b * TC + q, NB, stride=2 * TC)
                tiles[step * STEP + p, lines, :] -= total[:, b * HALF : (b + 1) * HALF]

    steps = TR // STEP
    stores = [pltpu.make_async_copy(tiles.at[p], out.at[p], out_sems.at[p]) for p in range(TR)]
    for step in range(-1, steps):
        if step >= 0:
            for p in range(STEP):
                loads[step * STEP + p].wait()
        for q in range(TC):
            if step + 1 < steps and q < STEP:
                solve((step + 1) * STEP + q)
            if step >= 0:
                multiply(step, q)
        if step + 1 < steps:
            for p in range(STEP):
                panels[(step + 1) * STEP + p].start()
        if step >= 0:
            for p in range(STEP):
                stores[step * STEP + p].start()
    for copy in stores + panels:
        copy.wait()


def finish(pieces, cols, pivots, matrix, inv, first, band):
    view = matrix.reshape(TR, NB, TC, 2, HALF).transpose(0, 1, 3, 2, 4).reshape(TR, LINES, HALF)
    out, panel = pl.pallas_call(
        last_kernel,
        out_shape=(
            jax.ShapeDtypeStruct((TR, LINES, HALF), F32),
            jax.ShapeDtypeStruct((TR, NB, NB), F32),
        ),
        in_specs=[ANY] * (SIDE + N_ROW + 4 + 4) + [SMEM],
        out_specs=[ANY] * 2,
        scratch_shapes=[
            pltpu.VMEM((TR, LINES, HALF), F32),
            pltpu.VMEM((ROWS, NB), F32),
            pltpu.VMEM((2, COLS, NB), F32),
            pltpu.VMEM((TR, NB, NB), BF16),
            pltpu.VMEM((TR, NB, NB), BF16),
            pltpu.VMEM((TR, NB, NB), BF16),
            pltpu.VMEM((TR, NB, NB), BF16),
            pltpu.VMEM((TC, PAIR, NB), BF16),
            pltpu.VMEM((TC, PAIR, NB), BF16),
            pltpu.VMEM((2, NB, NB), F32),
            pltpu.VMEM((NB, NB), F32),
            pltpu.SemaphoreType.DMA((SIDE,)),
            pltpu.SemaphoreType.DMA((N_ROW,)),
            pltpu.SemaphoreType.DMA((TR,)),
            pltpu.SemaphoreType.DMA((TR,)),
            pltpu.SemaphoreType.DMA((TR,)),
            pltpu.SemaphoreType.DMA((4,)),
        ],
        compiler_params=pltpu.CompilerParams(vmem_limit_bytes=40 * 1024 * 1024),
        cost_estimate=pl.CostEstimate(flops=200 * 2 * NB**3, bytes_accessed=20 * 2**20, transcendentals=0),
        name="solve_and_update",
    )(*pieces, *cols, *pivots, view, inv, *first, band)
    return out.reshape(TR, NB, 2, TC, HALF).transpose(0, 1, 3, 2, 4).reshape(TR, NB, TC, NB), panel


def body(matrix, diag_inverses, band):
    raw = lax.optimization_barrier(matrix[:, :, 0, :].reshape(ROWS, NB))
    panel1, panel2, cols, pivots = gather_all(raw, lax.axis_index("row"), lax.axis_index("col"))
    first = solve_first(panel1, diag_inverses)
    return finish(panel2, cols, pivots, matrix, diag_inverses, first, band)


def solution(mesh):
    in_specs = (P(None, "row", None, "col"), P(), P())
    out_specs = (P(None, "row", None, "col"), P(None, "row", None))
    return jax.shard_map(body, mesh=mesh, in_specs=in_specs, out_specs=out_specs, check_vma=False)
```

```python
import jax
import jax.numpy as jnp
from jax import lax
from jax.experimental import pallas as pl
from jax.experimental.pallas import tpu as pltpu
from jax.sharding import PartitionSpec as P

NB = 256
HALF = 128
TR = 8
TC = 4
N_ROW = 8
N_COL = 16
SIDE = 4
F32 = jnp.float32
BF16 = jnp.bfloat16


def split(value):
    high = value.astype(BF16)
    return high, (value - high.astype(F32)).astype(BF16)


def dot(a, b):
    return jnp.dot(a, b, preferred_element_type=F32)


def dot3(a, weights):
    high, low = split(a)
    return dot(jnp.concatenate([high, high, low], axis=1), weights)


def deep(value):
    high, low = split(value)
    return jnp.concatenate([high, low, high], axis=0)


def shift_plane(value, by, swapped):
    pairs = []
    for r in range(N_ROW):
        for x in range(SIDE):
            for z in range(SIDE):
                along_z = (r % 2 == 1) != swapped
                to = (x, (z + by) % SIDE) if along_z else ((x + by) % SIDE, z)
                pairs.append((r * N_COL + x * SIDE + z, r * N_COL + to[0] * SIDE + to[1]))
    return lax.ppermute(value, ("row", "col"), pairs)


def shift_line(value, by):
    return shift_plane(value, by, False)


def shift_cross(value, by):
    return shift_plane(value, by, True)


def send_far(value):
    pairs = []
    for r in range(N_ROW):
        for root in range(2):
            to = root + 2 if r % 2 else 2 * SIDE + root
            pairs.append((r * N_COL + root, r * N_COL + to))
    return lax.ppermute(value, ("row", "col"), pairs)


def shift_y(value, by):
    pairs = [(y * 2 + k, (y + by) % SIDE * 2 + k) for y in range(SIDE) for k in range(2)]
    return lax.ppermute(value, "row", pairs)


def swap_core(value):
    return lax.ppermute(value, "row", [(r, r ^ 1) for r in range(N_ROW)])


def tile_choice(r, line, cross):
    turned = (cross - r // 4) % SIDE
    return (turned // 2, turned % 2) if r % 2 else (cross % 2, cross // 2)


def to_columns(value):
    pairs = []
    for r in range(N_ROW):
        for x in range(SIDE):
            for z in range(SIDE):
                line, cross = (z, x) if r % 2 else (x, z)
                odd, panel = tile_choice(r, line, cross)
                quarter = (line - panel * (r % 2)) % SIDE
                target = ((quarter + r // 2) % SIDE * 2 + panel) * N_COL + r + N_ROW * odd
                pairs.append((r * N_COL + x * SIDE + z, target))
    return lax.ppermute(value, ("row", "col"), pairs)


def relay_y(near, back, core):
    pairs = [(r, (r + (2 if r % 2 == 0 else -2)) % N_ROW) for r in range(N_ROW)]
    return lax.ppermute(jnp.where(core == 0, near, back), "row", pairs)


def choose(place, own, near, far, back):
    return jnp.where(place == 0, own, jnp.where(place == 1, near, jnp.where(place == 2, far, back)))


def join(one, two):
    return jnp.concatenate([one, two], axis=0)


PAIR = 2 * NB


def gather_all(raw, row, col):
    barrier = lax.optimization_barrier
    x, z, core = col // SIDE, col % SIDE, row % 2
    line, cross = jnp.where(core == 0, x, z), jnp.where(core == 0, z, x)

    near, back, far = barrier((
        shift_line(raw[PAIR : 2 * PAIR], 1),
        shift_line(raw[3 * PAIR :], -1),
        send_far(raw[2 * PAIR : 3 * PAIR]),
    ))
    places = raw[:PAIR], near, far, back
    own1 = choose(line, *places)
    own2 = choose((line + SIDE - 1) % SIDE, *places)

    near1, back2 = shift_cross(own1, 1), shift_cross(own2, -1)
    back1, near2 = shift_cross(own1, -1), shift_cross(own2, 1)
    far1, far2 = shift_cross(near1, 1), shift_cross(back2, -1)
    near1, far1, back1, near2, far2, back2 = barrier((near1, far1, back1, near2, far2, back2))
    after = (cross + SIDE - 1) % SIDE
    block1 = choose(cross, own1, near1, far1, back1)
    block2 = jnp.where(
        core == 0,
        choose(after, own1, near1, far1, back1),
        choose(cross, own2, near2, far2, back2),
    )
    turned = (cross - row // 4) % SIDE
    odd = jnp.where(core == 0, cross % 2, turned // 2)
    panel = jnp.where(core == 0, cross // 2, turned % 2)
    tile = lax.dynamic_slice(jnp.where(panel == 0, block1, block2), (odd * NB, 0), (NB, NB))
    block1, block2, tile, pivot = barrier((block1, block2, tile, block1[:NB]))

    corner = [(N_COL + SIDE * a, N_COL + SIDE * a + 2) for a in range(SIDE)]
    near1, back2, back1, near2, own, pivot_far = barrier((
        shift_line(block1, 1),
        shift_line(block2, -1),
        shift_line(block1, -1),
        shift_line(block2, 1),
        to_columns(tile),
        lax.ppermute(pivot, ("row", "col"), corner),
    ))
    pivot = choose(z, pivot, near1[:NB], pivot_far, back1[:NB])
    near1, back2, own, pivot = barrier((near1, back2, own, pivot))
    far1, far2, up, down, own_other, *odd = barrier((
        shift_line(near1, 1),
        shift_line(back2, -1),
        shift_y(own, 1),
        shift_y(own, -1),
        swap_core(own),
        *[lax.ppermute(pivot, "row", [(1, to)]) for to in (3, 5, 7)],
    ))
    panel1 = [block1, near1, far1, back1]
    panel2 = [block2, near2, far2, back2]
    odd = jnp.where(row == 1, pivot, sum(odd))
    last, up_other, down_other, even = barrier((
        relay_y(up, down, core),
        swap_core(up),
        swap_core(down),
        lax.ppermute(odd, "row", [(1, 0), (3, 2), (5, 4), (7, 6)]),
    ))
    cols = [own, up, last, down, own_other, up_other, swap_core(last), down_other]
    pivots = [even, odd]
    return panel1, panel2, cols, pivots


VMEM = pl.BlockSpec(memory_space=pltpu.VMEM)
SMEM = pl.BlockSpec(memory_space=pltpu.SMEM)
ANY = pl.BlockSpec(memory_space=pl.ANY)
ROWS = TR * NB
COLS = TC * NB


def rows_at(index, size):
    return pl.ds(pl.multiple_of(index * size, size), size)


def plane_copies(refs, raw, sems, panel):
    c, core = lax.axis_index("col"), lax.rem(lax.axis_index("row"), 2)
    x, z = lax.div(c, SIDE), lax.rem(c, SIDE)
    line = jnp.where(core == 0, x, z + SIDE - panel)
    copies = []
    for n in range(SIDE):
        place = lax.rem(line + SIDE - n, SIDE)
        copies.append(pltpu.make_async_copy(refs[n], raw.at[rows_at(place, PAIR), :], sems.at[n]))
    return copies


def column_copies(tiles, raw, sems):
    r = lax.axis_index("row")
    y, core = lax.div(r, 2), lax.rem(r, 2)
    copies = []
    for n in range(N_ROW):
        k = lax.rem(y + SIDE - n % SIDE, SIDE) * 2 + lax.rem(core + n // SIDE, 2)
        source_y = lax.div(lax.rem(lax.axis_index("col"), N_ROW), 2)
        tile = lax.rem(lax.div(k, 2) + SIDE - source_y, SIDE)
        target = raw.at[lax.rem(k, 2), rows_at(tile, NB), :]
        copies.append(pltpu.make_async_copy(tiles[n], target, sems.at[n]))
    return copies


def first_kernel(*refs):
    pieces, inv_in, row_high, row_low, raw, inv, sems = refs[:SIDE], *refs[SIDE:]
    copies = plane_copies(pieces, raw, sems, 0)
    weights_copy = pltpu.make_async_copy(inv_in.at[0], inv, sems.at[SIDE])
    for copy in [weights_copy, *copies]:
        copy.start()
    weights_copy.wait()
    weights = deep(inv[...].T)
    for copy in copies:
        copy.wait()

    def row(p, carry):
        solved = dot3(raw[rows_at(p, PAIR), :], weights).reshape(2, NB, NB)
        high, low = split(solved)
        row_high[pl.ds(2 * p, 2)] = high
        row_low[pl.ds(2 * p, 2)] = low
        return carry

    lax.fori_loop(0, TR // 2, row, 0)


def solve_first(pieces, inv):
    return pl.pallas_call(
        first_kernel,
        out_shape=[jax.ShapeDtypeStruct((TR, NB, NB), BF16)] * 2,
        in_specs=[ANY] * (SIDE + 1),
        out_specs=[VMEM] * 2,
        scratch_shapes=[
            pltpu.VMEM((ROWS, NB), F32),
            pltpu.VMEM((NB, NB), F32),
            pltpu.SemaphoreType.DMA((SIDE + 1,)),
        ],
        compiler_params=pltpu.CompilerParams(vmem_limit_bytes=16 * 1024 * 1024),
        cost_estimate=pl.CostEstimate(flops=8 * 3 * 2 * NB**3, bytes_accessed=4 * 2**20, transcendentals=0),
        name="solve_first",
    )(*pieces, inv)


STEP = 2
LINES = NB * TC * 2
PART = 32


def last_kernel(*refs):
    pieces, cols = refs[:SIDE], refs[SIDE : SIDE + N_ROW]
    pivots, refs = refs[SIDE + N_ROW : SIDE + N_ROW + 2], refs[SIDE + N_ROW + 2 :]
    matrix, inv_in, high_in, low_in, band, out, panel, *refs = refs
    tiles, raw, raw_cols, row_high1, row_low1, row_high2, row_low2, col_high, col_low, even, odd, *refs = refs
    inv, pivot, sems, col_sems, in_sems, out_sems, panel_sems, small_sems = refs
    r, c = lax.axis_index("row"), lax.axis_index("col")
    copies = plane_copies(pieces, raw, sems, 1)
    col_copies = column_copies(cols, raw_cols, col_sems)
    loads = [pltpu.make_async_copy(matrix.at[p], tiles.at[p], in_sems.at[p]) for p in range(TR)]
    small = [(inv_in, inv), (pivots[0], pivot), (high_in, row_high1), (low_in, row_low1)]
    small = [pltpu.make_async_copy(a, b, small_sems.at[n]) for n, (a, b) in enumerate(small)]
    small[0].start()
    for n in range(2):

        @pl.when(lax.rem(r, 2) == n)
        def _():
            pltpu.make_async_copy(pivots[n], pivot, small_sems.at[1]).start()

    for copy in small[2:] + copies + col_copies + loads:
        copy.start()
    small[0].wait()
    weights0 = deep(inv[0].T)
    weights1 = deep(inv[1].T)
    small[1].wait()
    one_high, one_low = split(dot3(pivot[...], weights0).T)
    rest_weights = join(one_low, one_high)

    def used(high, low, code):
        full = dot(high, one_high)
        rest = dot(jnp.concatenate([high, low], axis=1), rest_weights)
        return jnp.where(code == 2, 0.0, full + jnp.where(code == 0, rest, 0.0))

    def column(q, carry):
        first = dot3(raw_cols[0, rows_at(q, NB), :], weights0)
        col_high[q, :NB, :], col_low[q, :NB, :] = split(first.T)
        high, low = split(first)
        tile = raw_cols[1, rows_at(q, NB), :] - used(high, low, band[q * N_COL + c, 1])
        col_high[q, NB:, :], col_low[q, NB:, :] = split(dot3(tile, weights1).T)
        return carry

    panels = [pltpu.make_async_copy(raw.at[pl.ds(p * NB, NB), :], panel.at[p], panel_sems.at[p]) for p in range(TR)]

    def solve(p):
        at = pl.ds(p * NB, NB)
        tile = raw[at, :] - used(row_high1[p], row_low1[p], band[p * N_ROW + r, 1])
        solved = dot3(tile, weights1)
        raw[at, :] = solved
        row_high2[p], row_low2[p] = split(solved)

    for copy in col_copies:
        copy.wait()
    lax.fori_loop(0, TC, column, 0, unroll=2)
    for copy in small[2:] + copies:
        copy.wait()

    size = STEP * NB

    def multiply(step, q, product):
        at = pl.ds(step * STEP, STEP)
        high = jnp.concatenate([row_high1[at].reshape(size, NB), row_high2[at].reshape(size, NB)], axis=1)
        low = jnp.concatenate([row_low1[at].reshape(size, NB), row_low2[at].reshape(size, NB)], axis=1)
        full = dot(high, col_high[q])
        rest = dot(jnp.concatenate([high, low], axis=1), join(col_low[q], col_high[q]))
        for p in range(STEP):
            code = band[(step * STEP + p) * N_ROW + r, q * N_COL + c]
            at = slice(p * NB, (p + 1) * NB)
            total = jnp.where(code == 2, 0.0, full[at] + jnp.where(code == 0, rest[at], 0.0))
            for b in range(2):
                product[b * TC + q, at, :] = total[:, b * HALF : (b + 1) * HALF]

    def subtract(step, share, product):
        for a in range(share * size // TC, (share + 1) * size // TC, PART):
            turned = product[:, a : a + PART, :].transpose(1, 0, 2).reshape(PART * 2 * TC, HALF)
            at = pl.ds(a % NB * 2 * TC, PART * 2 * TC)
            tiles[step * STEP + a // NB, at, :] -= turned

    steps = TR // STEP
    stores = [pltpu.make_async_copy(tiles.at[p], out.at[p], out_sems.at[p]) for p in range(TR)]
    for step in range(-1, steps + 1):
        product, before = (even, odd) if step % 2 == 0 else (odd, even)
        if step > 0:
            for p in range(STEP):
                loads[(step - 1) * STEP + p].wait()
        for q in range(TC):
            if step + 1 < steps and q < STEP:
                solve((step + 1) * STEP + q)
            if 0 <= step < steps:
                multiply(step, q, product)
            if step > 0:
                subtract(step - 1, q, before)
        if step + 1 < steps:
            for p in range(STEP):
                panels[(step + 1) * STEP + p].start()
        if step > 0:
            for p in range(STEP):
                stores[(step - 1) * STEP + p].start()
    for copy in stores + panels:
        copy.wait()


def finish(pieces, cols, pivots, matrix, inv, first, band):
    view = matrix.reshape(TR, NB, TC, 2, HALF).transpose(0, 1, 3, 2, 4).reshape(TR, LINES, HALF)
    out, panel = pl.pallas_call(
        last_kernel,
        out_shape=(
            jax.ShapeDtypeStruct((TR, LINES, HALF), F32),
            jax.ShapeDtypeStruct((TR, NB, NB), F32),
        ),
        in_specs=[ANY] * (SIDE + N_ROW + 2 + 4) + [SMEM],
        out_specs=[ANY] * 2,
        scratch_shapes=[
            pltpu.VMEM((TR, LINES, HALF), F32),
            pltpu.VMEM((ROWS, NB), F32),
            pltpu.VMEM((2, COLS, NB), F32),
            pltpu.VMEM((TR, NB, NB), BF16),
            pltpu.VMEM((TR, NB, NB), BF16),
            pltpu.VMEM((TR, NB, NB), BF16),
            pltpu.VMEM((TR, NB, NB), BF16),
            pltpu.VMEM((TC, PAIR, NB), BF16),
            pltpu.VMEM((TC, PAIR, NB), BF16),
            pltpu.VMEM((2 * TC, STEP * NB, HALF), F32),
            pltpu.VMEM((2 * TC, STEP * NB, HALF), F32),
            pltpu.VMEM((2, NB, NB), F32),
            pltpu.VMEM((NB, NB), F32),
            pltpu.SemaphoreType.DMA((SIDE,)),
            pltpu.SemaphoreType.DMA((N_ROW,)),
            pltpu.SemaphoreType.DMA((TR,)),
            pltpu.SemaphoreType.DMA((TR,)),
            pltpu.SemaphoreType.DMA((TR,)),
            pltpu.SemaphoreType.DMA((4,)),
        ],
        compiler_params=pltpu.CompilerParams(vmem_limit_bytes=40 * 1024 * 1024),
        cost_estimate=pl.CostEstimate(flops=200 * 2 * NB**3, bytes_accessed=20 * 2**20, transcendentals=0),
        name="solve_and_update",
    )(*pieces, *cols, *pivots, view, inv, *first, band)
    return out.reshape(TR, NB, 2, TC, HALF).transpose(0, 1, 3, 2, 4).reshape(TR, NB, TC, NB), panel


def body(matrix, diag_inverses, band):
    raw = lax.optimization_barrier(matrix[:, :, 0, :].reshape(ROWS, NB))
    panel1, panel2, cols, pivots = gather_all(raw, lax.axis_index("row"), lax.axis_index("col"))
    first = solve_first(panel1, diag_inverses)
    return finish(panel2, cols, pivots, matrix, diag_inverses, first, band)


def solution(mesh):
    in_specs = (P(None, "row", None, "col"), P(), P())
    out_specs = (P(None, "row", None, "col"), P(None, "row", None))
    return jax.shard_map(body, mesh=mesh, in_specs=in_specs, out_specs=out_specs, check_vma=False)
```

```python
import jax
import jax.numpy as jnp
from jax import lax
from jax.experimental import pallas as pl
from jax.experimental.pallas import tpu as pltpu
from jax.sharding import PartitionSpec as P

NB = 256
HALF = 128
TR = 8
TC = 4
N_ROW = 8
N_COL = 16
SIDE = 4
F32 = jnp.float32
BF16 = jnp.bfloat16


def split(value):
    high = value.astype(BF16)
    return high, (value - high.astype(F32)).astype(BF16)


def dot(a, b):
    return jnp.dot(a, b, preferred_element_type=F32)


def dot3(a, weights):
    high, low = split(a)
    return dot(jnp.concatenate([high, high, low], axis=1), weights)


def deep(value):
    high, low = split(value)
    return jnp.concatenate([high, low, high], axis=0)


def shift_plane(value, by, swapped):
    pairs = []
    for r in range(N_ROW):
        for x in range(SIDE):
            for z in range(SIDE):
                along_z = (r % 2 == 1) != swapped
                to = (x, (z + by) % SIDE) if along_z else ((x + by) % SIDE, z)
                pairs.append((r * N_COL + x * SIDE + z, r * N_COL + to[0] * SIDE + to[1]))
    return lax.ppermute(value, ("row", "col"), pairs)


def shift_line(value, by):
    return shift_plane(value, by, False)


def shift_cross(value, by):
    return shift_plane(value, by, True)


def send_far(value):
    pairs = []
    for r in range(N_ROW):
        for root in range(2):
            to = root + 2 if r % 2 else 2 * SIDE + root
            pairs.append((r * N_COL + root, r * N_COL + to))
    return lax.ppermute(value, ("row", "col"), pairs)


def shift_y(value, by):
    pairs = [(y * 2 + k, (y + by) % SIDE * 2 + k) for y in range(SIDE) for k in range(2)]
    return lax.ppermute(value, "row", pairs)


def swap_core(value):
    return lax.ppermute(value, "row", [(r, r ^ 1) for r in range(N_ROW)])


def tile_choice(r, line, cross):
    turned = (cross - r // 4) % SIDE
    return (turned // 2, turned % 2) if r % 2 else (cross % 2, cross // 2)


def to_columns(value):
    pairs = []
    for r in range(N_ROW):
        for x in range(SIDE):
            for z in range(SIDE):
                line, cross = (z, x) if r % 2 else (x, z)
                odd, panel = tile_choice(r, line, cross)
                quarter = (line - panel * (r % 2)) % SIDE
                target = ((quarter + r // 2) % SIDE * 2 + panel) * N_COL + r + N_ROW * odd
                pairs.append((r * N_COL + x * SIDE + z, target))
    return lax.ppermute(value, ("row", "col"), pairs)


def relay_y(near, back, core):
    pairs = [(r, (r + (2 if r % 2 == 0 else -2)) % N_ROW) for r in range(N_ROW)]
    return lax.ppermute(jnp.where(core == 0, near, back), "row", pairs)


def choose(place, own, near, far, back):
    return jnp.where(place == 0, own, jnp.where(place == 1, near, jnp.where(place == 2, far, back)))


def join(one, two):
    return jnp.concatenate([one, two], axis=0)


PAIR = 2 * NB


def gather_all(raw, row, col):
    barrier = lax.optimization_barrier
    x, z, core = col // SIDE, col % SIDE, row % 2
    line, cross = jnp.where(core == 0, x, z), jnp.where(core == 0, z, x)

    near, back, far = barrier((
        shift_line(raw[PAIR : 2 * PAIR], 1),
        shift_line(raw[3 * PAIR :], -1),
        send_far(raw[2 * PAIR : 3 * PAIR]),
    ))
    places = raw[:PAIR], near, far, back
    own1 = choose(line, *places)
    own2 = choose((line + SIDE - 1) % SIDE, *places)

    near1, back2 = shift_cross(own1, 1), shift_cross(own2, -1)
    back1, near2 = shift_cross(own1, -1), shift_cross(own2, 1)
    far1, far2 = shift_cross(near1, 1), shift_cross(back2, -1)
    near1, far1, back1, near2, far2, back2 = barrier((near1, far1, back1, near2, far2, back2))
    after = (cross + SIDE - 1) % SIDE
    block1 = choose(cross, own1, near1, far1, back1)
    block2 = jnp.where(
        core == 0,
        choose(after, own1, near1, far1, back1),
        choose(cross, own2, near2, far2, back2),
    )
    turned = (cross - row // 4) % SIDE
    odd = jnp.where(core == 0, cross % 2, turned // 2)
    panel = jnp.where(core == 0, cross // 2, turned % 2)
    tile = lax.dynamic_slice(jnp.where(panel == 0, block1, block2), (odd * NB, 0), (NB, NB))
    block1, block2, tile, pivot = barrier((block1, block2, tile, block1[:NB]))

    corner = [(N_COL + SIDE * a, N_COL + SIDE * a + 2) for a in range(SIDE)]
    near1, back2, back1, near2, own, pivot_far = barrier((
        shift_line(block1, 1),
        shift_line(block2, -1),
        shift_line(block1, -1),
        shift_line(block2, 1),
        to_columns(tile),
        lax.ppermute(pivot, ("row", "col"), corner),
    ))
    pivot = choose(z, pivot, near1[:NB], pivot_far, back1[:NB])
    near1, back2, own, pivot = barrier((near1, back2, own, pivot))
    far1, far2, up, down, own_other, *odd = barrier((
        shift_line(near1, 1),
        shift_line(back2, -1),
        shift_y(own, 1),
        shift_y(own, -1),
        swap_core(own),
        *[lax.ppermute(pivot, "row", [(1, to)]) for to in (3, 5, 7)],
    ))
    panel1 = [block1, near1, far1, back1]
    panel2 = [block2, near2, far2, back2]
    odd = jnp.where(row == 1, pivot, sum(odd))
    last, up_other, down_other, even = barrier((
        relay_y(up, down, core),
        swap_core(up),
        swap_core(down),
        lax.ppermute(odd, "row", [(1, 0), (3, 2), (5, 4), (7, 6)]),
    ))
    cols = (own, up, last, down, own_other, up_other, down_other)
    pivots = [even, odd]
    return panel1, panel2, cols, pivots


VMEM = pl.BlockSpec(memory_space=pltpu.VMEM)
SMEM = pl.BlockSpec(memory_space=pltpu.SMEM)
ANY = pl.BlockSpec(memory_space=pl.ANY)
ROWS = TR * NB
COLS = TC * NB


def rows_at(index, size):
    return pl.ds(pl.multiple_of(index * size, size), size)


def plane_copies(refs, raw, sems, panel):
    c, core = lax.axis_index("col"), lax.rem(lax.axis_index("row"), 2)
    x, z = lax.div(c, SIDE), lax.rem(c, SIDE)
    line = jnp.where(core == 0, x, z + SIDE - panel)
    copies = []
    for n in range(SIDE):
        place = lax.rem(line + SIDE - n, SIDE)
        copies.append(pltpu.make_async_copy(refs[n], raw.at[rows_at(place, PAIR), :], sems.at[n]))
    return copies


def column_copies(tiles, raw, sems):
    r = lax.axis_index("row")
    y, core = lax.div(r, 2), lax.rem(r, 2)
    copies = []
    for n in range(N_ROW):
        k = lax.rem(y + SIDE - n % SIDE, SIDE) * 2 + lax.rem(core + n // SIDE, 2)
        source_y = lax.div(lax.rem(lax.axis_index("col"), N_ROW), 2)
        tile = lax.rem(lax.div(k, 2) + SIDE - source_y, SIDE)
        target = raw.at[lax.rem(k, 2), rows_at(tile, NB), :]
        copies.append(pltpu.make_async_copy(tiles[n], target, sems.at[n]))
    return copies


def first_kernel(*refs):
    pieces, inv_in, row_high, row_low, raw, inv, sems = refs[:SIDE], *refs[SIDE:]
    copies = plane_copies(pieces, raw, sems, 0)
    weights_copy = pltpu.make_async_copy(inv_in.at[0], inv, sems.at[SIDE])
    for copy in [weights_copy, *copies]:
        copy.start()
    weights_copy.wait()
    weights = deep(inv[...].T)
    for copy in copies:
        copy.wait()

    def row(p, carry):
        solved = dot3(raw[rows_at(p, PAIR), :], weights).reshape(2, NB, NB)
        high, low = split(solved)
        row_high[pl.ds(2 * p, 2)] = high
        row_low[pl.ds(2 * p, 2)] = low
        return carry

    lax.fori_loop(0, TR // 2, row, 0)


def solve_first(pieces, inv):
    return pl.pallas_call(
        first_kernel,
        out_shape=[jax.ShapeDtypeStruct((TR, NB, NB), BF16)] * 2,
        in_specs=[ANY] * (SIDE + 1),
        out_specs=[VMEM] * 2,
        scratch_shapes=[
            pltpu.VMEM((ROWS, NB), F32),
            pltpu.VMEM((NB, NB), F32),
            pltpu.SemaphoreType.DMA((SIDE + 1,)),
        ],
        compiler_params=pltpu.CompilerParams(vmem_limit_bytes=16 * 1024 * 1024),
        cost_estimate=pl.CostEstimate(flops=8 * 3 * 2 * NB**3, bytes_accessed=4 * 2**20, transcendentals=0),
        name="solve_first",
    )(*pieces, inv)


STEP = 2
LINES = NB * TC * 2
PART = 32


def last_kernel(*refs):
    pieces, cols = refs[:SIDE], refs[SIDE : SIDE + N_ROW]
    pivots, refs = refs[SIDE + N_ROW : SIDE + N_ROW + 2], refs[SIDE + N_ROW + 2 :]
    matrix, inv_in, high_in, low_in, band, out, panel, *refs = refs
    tiles, raw, raw_cols, row_high1, row_low1, row_high2, row_low2, col_high, col_low, even, odd, *refs = refs
    inv, pivot, sems, col_sems, in_sems, out_sems, panel_sems, small_sems = refs
    r, c = lax.axis_index("row"), lax.axis_index("col")
    copies = plane_copies(pieces, raw, sems, 1)
    col_copies = column_copies(cols, raw_cols, col_sems)
    loads = [pltpu.make_async_copy(matrix.at[p], tiles.at[p], in_sems.at[p]) for p in range(TR)]
    small = [(inv_in, inv), (pivots[0], pivot), (high_in, row_high1), (low_in, row_low1)]
    small = [pltpu.make_async_copy(a, b, small_sems.at[n]) for n, (a, b) in enumerate(small)]
    small[0].start()
    for n in range(2):

        @pl.when(lax.rem(r, 2) == n)
        def _():
            pltpu.make_async_copy(pivots[n], pivot, small_sems.at[1]).start()

    for copy in small[2:] + copies + col_copies + loads:
        copy.start()
    small[0].wait()
    weights0 = deep(inv[0].T)
    weights1 = deep(inv[1].T)
    small[1].wait()
    one_high, one_low = split(dot3(pivot[...], weights0).T)
    rest_weights = join(one_low, one_high)

    def used(high, low, code):
        full = dot(high, one_high)
        rest = dot(jnp.concatenate([high, low], axis=1), rest_weights)
        return jnp.where(code == 2, 0.0, full + jnp.where(code == 0, rest, 0.0))

    def column(q, carry):
        first = dot3(raw_cols[0, rows_at(q, NB), :], weights0)
        col_high[q, :NB, :], col_low[q, :NB, :] = split(first.T)
        high, low = split(first)
        tile = raw_cols[1, rows_at(q, NB), :] - used(high, low, band[q * N_COL + c, 1])
        col_high[q, NB:, :], col_low[q, NB:, :] = split(dot3(tile, weights1).T)
        return carry

    panels = [pltpu.make_async_copy(raw.at[pl.ds(p * NB, NB), :], panel.at[p], panel_sems.at[p]) for p in range(TR)]

    def solve(p):
        at = pl.ds(p * NB, NB)
        tile = raw[at, :] - used(row_high1[p], row_low1[p], band[p * N_ROW + r, 1])
        solved = dot3(tile, weights1)
        raw[at, :] = solved
        row_high2[p], row_low2[p] = split(solved)

    for copy in col_copies:
        copy.wait()
    lax.fori_loop(0, TC, column, 0, unroll=2)
    for copy in small[2:] + copies:
        copy.wait()

    size = STEP * NB

    def multiply(step, q, product):
        at = pl.ds(step * STEP, STEP)
        high = jnp.concatenate([row_high1[at].reshape(size, NB), row_high2[at].reshape(size, NB)], axis=1)
        low = jnp.concatenate([row_low1[at].reshape(size, NB), row_low2[at].reshape(size, NB)], axis=1)
        full = dot(high, col_high[q])
        rest = dot(jnp.concatenate([high, low], axis=1), join(col_low[q], col_high[q]))
        for p in range(STEP):
            code = band[(step * STEP + p) * N_ROW + r, q * N_COL + c]
            at = slice(p * NB, (p + 1) * NB)
            total = jnp.where(code == 2, 0.0, full[at] + jnp.where(code == 0, rest[at], 0.0))
            for b in range(2):
                product[b * TC + q, at, :] = total[:, b * HALF : (b + 1) * HALF]

    def subtract(step, share, product):
        for a in range(share * size // TC, (share + 1) * size // TC, PART):
            turned = product[:, a : a + PART, :].transpose(1, 0, 2).reshape(PART * 2 * TC, HALF)
            at = pl.ds(a % NB * 2 * TC, PART * 2 * TC)
            tiles[step * STEP + a // NB, at, :] -= turned

    steps = TR // STEP
    stores = [pltpu.make_async_copy(tiles.at[p], out.at[p], out_sems.at[p]) for p in range(TR)]
    for step in range(-1, steps + 1):
        product, before = (even, odd) if step % 2 == 0 else (odd, even)
        if step > 0:
            for p in range(STEP):
                loads[(step - 1) * STEP + p].wait()
        for q in range(TC):
            if step + 1 < steps and q < STEP:
                solve((step + 1) * STEP + q)
            if 0 <= step < steps:
                multiply(step, q, product)
            if step > 0:
                subtract(step - 1, q, before)
        if step + 1 < steps:
            for p in range(STEP):
                panels[(step + 1) * STEP + p].start()
        if step > 0:
            for p in range(STEP):
                stores[(step - 1) * STEP + p].start()
    for copy in stores + panels:
        copy.wait()


def finish(pieces, cols, pivots, matrix, inv, first, band):
    view = matrix.reshape(TR, NB, TC, 2, HALF).transpose(0, 1, 3, 2, 4).reshape(TR, LINES, HALF)
    out, panel = pl.pallas_call(
        last_kernel,
        out_shape=(
            jax.ShapeDtypeStruct((TR, LINES, HALF), F32),
            jax.ShapeDtypeStruct((TR, NB, NB), F32),
        ),
        in_specs=[ANY] * (SIDE + N_ROW + 2 + 4) + [SMEM],
        out_specs=[ANY] * 2,
        scratch_shapes=[
            pltpu.VMEM((TR, LINES, HALF), F32),
            pltpu.VMEM((ROWS, NB), F32),
            pltpu.VMEM((2, COLS, NB), F32),
            pltpu.VMEM((TR, NB, NB), BF16),
            pltpu.VMEM((TR, NB, NB), BF16),
            pltpu.VMEM((TR, NB, NB), BF16),
            pltpu.VMEM((TR, NB, NB), BF16),
            pltpu.VMEM((TC, PAIR, NB), BF16),
            pltpu.VMEM((TC, PAIR, NB), BF16),
            pltpu.VMEM((2 * TC, STEP * NB, HALF), F32),
            pltpu.VMEM((2 * TC, STEP * NB, HALF), F32),
            pltpu.VMEM((2, NB, NB), F32),
            pltpu.VMEM((NB, NB), F32),
            pltpu.SemaphoreType.DMA((SIDE,)),
            pltpu.SemaphoreType.DMA((N_ROW,)),
            pltpu.SemaphoreType.DMA((TR,)),
            pltpu.SemaphoreType.DMA((TR,)),
            pltpu.SemaphoreType.DMA((TR,)),
            pltpu.SemaphoreType.DMA((4,)),
        ],
        compiler_params=pltpu.CompilerParams(vmem_limit_bytes=40 * 1024 * 1024),
        cost_estimate=pl.CostEstimate(flops=200 * 2 * NB**3, bytes_accessed=20 * 2**20, transcendentals=0),
        name="solve_and_update",
    )(*pieces, *cols, *pivots, view, inv, *first, band)
    return out.reshape(TR, NB, 2, TC, HALF).transpose(0, 1, 3, 2, 4).reshape(TR, NB, TC, NB), panel


def body(matrix, diag_inverses, band):
    raw = lax.optimization_barrier(matrix[:, :, 0, :].reshape(ROWS, NB))
    panel1, panel2, cols, pivots = gather_all(raw, lax.axis_index("row"), lax.axis_index("col"))
    first = solve_first(panel1, diag_inverses)
    cols, first = lax.optimization_barrier((cols, first))
    own, up, last, down, own_other, up_other, down_other = cols
    cols = [own, up, last, down, own_other, up_other, swap_core(last), down_other]
    return finish(panel2, cols, pivots, matrix, diag_inverses, first, band)


def solution(mesh):
    in_specs = (P(None, "row", None, "col"), P(), P())
    out_specs = (P(None, "row", None, "col"), P(None, "row", None))
    return jax.shard_map(body, mesh=mesh, in_specs=in_specs, out_specs=out_specs, check_vma=False)
```
